32 devices in a mesh: leaf: 16 (over z, y, core), blk: 2 (over x).
Axes of the slice: x: 2, y: 2, z: 4, core: 2. Of those that a mesh axis runs over, the one named last changes fastest.
Arguments:
- leaf_rows: bfloat16 [32, 8, 512, 512], P('leaf', None, 'blk'), may hold values from -2 to 2
- leaf_weight: bfloat16 [32, 8, 512], P('leaf', None, 'blk'), may hold values from 0.25 to 4
- branching: int32 [32], P('leaf'), may hold values from 1 to 8, as said below
- sibling: int32 [16, 2], P('leaf'), may hold values from 0 to 1, each once within a row
- node_block: bfloat16 [512, 32, 512], P('blk', 'leaf'), may hold values from -6 to 6
- na_rows: bfloat16 [16384, 512], P(('leaf', 'blk')), may hold values from -3 to 3
- na_weight: bfloat16 [16384], P(('leaf', 'blk')), may hold values from 0.25 to 4
- na_route: int32 [16384, 1], P(('leaf', 'blk')), may hold values from 0 to 31; in each aligned block of 512 rows (0 to 511, 512 to 1023, ...) at most 24 rows name the same one
Outputs:
- node_schur: float32 [512, 32, 512], P('blk', 'leaf')
- merged: float32 [512, 32, 512], P('blk', 'leaf')
The draws below stay inside these ranges and needn't reach their ends.
Inputs may be any that keep to these rules, and one draw needn't show every extreme that they name: `branching`: some node has exactly 8 children. `sibling`: each row is a permutation. `na_route`: within the rows of one device, no node is named by more than 24 rows, a bound that some block reaches.
All inputs are finite; a program needn't handle non-finite values.
Results may differ from the reference program's by a relative error of at most 0.0012.
Values may be sent and summed in bfloat16 or wider, within the bound.
No kernel may reach another device: no remote copies, remote signals or barrier semaphores. Data moves between devices by JAX's collectives and lax.ppermute only.
A program may use at most 64 MiB of HBM per device.

```python
import math
import jax
import jax.numpy as jnp
import numpy as np
from jax import lax

S = 512
KL = 512
MAXB = 8
NODE_DEV = 2
NA_DEV = 512
SUBTREES = 16
NODES = 32
NA_ROWS = 16384
CAP = 24
N_BLK = 2


def draw_branching(key, part):
    first_key = jax.random.fold_in(key, 11)
    second_key = jax.random.fold_in(key, 12)
    third_key = jax.random.fold_in(key, 13)
    fourth_key = jax.random.fold_in(key, 14)
    level = jax.random.randint(first_key, (SUBTREES,), 1, MAXB + 1)
    forced = jax.random.randint(second_key, (), 0, SUBTREES)
    level = jnp.where(jnp.arange(SUBTREES) == forced, MAXB, level)
    counts = jax.random.randint(third_key, (SUBTREES, NODE_DEV), 1, level[:, None] + 1)
    picked = jax.random.randint(fourth_key, (SUBTREES,), 0, NODE_DEV)
    counts = jnp.where(jnp.arange(NODE_DEV)[None, :] == picked[:, None], level[:, None], counts)
    return counts.reshape(-1).astype(jnp.int32)


def shard_levels(own_key, extent, split, low, top_value):
    def one(axis_at, blocks):
        draws = jax.random.uniform(jax.random.fold_in(jax.random.fold_in(own_key, 6), axis_at), (blocks,), jnp.float32, low / len(split), top_value / len(split))
        return jnp.repeat(jnp.exp(draws), extent[axis_at] // blocks).reshape((-1,) + (1,) * (len(extent) - axis_at - 1))

    factor_of = one(*split[0])
    for cut in split[1:]:
        factor_of = factor_of * one(*cut)
    return factor_of


def routed_block(key, own, number, rows, number_of, top, bound, slope):
    ranking = jax.random.permutation(key, number_of)
    packed, ordinary = shares(number_of, rows * top, bound, slope, True), shares(number_of, rows * top, bound, slope, False)
    places = jnp.arange(number_of)

    def named(tallies, rotation):
        used = int((tallies > 0).sum())
        fixed = max(1, used // 4)
        shifted = fixed + (places - fixed + rotation * (used - fixed)) % max(1, number_of - fixed)
        return jnp.zeros((number_of,), jnp.int32).at[ranking[jnp.where(places < fixed, places, shifted)]].set(jnp.asarray(tallies, jnp.int32))

    tallies = jnp.where(number % 4 == 0, named(packed, number // 4), named(ordinary, number - number // 4 - 1))
    mixed = jax.random.permutation(jax.random.fold_in(own, 3), number_of)
    donor, receiver = mixed[0:number_of // 2 * 2:2], mixed[1:number_of // 2 * 2:2]
    margin = jnp.minimum(tallies[donor] - 1, bound - tallies[receiver]) // 2
    margin = jnp.where((donor == ranking[0]) | (receiver == ranking[0]) | (tallies[receiver] == 0), 0, jnp.maximum(margin, 0))
    shifted = jax.random.randint(jax.random.fold_in(own, 4), (number_of // 2,), 0, 1 << 20) % (margin + 1)
    tallies = tallies.at[donor].add(-shifted).at[receiver].add(shifted)
    members = jnp.searchsorted(jnp.cumsum(tallies), jnp.arange(rows * top), side="right").astype(jnp.int32)
    grid = members.reshape(top, rows).T
    grid = grid[jax.random.permutation(jax.random.fold_in(own, 1), rows)]
    rotation = jax.random.randint(jax.random.fold_in(own, 2), (rows, 1), 0, top)
    return jnp.take_along_axis(grid, (jnp.arange(top)[None, :] + rotation) % top, axis=1)


def shares(number_of, total, limit, skew, full):
    weights = [(1 << 20) // math.isqrt(grade ** skew) + 1 for grade in range(1, number_of + 1)]
    largest = limit if full else min(limit, max(-(-total // number_of), total * weights[0] // sum(weights)))
    least = 1 if total - largest >= number_of - 1 else 0
    given, surplus = [largest] + [least] * (number_of - 1), total - largest - least * (number_of - 1)
    while surplus > 0:
        free = [i for i in range(1, number_of) if given[i] < largest] or [i for i in range(1, number_of) if given[i] < limit]
        mass, budget = sum([weights[i] for i in free]), surplus
        for i in free:
            extra = min(limit - given[i], max(1, budget * weights[i] // mass), surplus)
            given[i] = given[i] + extra
            surplus = surplus - extra
    return np.array(given)


def bell_draw(stream_key, shape, scale, bound, pieces=(), kind=jnp.bfloat16):
    array = scale * jax.random.normal(stream_key, shape, jnp.float32)
    if pieces:
        array = array * shard_levels(stream_key, shape, pieces, -0.22, 0.18)
    return jnp.clip(array, -bound, bound).astype(kind)


def setup_inputs(seed: int = 0) -> dict:
    streams_of = jax.random.split(jax.random.key(seed), 9)
    leaf_rows = bell_draw(streams_of[0], (NODES, MAXB, KL, S), ((MAXB * KL) ** -0.25), 2.0, ((0, 16), (2, 2)))
    leaf_weight = jnp.clip(jnp.exp(math.log(4.0) - 2.7725887 * jax.random.uniform(streams_of[1], (NODES, MAXB, KL), jnp.float32) ** shard_levels(streams_of[1], (NODES, MAXB, KL), ((0, 16), (2, 2)), -0.2, 0.2)), 0.25, 4.0).astype(jnp.bfloat16)
    branching = draw_branching(jax.random.fold_in(streams_of[8], 71), 0)
    sibling = jax.vmap(lambda own: jax.random.permutation(own, NODE_DEV))(jax.random.split(streams_of[3], SUBTREES)).reshape((SUBTREES, NODE_DEV)).astype(jnp.int32)
    node_block = bell_draw(streams_of[4], (S, NODES, S), 1.0, 6.0, ((0, 2), (1, 16)))
    na_rows = bell_draw(streams_of[5], (NA_ROWS, S), ((NA_DEV * N_BLK // NODE_DEV) ** -0.25), 3.0, ((0, 32),))
    na_weight = jnp.clip(jnp.exp(math.log(4.0) - 2.7725887 * jax.random.uniform(streams_of[6], (NA_ROWS,), jnp.float32) ** shard_levels(streams_of[6], (NA_ROWS,), ((0, 32),), -0.2, 0.2)), 0.25, 4.0).astype(jnp.bfloat16)
    na_route_keys = jax.random.split(jax.random.fold_in(streams_of[7], 1), NA_ROWS // NA_DEV)
    na_route_turns = jax.random.permutation(jax.random.fold_in(streams_of[7], 3), NA_ROWS // NA_DEV)
    na_route = jax.vmap(lambda own, number: routed_block(jax.random.fold_in(streams_of[7], 2), own, number, NA_DEV, NODES, 1, CAP, 2))(na_route_keys, na_route_turns).reshape((NA_ROWS, 1))
    return {"leaf_rows": leaf_rows, "leaf_weight": leaf_weight, "branching": branching, "sibling": sibling, "node_block": node_block, "na_rows": na_rows, "na_weight": na_weight, "na_route": na_route}


def bucket_rows(route, rows, weight, total_nodes, capacity):
    count = route.shape[0]
    order = jnp.argsort(route, stable=True)
    sorted_route = route[order].astype(jnp.int32)
    first = jnp.searchsorted(sorted_route, sorted_route, side="left").astype(jnp.int32)
    position = jnp.arange(count, dtype=jnp.int32) - first
    slot = sorted_route * capacity + position
    width = rows.shape[1]
    filled = jnp.zeros((total_nodes * capacity, width), rows.dtype).at[slot].set(rows[order])
    weights = jnp.zeros((total_nodes * capacity,), weight.dtype).at[slot].set(weight[order])
    return filled, weights


def reference(leaf_rows, leaf_weight, branching, sibling, node_block, na_rows, na_weight, na_route):
    live = (jnp.arange(MAXB, dtype=jnp.int32)[None, :] < branching[:, None]).astype(jnp.float32)

    def one_node(items):
        rows, weight, alive = items
        scaled = (rows.astype(jnp.float32) * (weight.astype(jnp.float32) * alive[:, None])[..., None]).astype(jnp.bfloat16)
        return jnp.dot(scaled.reshape(-1, S).T, rows.reshape(-1, S), preferred_element_type=jnp.float32)

    leaf_sum = lax.map(one_node, (leaf_rows, leaf_weight, live))
    blocks = NA_ROWS // NA_DEV
    block_rows = na_rows.reshape(blocks, NA_DEV, S)
    block_weight = na_weight.reshape(blocks, NA_DEV)
    block_route = na_route.reshape(blocks, NA_DEV)

    def add_block(carry, items):
        rows, weight, route = items
        filled, weights = bucket_rows(route, rows, weight, NODES, CAP)
        scaled = (filled.astype(jnp.float32) * weights.astype(jnp.float32)[:, None]).astype(jnp.bfloat16)
        scaled = scaled.reshape(NODES, CAP, S).astype(jnp.float32)
        plain = filled.reshape(NODES, CAP, S).astype(jnp.float32)
        term = jnp.einsum("ncs,nct->nst", scaled, plain, precision=lax.Precision.HIGHEST)
        return carry + term, None

    na_sum, _ = lax.scan(add_block, jnp.zeros((NODES, S, S), jnp.float32), (block_rows, block_weight, block_route))
    node_schur = node_block.astype(jnp.float32) + jnp.transpose(leaf_sum + na_sum, (1, 0, 2))
    index = jnp.arange(NODES, dtype=jnp.int32)
    subtree = index // NODE_DEV
    within = index % NODE_DEV
    partner = jnp.bitwise_xor(subtree, 1) * NODE_DEV + sibling[subtree, within]
    merged = node_schur + jnp.take(node_schur, partner.astype(jnp.int32), axis=1)
    return node_schur, merged
```

```python
import functools

import jax
import jax.numpy as jnp
from jax import lax
from jax.experimental import pallas as pl
from jax.experimental.pallas import tpu as pltpu
from jax.sharding import PartitionSpec as P

F32 = jnp.float32
BF16 = jnp.bfloat16
I32 = jnp.int32
LANES = 128
GROUP = 16
VMEM = pl.BlockSpec(memory_space=pltpu.VMEM)
SMEM = pl.BlockSpec(memory_space=pltpu.SMEM)
CODE = 32000.0


class Plan:
    def __init__(self, leaf_count, node_dev, capacity, state):
        self.leaf_count, self.node_dev, self.capacity, self.state = leaf_count, node_dev, capacity, state
        self.full = capacity // GROUP * GROUP
        self.rest = capacity - self.full
        self.rows = -(-node_dev * capacity // GROUP) * GROUP
        self.groups = self.rows // GROUP
        self.slabs = state // LANES
        self.block = self.slabs * self.rows + GROUP
        self.groups_of = [
            [g for g in range(self.groups) if q in {self.node_at(g * GROUP + i) for i in range(GROUP)}]
            for q in range(node_dev)
        ]
        self.depth = [leaf_count * GROUP * len(g) for g in self.groups_of]

    def node_at(self, row):
        if row < self.node_dev * self.full:
            return row // self.full
        return min((row - self.node_dev * self.full) // self.rest, self.node_dev - 1) if self.rest else 0


def dot_t(a, b):
    return lax.dot_general(a, b, (((0,), (0,)), ((), ())), preferred_element_type=F32)


def bucket_kernel(plan, route_ref, weight_ref, rows_ref, out_ref):
    count = rows_ref.shape[0]
    nodes = plan.leaf_count * plan.node_dev
    route = route_ref[...]
    member = lax.broadcasted_iota(I32, (nodes, count), 0) == route
    before = (
        lax.broadcasted_iota(I32, (count, count), 0) < lax.broadcasted_iota(I32, (count, count), 1)
    ).astype(BF16)
    seen = jnp.dot(member.astype(BF16), before, preferred_element_type=F32)
    position = jnp.sum(jnp.where(member, seen, 0.0), axis=0, keepdims=True).astype(I32)
    owner = route // plan.node_dev
    q = route - owner * plan.node_dev
    slot = owner * plan.rows + jnp.where(
        position < plan.full,
        q * plan.full + position,
        plan.node_dev * plan.full + q * plan.rest + position - plan.full,
    )
    total = plan.leaf_count * plan.rows
    hit = lax.broadcasted_iota(I32, (total, count), 0) == slot
    filled = jnp.dot(
        jnp.where(hit, 1.0, 0.0).astype(BF16), rows_ref[...], preferred_element_type=F32
    ).astype(BF16)
    weights = jnp.dot(
        jnp.where(hit, weight_ref[...].astype(F32), 0.0).astype(BF16),
        jnp.ones((count, LANES), BF16),
        preferred_element_type=F32,
    )
    lane = lax.broadcasted_iota(I32, (GROUP, LANES), 1)
    sub = lax.broadcasted_iota(I32, (GROUP, LANES), 0)
    want = []
    for g in range(plan.groups):
        q_of = jnp.zeros((GROUP, LANES), I32)
        for i in range(1, GROUP):
            step = plan.node_at(g * GROUP + i) - plan.node_at(g * GROUP + i - 1)
            if step:
                q_of = q_of + jnp.where(sub >= i, step, 0)
        want.append(lane == g * plan.node_dev + plan.node_at(g * GROUP) + q_of)
    for d in range(plan.leaf_count):
        at = d * plan.rows
        for c in range(plan.slabs):
            out_ref[d, c * plan.rows : (c + 1) * plan.rows, :] = filled[
                at : at + plan.rows, c * LANES : (c + 1) * LANES
            ]
        extra = jnp.zeros((GROUP, LANES), F32)
        for g in range(plan.groups):
            extra = jnp.where(want[g], weights[at + g * GROUP : at + (g + 1) * GROUP, :], extra)
        out_ref[d, plan.slabs * plan.rows :, :] = extra.astype(BF16)


def leaf_kernel(place_ref, branching_ref, weight_ref, rows_ref, block_ref, own_ref, send_ref, total):
    n = pl.program_id(0)
    share = own_ref.shape[1]
    peers = send_ref.shape[0]
    blk = place_ref[0]
    columns = jnp.transpose(weight_ref[0].astype(F32))
    total[...] = jnp.zeros_like(total)
    for b in range(rows_ref.shape[1]):

        @pl.when(b < branching_ref[n])
        def _():
            rows = rows_ref[0, b]
            scaled = (rows.astype(F32) * columns[:, b : b + 1]).astype(BF16)
            total[...] += dot_t(scaled, rows)

    own_ref[0] = total[pl.ds(pl.multiple_of(blk * share, share), share), :] + block_ref[0].astype(F32)
    for e in range(1, peers + 1):
        at = pl.multiple_of((blk ^ e) * share, share)
        send_ref[e - 1, 0] = total[pl.ds(at, share), :]


def send_kernel(plan, place_ref, got_ref, part_ref, code_ref, plain_ref, scaled_ref, total=None):
    blk = place_ref[0]
    peers, _, share, state = part_ref.shape
    for d in range(plan.leaf_count):
        extra = got_ref[d, plan.slabs * plan.rows :, :].astype(F32)
        for g in range(plan.groups):
            rows = jnp.concatenate(
                [
                    got_ref[d, c * plan.rows + g * GROUP : c * plan.rows + (g + 1) * GROUP, :]
                    for c in range(plan.slabs)
                ],
                axis=1,
            )
            wide = rows.astype(F32)
            for q in range(plan.node_dev):
                if g not in plan.groups_of[q]:
                    continue
                at = (plan.groups_of[q].index(g) * plan.leaf_count + d) * GROUP
                j = g * plan.node_dev + q
                plain_ref[q, at : at + GROUP, :] = rows
                scaled_ref[q, at : at + GROUP, :] = (wide * extra[:, j : j + 1]).astype(BF16)
    for q in range(plan.node_dev):
        product = Product(scaled_ref.at[q], plain_ref.at[q], total)
        for e in range(1, peers + 1):
            at = pl.multiple_of((blk ^ e) * share, share)
            encode(part_ref[e - 1, q] + product.rows(at, share), code_ref.at[e - 1], q, share)


class Product:
    def __init__(self, scaled_ref, plain_ref, total):
        self.scaled_ref, self.plain_ref, self.total = scaled_ref, plain_ref, total
        if total is not None:
            total[...] = dot_t(scaled_ref[...], plain_ref[...])

    def rows(self, at, share):
        if self.total is not None:
            return self.total[pl.ds(at, share), :]
        return dot_t(self.scaled_ref[:, pl.ds(at, share)], self.plain_ref[...])


def encode(value, code_ref, q, share):
    state = value.shape[1]
    most = jnp.max(jnp.abs(value), axis=1, keepdims=True)
    power = jnp.ceil(jnp.log2(jnp.maximum(most, 1e-30)))
    code_ref[q * share : (q + 1) * share, :] = (
        jnp.round(value * (CODE * jnp.exp2(-power))).astype(I32).astype(jnp.int16)
    )
    width = min(share, LANES)
    eye = lax.broadcasted_iota(I32, (width, LANES), 0) == lax.broadcasted_iota(I32, (width, LANES), 1)
    parts = []
    for k in range(0, share, width):
        parts.append(jnp.sum(jnp.where(eye, power[k : k + width], 0.0), axis=0, keepdims=True))
    line = jnp.concatenate(parts + [jnp.zeros((1, state - LANES * len(parts)), F32)], axis=1)
    line = jnp.broadcast_to(line, (GROUP, state)).astype(I32).astype(jnp.int16)
    base = code_ref.shape[0] - GROUP * (code_ref.shape[0] // share - q)
    code_ref[base : base + GROUP, :] = line


def decode(code_ref, q, share):
    base = code_ref.shape[0] - GROUP * (code_ref.shape[0] // share - q)
    line = code_ref[base : base + GROUP, :].astype(I32).astype(F32)[0:1, :]
    width = min(share, LANES)
    eye = lax.broadcasted_iota(I32, (width, LANES), 0) == lax.broadcasted_iota(I32, (width, LANES), 1)
    parts = []
    for k in range(share // width):
        one = line[:, k * LANES : (k + 1) * LANES]
        parts.append(jnp.sum(jnp.where(eye, one, 0.0), axis=1, keepdims=True))
    power = jnp.concatenate(parts, axis=0)
    value = code_ref[q * share : (q + 1) * share, :].astype(I32).astype(F32)
    return value * (jnp.exp2(power) * (1.0 / CODE))


def own_kernel(place_ref, part_ref, plain_ref, scaled_ref, own_ref, total=None):
    nodes, share, _ = part_ref.shape
    at = pl.multiple_of(place_ref[0] * share, share)
    for q in range(nodes):
        own_ref[q] = part_ref[q] + Product(scaled_ref.at[q], plain_ref.at[q], total).rows(at, share)


def node_kernel(own_ref, code_ref, out_ref, node_ref):
    nodes, share, _ = own_ref.shape
    for q in range(nodes):
        value = own_ref[q]
        for e in range(code_ref.shape[0]):
            value = value + decode(code_ref.at[e], q, share)
        node_ref[q] = value
        out_ref[:, q, :] = value


def merge_kernel(sibling_ref, node_ref, partner_ref, out_ref):
    for q in range(node_ref.shape[0]):
        out_ref[:, q, :] = node_ref[q] + partner_ref[sibling_ref[0, q]]


def call(kernel, out_shape, in_specs, flops=0, moved=1 << 20, **more):
    outs = jax.tree.map(lambda _: VMEM, out_shape)
    more.setdefault("out_specs", outs)
    return pl.pallas_call(
        kernel,
        out_shape=out_shape,
        in_specs=in_specs,
        compiler_params=pltpu.CompilerParams(vmem_limit_bytes=32 << 20),
        cost_estimate=pl.CostEstimate(flops=flops, bytes_accessed=moved, transcendentals=0),
        **more,
    )


def shards(leaf_rows, leaf_weight, branching, sibling, node_block, na_rows, na_weight, na_route):
    leaf_count, blk_count = lax.axis_size("leaf"), lax.axis_size("blk")
    node_dev, most_children, depth, state = leaf_rows.shape
    count = na_rows.shape[0]
    share = state // blk_count
    peers = blk_count - 1
    plan = Plan(leaf_count, node_dev, 3 * count // (2 * leaf_count * node_dev), state)
    place = lax.axis_index("blk").astype(I32).reshape(1)
    whole = [pltpu.VMEM((state, state), F32)] if share % LANES else []
    shape = jax.ShapeDtypeStruct

    with jax.named_scope("bucket"):
        blocks = call(
            functools.partial(bucket_kernel, plan),
            shape((leaf_count, plan.block, LANES), BF16),
            [VMEM, VMEM, VMEM],
            flops=2 * plan.leaf_count * plan.rows * count * state,
        )(na_route.reshape(1, count), na_weight.reshape(1, count), na_rows)
    got = lax.all_to_all(blocks, "leaf", split_axis=0, concat_axis=0, tiled=True)

    with jax.named_scope("leaf_products"):
        own_part, send_part = call(
            leaf_kernel,
            (shape((node_dev, share, state), F32), shape((peers, node_dev, share, state), F32)),
            [
                SMEM,
                SMEM,
                pl.BlockSpec((1, most_children, depth), lambda n: (n, 0, 0)),
                pl.BlockSpec((1, most_children, depth, state), lambda n: (n, 0, 0, 0)),
                pl.BlockSpec((1, share, state), lambda n: (n, 0, 0)),
            ],
            out_specs=(
                pl.BlockSpec((1, share, state), lambda n: (n, 0, 0)),
                pl.BlockSpec((peers, 1, share, state), lambda n: (0, n, 0, 0)),
            ),
            grid=(node_dev,),
            scratch_shapes=[pltpu.VMEM((state, state), F32)],
            flops=2 * node_dev * most_children * depth * state * state,
            moved=8 << 20,
        )(place, branching, leaf_weight, leaf_rows, jnp.transpose(node_block, (1, 0, 2)))

    with jax.named_scope("routed_send"):
        code, plain, scaled = call(
            functools.partial(send_kernel, plan),
            (
                shape((peers, node_dev * (share + GROUP), state), jnp.int16),
                shape((node_dev, max(plan.depth), state), BF16),
                shape((node_dev, max(plan.depth), state), BF16),
            ),
            [SMEM, VMEM, VMEM],
            scratch_shapes=whole,
            flops=2 * node_dev * max(plan.depth) * state * state,
        )(place, got, send_part)
    received = [
        lax.ppermute(code[e - 1], "blk", [(i, i ^ e) for i in range(blk_count)])
        for e in range(1, blk_count)
    ]
    with jax.named_scope("routed_own"):
        own = call(
            own_kernel,
            shape((node_dev, share, state), F32),
            [SMEM, VMEM, VMEM, VMEM],
            scratch_shapes=whole,
            flops=2 * node_dev * max(plan.depth) * share * state,
        )(place, own_part, plain, scaled)
    with jax.named_scope("node"):
        node_schur, node = call(
            node_kernel,
            (shape((share, node_dev, state), F32), shape((node_dev, share, state), F32)),
            [VMEM, VMEM],
        )(own, jnp.stack(received) if peers > 1 else received[0][None])
    partner = lax.ppermute(node, "leaf", [(i, i ^ 1) for i in range(leaf_count)])
    with jax.named_scope("merge"):
        merged = call(
            merge_kernel, shape((share, node_dev, state), F32), [SMEM, VMEM, VMEM]
        )(sibling, node, partner)
    return (node_schur, merged)


def solution(mesh):
    return jax.shard_map(
        shards,
        mesh=mesh,
        in_specs=(
            P("leaf", None, "blk", None),
            P("leaf", None, "blk"),
            P("leaf"),
            P("leaf", None),
            P("blk", "leaf", None),
            P(("leaf", "blk"), None),
            P(("leaf", "blk")),
            P(("leaf", "blk"), None),
        ),
        out_specs=(P("blk", "leaf", None), P("blk", "leaf", None)),
        check_vma=False,
    )
```

```python
import functools

import jax
import jax.numpy as jnp
from jax import lax
from jax.experimental import pallas as pl
from jax.experimental.pallas import tpu as pltpu
from jax.sharding import PartitionSpec as P

F32 = jnp.float32
BF16 = jnp.bfloat16
I32 = jnp.int32
LANES = 128
GROUP = 16
VMEM = pl.BlockSpec(memory_space=pltpu.VMEM)
SMEM = pl.BlockSpec(memory_space=pltpu.SMEM)
CODE = 32000.0


class Plan:
    def __init__(self, leaf_count, node_dev, capacity, state):
        self.leaf_count, self.node_dev, self.capacity, self.state = leaf_count, node_dev, capacity, state
        self.full = capacity // GROUP * GROUP
        self.rest = capacity - self.full
        self.rows = -(-node_dev * capacity // GROUP) * GROUP
        self.groups = self.rows // GROUP
        self.slabs = state // LANES
        self.block = self.slabs * self.rows + GROUP
        self.groups_of = [
            [g for g in range(self.groups) if q in {self.node_at(g * GROUP + i) for i in range(GROUP)}]
            for q in range(node_dev)
        ]
        self.depth = [leaf_count * GROUP * len(g) for g in self.groups_of]

    def node_at(self, row):
        if row < self.node_dev * self.full:
            return row // self.full
        return min((row - self.node_dev * self.full) // self.rest, self.node_dev - 1) if self.rest else 0


def dot_t(a, b):
    return lax.dot_general(a, b, (((0,), (0,)), ((), ())), preferred_element_type=F32)


def bucket_kernel(plan, route_ref, weight_ref, rows_ref, out_ref):
    count = rows_ref.shape[0]
    nodes = plan.leaf_count * plan.node_dev
    route = route_ref[...]
    member = lax.broadcasted_iota(I32, (nodes, count), 0) == route
    before = (
        lax.broadcasted_iota(I32, (count, count), 0) < lax.broadcasted_iota(I32, (count, count), 1)
    ).astype(BF16)
    seen = jnp.dot(member.astype(BF16), before, preferred_element_type=F32)
    position = jnp.sum(jnp.where(member, seen, 0.0), axis=0, keepdims=True).astype(I32)
    owner = route // plan.node_dev
    q = route - owner * plan.node_dev
    slot = owner * plan.rows + jnp.where(
        position < plan.full,
        q * plan.full + position,
        plan.node_dev * plan.full + q * plan.rest + position - plan.full,
    )
    total = plan.leaf_count * plan.rows
    hit = lax.broadcasted_iota(I32, (total, count), 0) == slot
    filled = jnp.dot(
        jnp.where(hit, 1.0, 0.0).astype(BF16), rows_ref[...], preferred_element_type=F32
    ).astype(BF16)
    weights = jnp.dot(
        jnp.where(hit, weight_ref[...].astype(F32), 0.0).astype(BF16),
        jnp.ones((count, LANES), BF16),
        preferred_element_type=F32,
    )
    lane = lax.broadcasted_iota(I32, (GROUP, LANES), 1)
    sub = lax.broadcasted_iota(I32, (GROUP, LANES), 0)
    want = []
    for g in range(plan.groups):
        q_of = jnp.zeros((GROUP, LANES), I32)
        for i in range(1, GROUP):
            step = plan.node_at(g * GROUP + i) - plan.node_at(g * GROUP + i - 1)
            if step:
                q_of = q_of + jnp.where(sub >= i, step, 0)
        want.append(lane == g * plan.node_dev + plan.node_at(g * GROUP) + q_of)
    for d in range(plan.leaf_count):
        at = d * plan.rows
        for c in range(plan.slabs):
            out_ref[d, c * plan.rows : (c + 1) * plan.rows, :] = filled[
                at : at + plan.rows, c * LANES : (c + 1) * LANES
            ]
        extra = jnp.zeros((GROUP, LANES), F32)
        for g in range(plan.groups):
            extra = jnp.where(want[g], weights[at + g * GROUP : at + (g + 1) * GROUP, :], extra)
        out_ref[d, plan.slabs * plan.rows :, :] = extra.astype(BF16)


def leaf_kernel(place_ref, branching_ref, weight_ref, rows_ref, block_ref, own_ref, send_ref, total):
    n = pl.program_id(0)
    share = own_ref.shape[1]
    peers = send_ref.shape[0]
    blk = place_ref[0]
    columns = jnp.transpose(weight_ref[0].astype(F32))
    total[...] = jnp.zeros_like(total)
    for b in range(rows_ref.shape[1]):

        @pl.when(b < branching_ref[n])
        def _():
            rows = rows_ref[0, b]
            scaled = (rows.astype(F32) * columns[:, b : b + 1]).astype(BF16)
            total[...] += dot_t(scaled, rows)

    own_ref[0] = total[pl.ds(pl.multiple_of(blk * share, share), share), :] + block_ref[0].astype(F32)
    for e in range(1, peers + 1):
        at = pl.multiple_of((blk ^ e) * share, share)
        send_ref[e - 1, 0] = total[pl.ds(at, share), :]


class Product:
    def __init__(self, scaled_ref, plain_ref, total):
        self.scaled_ref, self.plain_ref, self.total = scaled_ref, plain_ref, total
        if total is not None:
            total[...] = dot_t(scaled_ref[...], plain_ref[...])

    def rows(self, at, share):
        if self.total is not None:
            return self.total[pl.ds(at, share), :]
        return dot_t(self.scaled_ref[:, pl.ds(at, share)], self.plain_ref[...])


def gather_rows(plan, got_ref, plain_ref, scaled_ref):
    for d in range(plan.leaf_count):
        extra = got_ref[d, plan.slabs * plan.rows :, :].astype(F32)
        for g in range(plan.groups):
            rows = jnp.concatenate(
                [
                    got_ref[d, c * plan.rows + g * GROUP : c * plan.rows + (g + 1) * GROUP, :]
                    for c in range(plan.slabs)
                ],
                axis=1,
            )
            wide = rows.astype(F32)
            for q in range(plan.node_dev):
                if g not in plan.groups_of[q]:
                    continue
                at = (plan.groups_of[q].index(g) * plan.leaf_count + d) * GROUP
                j = g * plan.node_dev + q
                plain_ref[q, at : at + GROUP, :] = rows
                scaled_ref[q, at : at + GROUP, :] = (wide * extra[:, j : j + 1]).astype(BF16)


def scale_of(most):
    power = jnp.ceil(8.0 * jnp.log2(jnp.maximum(most, 1e-30)))
    return power, CODE * jnp.exp2(-0.125 * power)


def to_code(value):
    return jnp.round(value).astype(I32).astype(jnp.int16)


def from_code(code):
    return code.astype(I32).astype(F32)


def diagonal(width):
    return lax.broadcasted_iota(I32, (width, width), 0) == lax.broadcasted_iota(I32, (width, width), 1)


def as_line(column):
    return jnp.sum(jnp.where(diagonal(column.shape[0]), column, 0.0), axis=0, keepdims=True)


def as_column(line):
    return jnp.sum(jnp.where(diagonal(line.shape[1]), line, 0.0), axis=1, keepdims=True)


def send_plain(plan, place_ref, got_ref, part_ref, code_ref, plain_ref, scaled_ref, total=None):
    blk = place_ref[0]
    peers, nodes, share, state = part_ref.shape
    gather_rows(plan, got_ref, plain_ref, scaled_ref)
    for q in range(nodes):
        product = Product(scaled_ref.at[q], plain_ref.at[q], total)
        for e in range(1, peers + 1):
            at = pl.multiple_of((blk ^ e) * share, share)
            value = part_ref[e - 1, q] + product.rows(at, share)
            power, factor = scale_of(jnp.max(jnp.abs(value), axis=1, keepdims=True))
            code_ref[e - 1, q * share : (q + 1) * share, :] = to_code(value * factor)
            line = jnp.concatenate([as_line(power), jnp.zeros((1, state - share), F32)], axis=1)
            base = nodes * share + q * GROUP
            code_ref[e - 1, base : base + GROUP, :] = to_code(jnp.broadcast_to(line, (GROUP, state)))


def decode_plain(place, code_ref, nodes, share):
    values = []
    for q in range(nodes):
        base = nodes * share + q * GROUP
        value = None
        for e in range(code_ref.shape[0]):
            power = as_column(from_code(code_ref[e, base : base + GROUP, :])[0:1, :share])
            term = from_code(code_ref[e, q * share : (q + 1) * share, :]) * (
                jnp.exp2(0.125 * power) * (1.0 / CODE)
            )
            value = term if value is None else value + term
        values.append(value)
    return values


def send_folded(plan, place_ref, got_ref, part_ref, code_ref, plain_ref, scaled_ref):
    share = part_ref.shape[2]
    mine = pl.ds(pl.multiple_of(place_ref[0] * share, share), share)
    theirs = pl.ds(pl.multiple_of((1 - place_ref[0]) * share, share), share)
    gather_rows(plan, got_ref, plain_ref, scaled_ref)
    square, beside = [], []
    for q in range(2):
        scaled = scaled_ref[q, :, theirs]
        square.append(part_ref[0, q, :, theirs] + dot_t(scaled, plain_ref[q, :, theirs]))
        beside.append(part_ref[0, q, :, mine] + dot_t(scaled, plain_ref[q, :, mine]))
    most = jnp.maximum(
        jnp.maximum(jnp.abs(square[0]), jnp.abs(square[1])),
        jnp.maximum(jnp.abs(beside[0]), jnp.abs(beside[1])),
    )
    power, factor = scale_of(jnp.max(most, axis=1, keepdims=True))
    row = lax.broadcasted_iota(I32, (share, share), 0)
    column = lax.broadcasted_iota(I32, (share, share), 1)
    lower = square[1] * factor
    code_ref[0, :share, 0:share] = to_code(jnp.where(column >= row, square[0] * factor, lower))
    code_ref[0, :share, share : 2 * share] = to_code(beside[0] * factor)
    code_ref[0, :share, 2 * share :] = to_code(beside[1] * factor)
    corner = jnp.sum(jnp.where(column == row, jnp.round(lower), 0.0), axis=0, keepdims=True)
    line = jnp.concatenate([as_line(power), corner, jnp.zeros((1, share), F32)], axis=1)
    code_ref[0, share:, :] = to_code(jnp.broadcast_to(line, (GROUP, 3 * share)))


def decode_folded(place, code_ref, nodes, share):
    line = from_code(code_ref[0, share:, :])[0:1, :]
    step = jnp.exp2(0.125 * as_column(line[:, :share])) * (1.0 / CODE)
    both = from_code(code_ref[0, :share, 0:share]) * step
    turned = jnp.transpose(both)
    corner = as_column(line[:, share : 2 * share]) * step
    row = lax.broadcasted_iota(I32, (share, share), 0)
    column = lax.broadcasted_iota(I32, (share, share), 1)
    squares = [
        jnp.where(column >= row, both, turned),
        jnp.where(column < row, both, jnp.where(column == row, corner, turned)),
    ]
    values = []
    for q in range(2):
        beside = from_code(code_ref[0, :share, (1 + q) * share : (2 + q) * share]) * step
        first = place == 0
        values.append(
            jnp.concatenate(
                [jnp.where(first, squares[q], beside), jnp.where(first, beside, squares[q])], axis=1
            )
        )
    return values


def own_kernel(place_ref, part_ref, plain_ref, scaled_ref, own_ref, total=None):
    nodes, share, _ = part_ref.shape
    at = pl.multiple_of(place_ref[0] * share, share)
    for q in range(nodes):
        own_ref[q] = part_ref[q] + Product(scaled_ref.at[q], plain_ref.at[q], total).rows(at, share)


def node_kernel(decode, place_ref, own_ref, code_ref, out_ref, node_ref):
    nodes, share, _ = own_ref.shape
    arrived = decode(place_ref[0], code_ref, nodes, share)
    for q in range(nodes):
        value = own_ref[q] + arrived[q]
        node_ref[q] = value
        out_ref[:, q, :] = value


def merge_kernel(decode, place_ref, sibling_ref, node_ref, own_ref, code_ref, out_ref, partner_ref):
    nodes, share, _ = own_ref.shape
    arrived = decode(place_ref[0], code_ref, nodes, share)
    for q in range(nodes):
        partner_ref[q] = own_ref[q] + arrived[q]
    for q in range(nodes):
        out_ref[:, q, :] = node_ref[q] + partner_ref[sibling_ref[0, q]]


def call(kernel, out_shape, in_specs, flops=0, moved=1 << 20, **more):
    outs = jax.tree.map(lambda _: VMEM, out_shape)
    more.setdefault("out_specs", outs)
    return pl.pallas_call(
        kernel,
        out_shape=out_shape,
        in_specs=in_specs,
        compiler_params=pltpu.CompilerParams(vmem_limit_bytes=32 << 20),
        cost_estimate=pl.CostEstimate(flops=flops, bytes_accessed=moved, transcendentals=0),
        **more,
    )


def shards(leaf_rows, leaf_weight, branching, sibling, node_block, na_rows, na_weight, na_route):
    leaf_count, blk_count = lax.axis_size("leaf"), lax.axis_size("blk")
    node_dev, most_children, depth, state = leaf_rows.shape
    count = na_rows.shape[0]
    share = state // blk_count
    peers = blk_count - 1
    plan = Plan(leaf_count, node_dev, 3 * count // (2 * leaf_count * node_dev), state)
    place = lax.axis_index("blk").astype(I32).reshape(1)
    whole = [pltpu.VMEM((state, state), F32)] if share % LANES else []
    shape = jax.ShapeDtypeStruct

    with jax.named_scope("bucket"):
        blocks = call(
            functools.partial(bucket_kernel, plan),
            shape((leaf_count, plan.block, LANES), BF16),
            [VMEM, VMEM, VMEM],
            flops=2 * plan.leaf_count * plan.rows * count * state,
        )(na_route.reshape(1, count), na_weight.reshape(1, count), na_rows)
    got = lax.all_to_all(blocks, "leaf", split_axis=0, concat_axis=0, tiled=True)

    with jax.named_scope("leaf_products"):
        own_part, send_part = call(
            leaf_kernel,
            (shape((node_dev, share, state), F32), shape((peers, node_dev, share, state), F32)),
            [
                SMEM,
                SMEM,
                pl.BlockSpec((1, most_children, depth), lambda n: (n, 0, 0)),
                pl.BlockSpec((1, most_children, depth, state), lambda n: (n, 0, 0, 0)),
                pl.BlockSpec((1, share, state), lambda n: (n, 0, 0)),
            ],
            out_specs=(
                pl.BlockSpec((1, share, state), lambda n: (n, 0, 0)),
                pl.BlockSpec((peers, 1, share, state), lambda n: (0, n, 0, 0)),
            ),
            grid=(node_dev,),
            scratch_shapes=[pltpu.VMEM((state, state), F32)],
            flops=2 * node_dev * most_children * depth * state * state,
            moved=8 << 20,
        )(place, branching, leaf_weight, leaf_rows, jnp.transpose(node_block, (1, 0, 2)))

    folded = blk_count == 2 and node_dev == 2 and share % LANES == 0
    decode = decode_folded if folded else decode_plain
    code_shape = (share + GROUP, 3 * share) if folded else (node_dev * (share + GROUP), state)
    with jax.named_scope("routed_send"):
        code, plain, scaled = call(
            functools.partial(send_folded if folded else send_plain, plan),
            (
                shape((peers, *code_shape), jnp.int16),
                shape((node_dev, max(plan.depth), state), BF16),
                shape((node_dev, max(plan.depth), state), BF16),
            ),
            [SMEM, VMEM, VMEM],
            scratch_shapes=whole,
            flops=2 * node_dev * max(plan.depth) * state * state,
        )(place, got, send_part)
    arrived = [
        lax.ppermute(code[e - 1], "blk", [(i, i ^ e) for i in range(blk_count)])
        for e in range(1, blk_count)
    ]
    arrived = jnp.stack(arrived) if peers > 1 else arrived[0][None]
    with jax.named_scope("routed_own"):
        own = call(
            own_kernel,
            shape((node_dev, share, state), F32),
            [SMEM, VMEM, VMEM, VMEM],
            scratch_shapes=whole,
            flops=2 * node_dev * max(plan.depth) * share * state,
        )(place, own_part, plain, scaled)
    to_partner = [(i, i ^ 1) for i in range(leaf_count)]
    partner_own = lax.ppermute(own, "leaf", to_partner)
    partner_arrived = lax.ppermute(arrived, "leaf", to_partner)
    with jax.named_scope("node"):
        node_schur, node = call(
            functools.partial(node_kernel, decode),
            (shape((share, node_dev, state), F32), shape((node_dev, share, state), F32)),
            [SMEM, VMEM, VMEM],
        )(place, own, arrived)
    with jax.named_scope("merge"):
        merged = call(
            functools.partial(merge_kernel, decode),
            shape((share, node_dev, state), F32),
            [SMEM, SMEM, VMEM, VMEM, VMEM],
            scratch_shapes=[pltpu.VMEM((node_dev, share, state), F32)],
        )(place, sibling, node, partner_own, partner_arrived)
    return (node_schur, merged)


def solution(mesh):
    return jax.shard_map(
        shards,
        mesh=mesh,
        in_specs=(
            P("leaf", None, "blk", None),
            P("leaf", None, "blk"),
            P("leaf"),
            P("leaf", None),
            P("blk", "leaf", None),
            P(("leaf", "blk"), None),
            P(("leaf", "blk")),
            P(("leaf", "blk"), None),
        ),
        out_specs=(P("blk", "leaf", None), P("blk", "leaf", None)),
        check_vma=False,
    )
```

```python
import functools

import jax
import jax.numpy as jnp
from jax import lax
from jax.experimental import pallas as pl
from jax.experimental.pallas import tpu as pltpu
from jax.sharding import PartitionSpec as P

F32 = jnp.float32
BF16 = jnp.bfloat16
I32 = jnp.int32
LANES = 128
GROUP = 16
EXTRA = 8
VMEM = pl.BlockSpec(memory_space=pltpu.VMEM)
SMEM = pl.BlockSpec(memory_space=pltpu.SMEM)
CODE = 32000.0


class Plan:
    def __init__(self, leaf_count, node_dev, capacity, state):
        self.leaf_count, self.node_dev, self.capacity, self.state = leaf_count, node_dev, capacity, state
        self.full = capacity // GROUP * GROUP
        self.rest = capacity - self.full
        self.rows = -(-node_dev * capacity // GROUP) * GROUP
        self.groups = self.rows // GROUP
        self.slabs = state // LANES
        self.block = self.slabs * self.rows + EXTRA
        self.groups_of = [
            [g for g in range(self.groups) if q in {self.node_at(g * GROUP + i) for i in range(GROUP)}]
            for q in range(node_dev)
        ]
        self.depth = [leaf_count * GROUP * len(g) for g in self.groups_of]

    def node_at(self, row):
        if row < self.node_dev * self.full:
            return row // self.full
        return min((row - self.node_dev * self.full) // self.rest, self.node_dev - 1) if self.rest else 0


def dot_t(a, b):
    return lax.dot_general(a, b, (((0,), (0,)), ((), ())), preferred_element_type=F32)


def bucket_kernel(plan, route_hbm, weight_hbm, rows_hbm, out_ref, route_ref, weight_ref, rows_ref, sems):
    count = rows_hbm.shape[0]
    state = plan.state
    copies = [
        pltpu.make_async_copy(route_hbm, route_ref, sems.at[0]),
        pltpu.make_async_copy(weight_hbm, weight_ref, sems.at[1]),
        pltpu.make_async_copy(rows_hbm, rows_ref.at[:, pl.ds(0, state)], sems.at[2]),
    ]
    for copy in copies:
        copy.start()
    nodes = plan.leaf_count * plan.node_dev
    before = (
        lax.broadcasted_iota(I32, (count, count), 0) < lax.broadcasted_iota(I32, (count, count), 1)
    ).astype(BF16)
    copies[0].wait()
    route = route_ref[...]
    member = lax.broadcasted_iota(I32, (nodes, count), 0) == route
    seen = jnp.dot(member.astype(BF16), before, preferred_element_type=F32)
    position = jnp.sum(jnp.where(member, seen, 0.0), axis=0, keepdims=True).astype(I32)
    owner = route // plan.node_dev
    q = route - owner * plan.node_dev
    slot = owner * plan.rows + jnp.where(
        position < plan.full,
        q * plan.full + position,
        plan.node_dev * plan.full + q * plan.rest + position - plan.full,
    )
    total = plan.leaf_count * plan.rows
    hit = jnp.where(lax.broadcasted_iota(I32, (total, count), 0) == slot, 1.0, 0.0).astype(BF16)
    copies[1].wait()
    rows_ref[:, state:] = dot_t(weight_ref[...], jnp.ones((1, LANES), BF16)).astype(BF16)
    copies[2].wait()
    filled = jnp.dot(hit, rows_ref[...], preferred_element_type=F32)
    weights = filled[:, state:]
    filled = filled[:, :state].astype(BF16)
    lane = lax.broadcasted_iota(I32, (EXTRA, LANES), 1)
    sub = lax.broadcasted_iota(I32, (EXTRA, LANES), 0)
    want = []
    for g in range(plan.rows // EXTRA):
        q_of = jnp.full((EXTRA, LANES), plan.node_at(g * EXTRA), I32)
        for i in range(1, EXTRA):
            step = plan.node_at(g * EXTRA + i) - plan.node_at(g * EXTRA + i - 1)
            if step:
                q_of = q_of + jnp.where(sub >= i, step, 0)
        want.append(lane == g * plan.node_dev + q_of)
    for d in range(plan.leaf_count):
        at = d * plan.rows
        for c in range(plan.slabs):
            out_ref[d, c * plan.rows : (c + 1) * plan.rows, :] = filled[
                at : at + plan.rows, c * LANES : (c + 1) * LANES
            ]
        extra = jnp.zeros((EXTRA, LANES), F32)
        for g in range(plan.rows // EXTRA):
            extra = jnp.where(want[g], weights[at + g * EXTRA : at + (g + 1) * EXTRA, :], extra)
        out_ref[d, plan.slabs * plan.rows :, :] = extra.astype(BF16)


def leaf_kernel(place_ref, branching_ref, weight_ref, rows_ref, block_ref, own_ref, send_ref, total):
    n = pl.program_id(0)
    share = own_ref.shape[1]
    peers = send_ref.shape[0]
    blk = place_ref[0]
    columns = jnp.transpose(weight_ref[0].astype(F32))
    total[...] = jnp.zeros_like(total)
    for b in range(rows_ref.shape[1]):

        @pl.when(b < branching_ref[n])
        def _():
            rows = rows_ref[0, b]
            scaled = (rows.astype(F32) * columns[:, b : b + 1]).astype(BF16)
            total[...] += dot_t(scaled, rows)

    own_ref[0] = total[pl.ds(pl.multiple_of(blk * share, share), share), :] + block_ref[0].astype(F32)
    for e in range(1, peers + 1):
        at = pl.multiple_of((blk ^ e) * share, share)
        send_ref[e - 1, 0] = total[pl.ds(at, share), :]


class Product:
    def __init__(self, scaled_ref, plain_ref, total):
        self.scaled_ref, self.plain_ref, self.total = scaled_ref, plain_ref, total
        if total is not None:
            total[...] = dot_t(scaled_ref[...], plain_ref[...])

    def rows(self, at, share):
        if self.total is not None:
            return self.total[pl.ds(at, share), :]
        return dot_t(self.scaled_ref[:, pl.ds(at, share)], self.plain_ref[...])


def gather_rows(plan, got_ref, plain_ref, scaled_ref):
    for d in range(plan.leaf_count):
        extra = got_ref[d, plan.slabs * plan.rows :, :].astype(F32)
        for g in range(plan.groups):
            rows = jnp.concatenate(
                [
                    got_ref[d, c * plan.rows + g * GROUP : c * plan.rows + (g + 1) * GROUP, :]
                    for c in range(plan.slabs)
                ],
                axis=1,
            )
            wide = rows.astype(F32)
            for q in range(plan.node_dev):
                if g not in plan.groups_of[q]:
                    continue
                at = (plan.groups_of[q].index(g) * plan.leaf_count + d) * GROUP
                first = g * GROUP // EXTRA * plan.node_dev + q
                places = range(first, first + GROUP // EXTRA * plan.node_dev, plan.node_dev)
                weight = jnp.concatenate([extra[:, j : j + 1] for j in places], axis=0)
                plain_ref[q, at : at + GROUP, :] = rows
                scaled_ref[q, at : at + GROUP, :] = (wide * weight).astype(BF16)


def scale_of(most):
    power = jnp.ceil(8.0 * jnp.log2(jnp.maximum(most, 1e-30)))
    return power, CODE * jnp.exp2(-0.125 * power)


def to_code(value):
    return jnp.round(value).astype(I32).astype(jnp.int16)


def from_code(code):
    return code.astype(I32).astype(F32)


def diagonal(width):
    return lax.broadcasted_iota(I32, (width, width), 0) == lax.broadcasted_iota(I32, (width, width), 1)


def as_line(column):
    return jnp.sum(jnp.where(diagonal(column.shape[0]), column, 0.0), axis=0, keepdims=True)


def as_column(line):
    return jnp.sum(jnp.where(diagonal(line.shape[1]), line, 0.0), axis=1, keepdims=True)


def send_plain(plan, place_ref, got_ref, part_ref, code_ref, plain_ref, scaled_ref, total=None):
    blk = place_ref[0]
    peers, nodes, share, state = part_ref.shape
    gather_rows(plan, got_ref, plain_ref, scaled_ref)
    for q in range(nodes):
        product = Product(scaled_ref.at[q], plain_ref.at[q], total)
        for e in range(1, peers + 1):
            at = pl.multiple_of((blk ^ e) * share, share)
            value = part_ref[e - 1, q] + product.rows(at, share)
            power, factor = scale_of(jnp.max(jnp.abs(value), axis=1, keepdims=True))
            code_ref[e - 1, q * share : (q + 1) * share, :] = to_code(value * factor)
            line = jnp.concatenate([as_line(power), jnp.zeros((1, state - share), F32)], axis=1)
            base = nodes * share + q * GROUP
            code_ref[e - 1, base : base + GROUP, :] = to_code(jnp.broadcast_to(line, (GROUP, state)))


def decode_plain(code_ref, nodes, share):
    values = []
    for q in range(nodes):
        base = nodes * share + q * GROUP
        value = None
        for e in range(code_ref.shape[0]):
            power = as_column(from_code(code_ref[e, base : base + GROUP, :])[0:1, :share])
            term = from_code(code_ref[e, q * share : (q + 1) * share, :]) * (
                jnp.exp2(0.125 * power) * (1.0 / CODE)
            )
            value = term if value is None else value + term
        values.append(value)
    return values


def send_folded(plan, place_ref, got_ref, part_ref, first_ref, second_ref, plain_ref, scaled_ref):
    share = part_ref.shape[2]
    half = share // 2
    mine = pl.ds(pl.multiple_of(place_ref[0] * share, share), share)
    theirs = pl.ds(pl.multiple_of((1 - place_ref[0]) * share, share), share)
    gather_rows(plan, got_ref, plain_ref, scaled_ref)
    square, beside = [], []
    for q in range(2):
        scaled = scaled_ref[q, :, theirs]
        square.append(part_ref[0, q, :, theirs] + dot_t(scaled, plain_ref[q, :, theirs]))
        beside.append(part_ref[0, q, :, mine] + dot_t(scaled, plain_ref[q, :, mine]))
    up, low = slice(0, half), slice(half, share)
    encode_part(
        first_ref, square[0][up, up], square[1][up, up], [s[up, low] for s in square] + [s[up, :] for s in beside]
    )
    encode_part(second_ref, square[0][low, low], square[1][low, low], [s[low, :] for s in beside])


def encode_part(code_ref, upper, lower, others):
    half = upper.shape[0]
    width = upper.shape[1]
    pieces = [o[:, c : c + width] for o in others for c in range(0, o.shape[1], width)]
    most = jnp.maximum(jnp.abs(upper), jnp.abs(lower))
    for piece in pieces:
        most = jnp.maximum(most, jnp.abs(piece))
    power, factor = scale_of(jnp.max(most, axis=1, keepdims=True))
    row = lax.broadcasted_iota(I32, (half, width), 0)
    column = lax.broadcasted_iota(I32, (half, width), 1)
    lower = lower * factor
    code_ref[:half, :] = to_code(jnp.where(column >= row, upper * factor, lower))
    for k, piece in enumerate(pieces):
        code_ref[(k + 1) * half : (k + 2) * half, :] = to_code(piece * factor)
    corner = jnp.sum(jnp.where(column == row, jnp.round(lower), 0.0), axis=0, keepdims=True)
    line = lax.broadcasted_iota(I32, (GROUP, width), 0)
    code_ref[(len(pieces) + 1) * half :, :] = to_code(
        jnp.where(line == 0, as_line(power), jnp.where(line == 1, corner, 0.0))
    )


def decode_part(code_ref):
    width = code_ref.shape[1]
    half = width
    count = code_ref.shape[0] // half
    lines = from_code(code_ref[count * half :, :])
    step = jnp.exp2(0.125 * as_column(lines[0:1, :])) * (1.0 / CODE)
    pieces = [from_code(code_ref[k * half : (k + 1) * half, :]) * step for k in range(count)]
    both = pieces[0]
    turned = jnp.transpose(both)
    corner = as_column(lines[1:2, :]) * step
    row = lax.broadcasted_iota(I32, (half, width), 0)
    column = lax.broadcasted_iota(I32, (half, width), 1)
    squares = [
        jnp.where(column >= row, both, turned),
        jnp.where(column < row, both, jnp.where(column == row, corner, turned)),
    ]
    return squares, pieces[1:]


def first_node_kernel(
    place_ref, part_ref, plain_ref, scaled_ref, code_ref, out_ref, node_ref, rest_ref
):
    share = part_ref.shape[1]
    half = share // 2
    at = pl.multiple_of(place_ref[0] * share, share)
    to = pl.multiple_of((1 - place_ref[0]) * share, share)
    squares, pieces = decode_part(code_ref)
    for q in range(2):
        own = part_ref[q] + dot_t(scaled_ref[q, :, pl.ds(at, share)], plain_ref[q])
        node_ref[q] = own[:half, :]
        rest_ref[q] = own[half:, :]
        node_ref[q, :, pl.ds(at, half)] += squares[q]
        node_ref[q, :, pl.ds(at + half, half)] += pieces[q]
        node_ref[q, :, pl.ds(to, half)] += pieces[2 + 2 * q]
        node_ref[q, :, pl.ds(to + half, half)] += pieces[3 + 2 * q]
        rest_ref[q, :, pl.ds(at, half)] += jnp.transpose(pieces[q])
        out_ref[:, q, :] = node_ref[q]


def add_second(place, code_ref, rest_ref, node_ref):
    half = rest_ref.shape[1]
    at = pl.multiple_of(place * 2 * half, half)
    to = pl.multiple_of((1 - place) * 2 * half, half)
    squares, pieces = decode_part(code_ref)
    for q in range(2):
        node_ref[q] = rest_ref[q]
        node_ref[q, :, pl.ds(at + half, half)] += squares[q]
        node_ref[q, :, pl.ds(to, half)] += pieces[2 * q]
        node_ref[q, :, pl.ds(to + half, half)] += pieces[2 * q + 1]


def second_node_kernel(place_ref, rest_ref, code_ref, _, out_ref, node_ref):
    add_second(place_ref[0], code_ref, rest_ref, node_ref)
    for q in range(2):
        out_ref[:, q, :] = node_ref[q]


def first_merge_kernel(sibling_ref, node_ref, partner_ref, out_ref):
    for q in range(2):
        out_ref[:, q, :] = node_ref[q] + partner_ref[sibling_ref[0, q]]


def second_merge_kernel(place_ref, sibling_ref, node_ref, rest_ref, code_ref, _, out_ref, partner_ref):
    add_second(place_ref[0], code_ref, rest_ref, partner_ref)
    for q in range(2):
        out_ref[:, q, :] = node_ref[q] + partner_ref[sibling_ref[0, q]]


def own_kernel(place_ref, part_ref, plain_ref, scaled_ref, own_ref, total=None):
    nodes, share, _ = part_ref.shape
    at = pl.multiple_of(place_ref[0] * share, share)
    for q in range(nodes):
        own_ref[q] = part_ref[q] + Product(scaled_ref.at[q], plain_ref.at[q], total).rows(at, share)


def node_kernel(own_ref, code_ref, out_ref, node_ref):
    nodes, share, _ = own_ref.shape
    arrived = decode_plain(code_ref, nodes, share)
    for q in range(nodes):
        value = own_ref[q] + arrived[q]
        node_ref[q] = value
        out_ref[:, q, :] = value


def merge_kernel(sibling_ref, node_ref, own_ref, code_ref, out_ref, partner_ref):
    nodes, share, _ = own_ref.shape
    arrived = decode_plain(code_ref, nodes, share)
    for q in range(nodes):
        partner_ref[q] = own_ref[q] + arrived[q]
    for q in range(nodes):
        out_ref[:, q, :] = node_ref[q] + partner_ref[sibling_ref[0, q]]


def call(kernel, out_shape, in_specs, flops=0, moved=1 << 20, vmem=32 << 20, **more):
    outs = jax.tree.map(lambda _: VMEM, out_shape)
    more.setdefault("out_specs", outs)
    return pl.pallas_call(
        kernel,
        out_shape=out_shape,
        in_specs=in_specs,
        compiler_params=pltpu.CompilerParams(vmem_limit_bytes=vmem),
        cost_estimate=pl.CostEstimate(flops=flops, bytes_accessed=moved, transcendentals=0),
        **more,
    )


def exchange_plain(plan, place, got, own_part, send_part, sibling, blk_count):
    peers, node_dev, share, state = send_part.shape
    shape = jax.ShapeDtypeStruct
    whole = [pltpu.VMEM((state, state), F32)] if share % LANES else []
    depth = max(plan.depth)
    to_partner = [(i, i ^ 1) for i in range(plan.leaf_count)]
    with jax.named_scope("routed_send"):
        code, plain, scaled = call(
            functools.partial(send_plain, plan),
            (
                shape((peers, node_dev * (share + GROUP), state), jnp.int16),
                shape((node_dev, depth, state), BF16),
                shape((node_dev, depth, state), BF16),
            ),
            [SMEM, VMEM, VMEM],
            scratch_shapes=whole,
            flops=2 * node_dev * depth * state * state,
        )(place, got, send_part)
    arrived = jnp.stack(
        [
            lax.ppermute(code[e - 1], "blk", [(i, i ^ e) for i in range(blk_count)])
            for e in range(1, blk_count)
        ]
    )
    with jax.named_scope("routed_own"):
        own = call(
            own_kernel,
            shape((node_dev, share, state), F32),
            [SMEM, VMEM, VMEM, VMEM],
            scratch_shapes=whole,
            flops=2 * node_dev * depth * share * state,
        )(place, own_part, plain, scaled)
    partner_own = lax.ppermute(own, "leaf", to_partner)
    partner_arrived = lax.ppermute(arrived, "leaf", to_partner)
    with jax.named_scope("node"):
        node_schur, node = call(
            node_kernel,
            (shape((share, node_dev, state), F32), shape((node_dev, share, state), F32)),
            [VMEM, VMEM],
        )(own, arrived)
    with jax.named_scope("merge"):
        merged = call(
            merge_kernel,
            shape((share, node_dev, state), F32),
            [SMEM, VMEM, VMEM, VMEM],
            scratch_shapes=[pltpu.VMEM((node_dev, share, state), F32)],
        )(sibling, node, partner_own, partner_arrived)
    return node_schur, merged


def exchange_folded(plan, place, got, own_part, send_part, sibling):
    _, node_dev, share, state = send_part.shape
    half = share // 2
    shape = jax.ShapeDtypeStruct
    depth = max(plan.depth)
    to_partner = [(i, i ^ 1) for i in range(plan.leaf_count)]
    across = [(0, 1), (1, 0)]
    result = shape((share, node_dev, state), F32)
    rows = shape((node_dev, half, state), F32)
    any_spec = pl.BlockSpec(memory_space=pl.ANY)
    part = [pl.BlockSpec((half, node_dev, state), lambda i, k=k: (k, 0, 0)) for k in range(2)]
    with jax.named_scope("routed_send"):
        first, second, plain, scaled = call(
            functools.partial(send_folded, plan),
            (
                shape((7 * half + GROUP, half), jnp.int16),
                shape((5 * half + GROUP, half), jnp.int16),
                shape((node_dev, depth, state), BF16),
                shape((node_dev, depth, state), BF16),
            ),
            [SMEM, VMEM, VMEM],
            flops=2 * node_dev * depth * share * state,
        )(place, got, send_part)
    first = lax.ppermute(first, "blk", across)
    second = lax.ppermute(second, "blk", across)
    with jax.named_scope("first_node"):
        node_schur, node, rest = call(
            first_node_kernel,
            (result, rows, rows),
            [SMEM, VMEM, VMEM, VMEM, VMEM],
            out_specs=(part[0], VMEM, VMEM),
            grid=(1,),
            flops=2 * node_dev * depth * share * state,
        )(place, own_part, plain, scaled, first)
    partner_node = lax.ppermute(node, "leaf", to_partner)
    partner_rest = lax.ppermute(rest, "leaf", to_partner)
    with jax.named_scope("first_merge"):
        merged = call(
            first_merge_kernel, result, [SMEM, VMEM, VMEM], out_specs=part[0], grid=(1,)
        )(sibling, node, partner_node)
    partner_second = lax.ppermute(second, "leaf", to_partner)
    with jax.named_scope("second_node"):
        node_schur, node = call(
            second_node_kernel,
            (result, rows),
            [SMEM, VMEM, VMEM, any_spec],
            out_specs=(part[1], VMEM),
            grid=(1,),
            input_output_aliases={3: 0},
        )(place, rest, second, node_schur)
    with jax.named_scope("second_merge"):
        merged = call(
            second_merge_kernel,
            result,
            [SMEM, SMEM, VMEM, VMEM, VMEM, any_spec],
            out_specs=part[1],
            grid=(1,),
            scratch_shapes=[pltpu.VMEM((node_dev, half, state), F32)],
            input_output_aliases={5: 0},
        )(place, sibling, node, partner_rest, partner_second, merged)
    return node_schur, merged


def shards(leaf_rows, leaf_weight, branching, sibling, node_block, na_rows, na_weight, na_route):
    leaf_count, blk_count = lax.axis_size("leaf"), lax.axis_size("blk")
    node_dev, most_children, depth, state = leaf_rows.shape
    count = na_rows.shape[0]
    share = state // blk_count
    peers = blk_count - 1
    plan = Plan(leaf_count, node_dev, 3 * count // (2 * leaf_count * node_dev), state)
    place = lax.axis_index("blk").astype(I32).reshape(1)
    shape = jax.ShapeDtypeStruct
    any_spec = pl.BlockSpec(memory_space=pl.ANY)

    with jax.named_scope("bucket"):
        blocks = call(
            functools.partial(bucket_kernel, plan),
            shape((leaf_count, plan.block, LANES), BF16),
            [any_spec, any_spec, any_spec],
            scratch_shapes=[
                pltpu.VMEM((1, count), I32),
                pltpu.VMEM((1, count), BF16),
                pltpu.VMEM((count, state + LANES), BF16),
                pltpu.SemaphoreType.DMA((3,)),
            ],
            vmem=60 << 20,
            flops=2 * plan.leaf_count * plan.rows * count * state,
        )(na_route.reshape(1, count), na_weight.reshape(1, count), na_rows)
    got = lax.all_to_all(blocks, "leaf", split_axis=0, concat_axis=0, tiled=True)

    with jax.named_scope("leaf_products"):
        own_part, send_part = call(
            leaf_kernel,
            (shape((node_dev, share, state), F32), shape((peers, node_dev, share, state), F32)),
            [
                SMEM,
                SMEM,
                pl.BlockSpec((1, most_children, depth), lambda n: (n, 0, 0)),
                pl.BlockSpec((1, most_children, depth, state), lambda n: (n, 0, 0, 0)),
                pl.BlockSpec((1, share, state), lambda n: (n, 0, 0)),
            ],
            out_specs=(
                pl.BlockSpec((1, share, state), lambda n: (n, 0, 0)),
                pl.BlockSpec((peers, 1, share, state), lambda n: (0, n, 0, 0)),
            ),
            grid=(node_dev,),
            scratch_shapes=[pltpu.VMEM((state, state), F32)],
            flops=2 * node_dev * most_children * depth * state * state,
            moved=8 << 20,
        )(place, branching, leaf_weight, leaf_rows, jnp.transpose(node_block, (1, 0, 2)))

    if blk_count == 2 and node_dev == 2 and share == 2 * LANES:
        return exchange_folded(plan, place, got, own_part, send_part, sibling)
    return exchange_plain(plan, place, got, own_part, send_part, sibling, blk_count)


def solution(mesh):
    return jax.shard_map(
        shards,
        mesh=mesh,
        in_specs=(
            P("leaf", None, "blk", None),
            P("leaf", None, "blk"),
            P("leaf"),
            P("leaf", None),
            P("blk", "leaf", None),
            P(("leaf", "blk"), None),
            P(("leaf", "blk")),
            P(("leaf", "blk"), None),
        ),
        out_specs=(P("blk", "leaf", None), P("blk", "leaf", None)),
        check_vma=False,
    )
```

```python
import functools

import jax
import jax.numpy as jnp
from jax import lax
from jax.experimental import pallas as pl
from jax.experimental.pallas import tpu as pltpu
from jax.sharding import PartitionSpec as P

F32 = jnp.float32
BF16 = jnp.bfloat16
I32 = jnp.int32
LANES = 128
GROUP = 16
EXTRA = 8
PIECES = 4
VMEM = pl.BlockSpec(memory_space=pltpu.VMEM)
SMEM = pl.BlockSpec(memory_space=pltpu.SMEM)
CODE = 32000.0
LONG = 20_000_000_000


class Plan:
    def __init__(self, leaf_count, node_dev, capacity, state):
        self.leaf_count, self.node_dev, self.capacity, self.state = leaf_count, node_dev, capacity, state
        self.full = capacity // GROUP * GROUP
        self.rest = capacity - self.full
        self.rows = -(-node_dev * capacity // GROUP) * GROUP
        self.groups = self.rows // GROUP
        self.slabs = state // LANES
        self.block = self.slabs * self.rows + EXTRA
        self.groups_of = [
            [g for g in range(self.groups) if q in {self.node_at(g * GROUP + i) for i in range(GROUP)}]
            for q in range(node_dev)
        ]
        self.depth = [leaf_count * GROUP * len(g) for g in self.groups_of]

    def node_at(self, row):
        if row < self.node_dev * self.full:
            return row // self.full
        return min((row - self.node_dev * self.full) // self.rest, self.node_dev - 1) if self.rest else 0


def dot_t(a, b):
    return lax.dot_general(a, b, (((0,), (0,)), ((), ())), preferred_element_type=F32)


def bucket_kernel(plan, route_hbm, weight_hbm, rows_hbm, out_hbm, route_ref, weight_ref, rows_ref, out_ref, sems):
    count = rows_hbm.shape[0]
    state = plan.state
    copies = [
        pltpu.make_async_copy(route_hbm, route_ref, sems.at[0]),
        pltpu.make_async_copy(weight_hbm, weight_ref, sems.at[1]),
        pltpu.make_async_copy(rows_hbm, rows_ref.at[:, pl.ds(0, state)], sems.at[2]),
    ]
    for copy in copies:
        copy.start()
    nodes = plan.leaf_count * plan.node_dev
    before = (
        lax.broadcasted_iota(I32, (count, count), 0) < lax.broadcasted_iota(I32, (count, count), 1)
    ).astype(BF16)
    copies[0].wait()
    route = route_ref[...]
    member = lax.broadcasted_iota(I32, (nodes, count), 0) == route
    seen = jnp.dot(member.astype(BF16), before, preferred_element_type=F32)
    position = jnp.sum(jnp.where(member, seen, 0.0), axis=0, keepdims=True).astype(I32)
    owner = route // plan.node_dev
    q = route - owner * plan.node_dev
    slot = owner * plan.rows + jnp.where(
        position < plan.full,
        q * plan.full + position,
        plan.node_dev * plan.full + q * plan.rest + position - plan.full,
    )
    copies[1].wait()
    weight = weight_ref[...].reshape(1, count)
    rows_ref[:, state:] = dot_t(weight, jnp.ones((1, LANES), BF16)).astype(BF16)
    lane = lax.broadcasted_iota(I32, (EXTRA, LANES), 1)
    sub = lax.broadcasted_iota(I32, (EXTRA, LANES), 0)
    want = []
    for g in range(plan.rows // EXTRA):
        q_of = jnp.full((EXTRA, LANES), plan.node_at(g * EXTRA), I32)
        for i in range(1, EXTRA):
            step = plan.node_at(g * EXTRA + i) - plan.node_at(g * EXTRA + i - 1)
            if step:
                q_of = q_of + jnp.where(sub >= i, step, 0)
        want.append(lane == g * plan.node_dev + q_of)
    copies[2].wait()
    each = plan.leaf_count // PIECES
    leaving = []
    for p in range(PIECES):
        place = lax.broadcasted_iota(I32, (each * plan.rows, count), 0) + p * each * plan.rows
        hit = jnp.where(place == slot, 1.0, 0.0).astype(BF16)
        filled = jnp.dot(hit, rows_ref[...], preferred_element_type=F32)
        weights = filled[:, state:]
        filled = filled[:, :state].astype(BF16)
        for i in range(each):
            at = i * plan.rows
            d = p * each + i
            for c in range(plan.slabs):
                out_ref[d, c * plan.rows : (c + 1) * plan.rows, :] = filled[
                    at : at + plan.rows, c * LANES : (c + 1) * LANES
                ]
            extra = jnp.zeros((EXTRA, LANES), F32)
            for g in range(plan.rows // EXTRA):
                extra = jnp.where(want[g], weights[at + g * EXTRA : at + (g + 1) * EXTRA, :], extra)
            out_ref[d, plan.slabs * plan.rows :, :] = extra.astype(BF16)
        span = pl.ds(p * each, each)
        leaving.append(pltpu.make_async_copy(out_ref.at[span], out_hbm.at[span], sems.at[3 + p]))
        leaving[-1].start()
    for copy in leaving:
        copy.wait()


def leaf_kernel(place_ref, branching_ref, weight_ref, rows_ref, block_ref, own_ref, send_ref, total):
    n = pl.program_id(0)
    share = own_ref.shape[1]
    peers = send_ref.shape[0]
    blk = place_ref[0]
    columns = jnp.transpose(weight_ref[0].astype(F32))
    total[...] = jnp.zeros_like(total)
    for b in range(rows_ref.shape[1]):

        @pl.when(b < branching_ref[n])
        def _():
            rows = rows_ref[0, b]
            scaled = (rows.astype(F32) * columns[:, b : b + 1]).astype(BF16)
            total[...] += dot_t(scaled, rows)

    own_ref[0] = total[pl.ds(pl.multiple_of(blk * share, share), share), :] + block_ref[0].astype(F32)
    for e in range(1, peers + 1):
        at = pl.multiple_of((blk ^ e) * share, share)
        send_ref[e - 1, 0] = total[pl.ds(at, share), :]


class Product:
    def __init__(self, scaled_ref, plain_ref, total):
        self.scaled_ref, self.plain_ref, self.total = scaled_ref, plain_ref, total
        if total is not None:
            total[...] = dot_t(scaled_ref[...], plain_ref[...])

    def rows(self, at, share):
        if self.total is not None:
            return self.total[pl.ds(at, share), :]
        return dot_t(self.scaled_ref[:, pl.ds(at, share)], self.plain_ref[...])


def gather_rows(plan, got_ref, plain_ref, scaled_ref):
    for d in range(plan.leaf_count):
        extra = got_ref[d, plan.slabs * plan.rows :, :].astype(F32)
        for g in range(plan.groups):
            rows = jnp.concatenate(
                [
                    got_ref[d, c * plan.rows + g * GROUP : c * plan.rows + (g + 1) * GROUP, :]
                    for c in range(plan.slabs)
                ],
                axis=1,
            )
            wide = rows.astype(F32)
            for q in range(plan.node_dev):
                if g not in plan.groups_of[q]:
                    continue
                at = (plan.groups_of[q].index(g) * plan.leaf_count + d) * GROUP
                first = g * GROUP // EXTRA * plan.node_dev + q
                places = range(first, first + GROUP // EXTRA * plan.node_dev, plan.node_dev)
                weight = jnp.concatenate([extra[:, j : j + 1] for j in places], axis=0)
                plain_ref[q, at : at + GROUP, :] = rows
                scaled_ref[q, at : at + GROUP, :] = (wide * weight).astype(BF16)


def scale_of(most):
    power = jnp.ceil(8.0 * jnp.log2(jnp.maximum(most, 1e-30)))
    return power, CODE * jnp.exp2(-0.125 * power)


def to_code(value):
    return jnp.round(value).astype(I32).astype(jnp.int16)


def from_code(code):
    return code.astype(I32).astype(F32)


def diagonal(width):
    return lax.broadcasted_iota(I32, (width, width), 0) == lax.broadcasted_iota(I32, (width, width), 1)


def as_line(column):
    return jnp.sum(jnp.where(diagonal(column.shape[0]), column, 0.0), axis=0, keepdims=True)


def as_column(line):
    return jnp.sum(jnp.where(diagonal(line.shape[1]), line, 0.0), axis=1, keepdims=True)


def send_plain(plan, place_ref, got_ref, part_ref, code_ref, plain_ref, scaled_ref, total=None):
    blk = place_ref[0]
    peers, nodes, share, state = part_ref.shape
    gather_rows(plan, got_ref, plain_ref, scaled_ref)
    for q in range(nodes):
        product = Product(scaled_ref.at[q], plain_ref.at[q], total)
        for e in range(1, peers + 1):
            at = pl.multiple_of((blk ^ e) * share, share)
            value = part_ref[e - 1, q] + product.rows(at, share)
            power, factor = scale_of(jnp.max(jnp.abs(value), axis=1, keepdims=True))
            code_ref[e - 1, q * share : (q + 1) * share, :] = to_code(value * factor)
            line = jnp.concatenate([as_line(power), jnp.zeros((1, state - share), F32)], axis=1)
            base = nodes * share + q * GROUP
            code_ref[e - 1, base : base + GROUP, :] = to_code(jnp.broadcast_to(line, (GROUP, state)))


def decode_plain(code_ref, nodes, share):
    values = []
    for q in range(nodes):
        base = nodes * share + q * GROUP
        value = None
        for e in range(code_ref.shape[0]):
            power = as_column(from_code(code_ref[e, base : base + GROUP, :])[0:1, :share])
            term = from_code(code_ref[e, q * share : (q + 1) * share, :]) * (
                jnp.exp2(0.125 * power) * (1.0 / CODE)
            )
            value = term if value is None else value + term
        values.append(value)
    return values


def send_folded(plan, place_ref, got_ref, part_ref, code_ref, plain_ref, scaled_ref):
    share = part_ref.shape[2]
    mine = pl.ds(pl.multiple_of(place_ref[0] * share, share), share)
    theirs = pl.ds(pl.multiple_of((1 - place_ref[0]) * share, share), share)
    gather_rows(plan, got_ref, plain_ref, scaled_ref)
    square, beside = [], []
    for q in range(2):
        scaled = scaled_ref[q, :, theirs]
        square.append(part_ref[0, q, :, theirs] + dot_t(scaled, plain_ref[q, :, theirs]))
        beside.append(part_ref[0, q, :, mine] + dot_t(scaled, plain_ref[q, :, mine]))
    most = jnp.maximum(
        jnp.maximum(jnp.abs(square[0]), jnp.abs(square[1])),
        jnp.maximum(jnp.abs(beside[0]), jnp.abs(beside[1])),
    )
    power, factor = scale_of(jnp.max(most, axis=1, keepdims=True))
    row = lax.broadcasted_iota(I32, (share, share), 0)
    column = lax.broadcasted_iota(I32, (share, share), 1)
    lower = square[1] * factor
    code_ref[:share, :] = to_code(jnp.where(column >= row, square[0] * factor, lower))
    for q in range(2):
        code_ref[(q + 1) * share : (q + 2) * share, :] = to_code(beside[q] * factor)
    corner = jnp.sum(jnp.where(column == row, jnp.round(lower), 0.0), axis=0, keepdims=True)
    line = lax.broadcasted_iota(I32, (GROUP, share), 0)
    code_ref[3 * share :, :] = to_code(
        jnp.where(line == 0, as_line(power), jnp.where(line == 1, corner, 0.0))
    )


def decode_folded(code_ref):
    share = code_ref.shape[1]
    lines = from_code(code_ref[3 * share :, :])
    step = jnp.transpose(jnp.exp2(0.125 * jnp.broadcast_to(lines[0:1, :], (8, share))) * (1.0 / CODE))[:, 0:1]
    both = from_code(code_ref[:share, :]) * step
    turned = jnp.transpose(both)
    row = lax.broadcasted_iota(I32, (share, share), 0)
    column = lax.broadcasted_iota(I32, (share, share), 1)
    return step, (
        jnp.where(column >= row, both, turned),
        jnp.where(column < row, both, jnp.where(column == row, lines[1:2, :] * step, turned)),
    )


def leave(out_ref, out_hbm, sems, p):
    each = out_ref.shape[0] // PIECES
    span = pl.ds(p * each, each)
    copy = pltpu.make_async_copy(out_ref.at[span], out_hbm.at[span], sems.at[p])
    copy.start()
    return copy


def node_folded(place_ref, own_ref, code_ref, out_hbm, node_ref, out_ref, sems):
    share = own_ref.shape[1]
    mine = pl.ds(pl.multiple_of(place_ref[0] * share, share), share)
    theirs = pl.ds(pl.multiple_of((1 - place_ref[0]) * share, share), share)
    step, squares = decode_folded(code_ref)
    each = share // PIECES
    copies = []
    for p in range(PIECES):
        rows = slice(p * each, (p + 1) * each)
        for q in range(2):
            beside = from_code(code_ref[(q + 1) * share + p * each : (q + 1) * share + (p + 1) * each, :])
            for columns, term in ((mine, squares[q][rows]), (theirs, beside * step[rows])):
                value = own_ref[q, rows, columns] + term
                out_ref[rows, q, columns] = value
                node_ref[q, rows, columns] = value
        copies.append(leave(out_ref, out_hbm, sems, p))
    for copy in copies:
        copy.wait()


def merge_folded(place_ref, sibling_ref, node_ref, own_ref, code_ref, out_hbm, out_ref, sems):
    share = node_ref.shape[1]
    mine = pl.ds(pl.multiple_of(place_ref[0] * share, share), share)
    theirs = pl.ds(pl.multiple_of((1 - place_ref[0]) * share, share), share)
    step, squares = decode_folded(code_ref)
    each = share // PIECES
    copies = []
    for p in range(PIECES):
        rows = slice(p * each, (p + 1) * each)
        for q in range(2):
            match = sibling_ref[0, q]
            square = jnp.where(match == 0, squares[0][rows], squares[1][rows])
            at = pl.multiple_of((match + 1) * share + p * each, each)
            beside = from_code(code_ref[pl.ds(at, each), :]) * step[rows]
            for columns, term in ((mine, square), (theirs, beside)):
                out_ref[rows, q, columns] = (
                    node_ref[q, rows, columns] + own_ref[match, rows, columns] + term
                )
        copies.append(leave(out_ref, out_hbm, sems, p))
    for copy in copies:
        copy.wait()


def own_kernel(place_ref, part_ref, plain_ref, scaled_ref, own_ref, total=None):
    nodes, share, _ = part_ref.shape
    at = pl.multiple_of(place_ref[0] * share, share)
    for q in range(nodes):
        own_ref[q] = part_ref[q] + Product(scaled_ref.at[q], plain_ref.at[q], total).rows(at, share)


def node_kernel(own_ref, code_ref, out_ref, node_ref):
    nodes, share, _ = own_ref.shape
    arrived = decode_plain(code_ref, nodes, share)
    for q in range(nodes):
        value = own_ref[q] + arrived[q]
        node_ref[q] = value
        out_ref[:, q, :] = value


def merge_kernel(sibling_ref, node_ref, own_ref, code_ref, out_ref, partner_ref):
    nodes, share, _ = own_ref.shape
    arrived = decode_plain(code_ref, nodes, share)
    for q in range(nodes):
        partner_ref[q] = own_ref[q] + arrived[q]
    for q in range(nodes):
        out_ref[:, q, :] = node_ref[q] + partner_ref[sibling_ref[0, q]]


def call(kernel, out_shape, in_specs, flops=0, moved=1 << 20, vmem=32 << 20, **more):
    outs = jax.tree.map(lambda _: VMEM, out_shape)
    more.setdefault("out_specs", outs)
    return pl.pallas_call(
        kernel,
        out_shape=out_shape,
        in_specs=in_specs,
        compiler_params=pltpu.CompilerParams(vmem_limit_bytes=vmem),
        cost_estimate=pl.CostEstimate(flops=flops, bytes_accessed=moved, transcendentals=0),
        **more,
    )


def exchange_plain(plan, place, got, own_part, send_part, sibling, blk_count):
    peers, node_dev, share, state = send_part.shape
    shape = jax.ShapeDtypeStruct
    whole = [pltpu.VMEM((state, state), F32)] if share % LANES else []
    depth = max(plan.depth)
    to_partner = [(i, i ^ 1) for i in range(plan.leaf_count)]
    with jax.named_scope("routed_send"):
        code, plain, scaled = call(
            functools.partial(send_plain, plan),
            (
                shape((peers, node_dev * (share + GROUP), state), jnp.int16),
                shape((node_dev, depth, state), BF16),
                shape((node_dev, depth, state), BF16),
            ),
            [SMEM, VMEM, VMEM],
            scratch_shapes=whole,
            flops=2 * node_dev * depth * state * state,
        )(place, got, send_part)
    arrived = jnp.stack(
        [
            lax.ppermute(code[e - 1], "blk", [(i, i ^ e) for i in range(blk_count)])
            for e in range(1, blk_count)
        ]
    )
    with jax.named_scope("routed_own"):
        own = call(
            own_kernel,
            shape((node_dev, share, state), F32),
            [SMEM, VMEM, VMEM, VMEM],
            scratch_shapes=whole,
            flops=2 * node_dev * depth * share * state,
        )(place, own_part, plain, scaled)
    partner_own = lax.ppermute(own, "leaf", to_partner)
    partner_arrived = lax.ppermute(arrived, "leaf", to_partner)
    with jax.named_scope("node"):
        node_schur, node = call(
            node_kernel,
            (shape((share, node_dev, state), F32), shape((node_dev, share, state), F32)),
            [VMEM, VMEM],
        )(own, arrived)
    with jax.named_scope("merge"):
        merged = call(
            merge_kernel,
            shape((share, node_dev, state), F32),
            [SMEM, VMEM, VMEM, VMEM],
            scratch_shapes=[pltpu.VMEM((node_dev, share, state), F32)],
        )(sibling, node, partner_own, partner_arrived)
    return node_schur, merged


def exchange_folded(plan, place, got, own_part, send_part, sibling):
    _, node_dev, share, state = send_part.shape
    shape = jax.ShapeDtypeStruct
    depth = max(plan.depth)
    to_partner = [(i, i ^ 1) for i in range(plan.leaf_count)]
    result = shape((share, node_dev, state), F32)
    rows = shape((node_dev, share, state), F32)
    any_spec = pl.BlockSpec(memory_space=pl.ANY)
    scratch = [pltpu.VMEM((share, node_dev, state), F32), pltpu.SemaphoreType.DMA((PIECES,))]
    with jax.named_scope("routed_send"):
        code, plain, scaled = call(
            functools.partial(send_folded, plan),
            (
                shape((3 * share + GROUP, share), jnp.int16),
                shape((node_dev, depth, state), BF16),
                shape((node_dev, depth, state), BF16),
            ),
            [SMEM, VMEM, VMEM],
            flops=2 * node_dev * depth * share * state,
        )(place, got, send_part)
    arrived = lax.ppermute(code, "blk", [(0, 1), (1, 0)])
    with jax.named_scope("routed_own"):
        own = call(own_kernel, rows, [SMEM, VMEM, VMEM, VMEM], flops=LONG)(place, own_part, plain, scaled)
    partner_own = lax.ppermute(own, "leaf", to_partner)
    partner_arrived = lax.ppermute(arrived, "leaf", to_partner)
    with jax.named_scope("node"):
        node_schur, node = call(
            node_folded,
            (result, rows),
            [SMEM, VMEM, VMEM],
            out_specs=(any_spec, VMEM),
            scratch_shapes=scratch,
            flops=LONG,
        )(place, own, arrived)
    with jax.named_scope("merge"):
        merged = call(
            merge_folded,
            result,
            [SMEM, SMEM, VMEM, VMEM, VMEM],
            out_specs=any_spec,
            scratch_shapes=scratch,
        )(place, sibling, node, partner_own, partner_arrived)
    return node_schur, merged


def shards(leaf_rows, leaf_weight, branching, sibling, node_block, na_rows, na_weight, na_route):
    leaf_count, blk_count = lax.axis_size("leaf"), lax.axis_size("blk")
    node_dev, most_children, depth, state = leaf_rows.shape
    count = na_rows.shape[0]
    share = state // blk_count
    peers = blk_count - 1
    plan = Plan(leaf_count, node_dev, 3 * count // (2 * leaf_count * node_dev), state)
    place = lax.axis_index("blk").astype(I32).reshape(1)
    shape = jax.ShapeDtypeStruct
    any_spec = pl.BlockSpec(memory_space=pl.ANY)

    with jax.named_scope("bucket"):
        blocks = call(
            functools.partial(bucket_kernel, plan),
            shape((leaf_count, plan.block, LANES), BF16),
            [any_spec, any_spec, any_spec],
            scratch_shapes=[
                pltpu.VMEM((1, count), I32),
                pltpu.VMEM((count,), BF16),
                pltpu.VMEM((count, state + LANES), BF16),
                pltpu.VMEM((leaf_count, plan.block, LANES), BF16),
                pltpu.SemaphoreType.DMA((3 + PIECES,)),
            ],
            out_specs=any_spec,
            vmem=60 << 20,
            flops=2 * plan.leaf_count * plan.rows * count * state,
        )(na_route.reshape(1, count), na_weight, na_rows)
    got = lax.all_to_all(blocks, "leaf", split_axis=0, concat_axis=0, tiled=True)

    with jax.named_scope("leaf_products"):
        own_part, send_part = call(
            leaf_kernel,
            (shape((node_dev, share, state), F32), shape((peers, node_dev, share, state), F32)),
            [
                SMEM,
                SMEM,
                pl.BlockSpec((1, most_children, depth), lambda n: (n, 0, 0)),
                pl.BlockSpec((1, most_children, depth, state), lambda n: (n, 0, 0, 0)),
                pl.BlockSpec((1, share, state), lambda n: (n, 0, 0)),
            ],
            out_specs=(
                pl.BlockSpec((1, share, state), lambda n: (n, 0, 0)),
                pl.BlockSpec((peers, 1, share, state), lambda n: (0, n, 0, 0)),
            ),
            grid=(node_dev,),
            scratch_shapes=[pltpu.VMEM((state, state), F32)],
            flops=2 * node_dev * most_children * depth * state * state,
            moved=8 << 20,
        )(place, branching, leaf_weight, leaf_rows, jnp.transpose(node_block, (1, 0, 2)))

    if blk_count == 2 and node_dev == 2 and share == 2 * LANES:
        return exchange_folded(plan, place, got, own_part, send_part, sibling)
    return exchange_plain(plan, place, got, own_part, send_part, sibling, blk_count)


def solution(mesh):
    return jax.shard_map(
        shards,
        mesh=mesh,
        in_specs=(
            P("leaf", None, "blk", None),
            P("leaf", None, "blk"),
            P("leaf"),
            P("leaf", None),
            P("blk", "leaf", None),
            P(("leaf", "blk"), None),
            P(("leaf", "blk")),
            P(("leaf", "blk"), None),
        ),
        out_specs=(P("blk", "leaf", None), P("blk", "leaf", None)),
        check_vma=False,
    )
```

```python
import functools

import jax
import jax.numpy as jnp
from jax import lax
from jax.experimental import pallas as pl
from jax.experimental.pallas import tpu as pltpu
from jax.sharding import PartitionSpec as P

F32 = jnp.float32
BF16 = jnp.bfloat16
I32 = jnp.int32
LANES = 128
GROUP = 16
EXTRA = 8
PIECES = 4
VMEM = pl.BlockSpec(memory_space=pltpu.VMEM)
SMEM = pl.BlockSpec(memory_space=pltpu.SMEM)
CODE = 32000.0
SPLIT = ("outer", "inner")
INNER = 4
LONG = 20_000_000_000


class Plan:
    def __init__(self, leaf_count, node_dev, capacity, state, unit, inner=0):
        self.inner = inner
        self.leaf_count, self.node_dev, self.capacity, self.state = leaf_count, node_dev, capacity, state
        self.full = capacity // GROUP * GROUP
        self.rest = capacity - self.full
        self.rows = -(-node_dev * capacity // unit) * unit
        self.groups = self.rows // GROUP
        self.slabs = state // LANES
        self.block = self.slabs * self.rows + EXTRA
        self.groups_of = [
            [g for g in range(self.groups) if q in {self.node_at(g * GROUP + i) for i in range(GROUP)}]
            for q in range(node_dev)
        ]
        self.depth = [leaf_count * GROUP * len(g) for g in self.groups_of]

    def block_of(self, node):
        if not self.inner:
            return node
        group = node // (2 * self.inner) * (2 * self.inner)
        leaf = node // 2
        return group + (node - 2 * leaf) * self.inner + (leaf - group // 2)

    def node_at(self, row):
        if row < self.node_dev * self.full:
            return row // self.full
        return min((row - self.node_dev * self.full) // self.rest, self.node_dev - 1) if self.rest else 0


def dot_t(a, b):
    return lax.dot_general(a, b, (((0,), (0,)), ((), ())), preferred_element_type=F32)


def bucket_kernel(plan, route_hbm, weight_hbm, rows_hbm, out_hbm, route_ref, weight_ref, rows_ref, out_ref, sems):
    count = rows_hbm.shape[0]
    state = plan.state
    copies = [
        pltpu.make_async_copy(route_hbm, route_ref, sems.at[0]),
        pltpu.make_async_copy(weight_hbm, weight_ref, sems.at[1]),
        pltpu.make_async_copy(rows_hbm, rows_ref.at[:, pl.ds(0, state)], sems.at[2]),
    ]
    for copy in copies:
        copy.start()
    nodes = plan.leaf_count * plan.node_dev
    before = (
        lax.broadcasted_iota(I32, (count, count), 0) < lax.broadcasted_iota(I32, (count, count), 1)
    ).astype(BF16)
    copies[0].wait()
    route = route_ref[...]
    member = lax.broadcasted_iota(I32, (nodes, count), 0) == route
    seen = jnp.dot(member.astype(BF16), before, preferred_element_type=F32)
    position = jnp.sum(jnp.where(member, seen, 0.0), axis=0, keepdims=True).astype(I32)
    route = plan.block_of(route)
    owner = route // plan.node_dev
    q = route - owner * plan.node_dev
    slot = owner * plan.rows + jnp.where(
        position < plan.full,
        q * plan.full + position,
        plan.node_dev * plan.full + q * plan.rest + position - plan.full,
    )
    copies[1].wait()
    weight = weight_ref[...].reshape(1, count)
    rows_ref[:, state:] = dot_t(weight, jnp.ones((1, LANES), BF16)).astype(BF16)
    lane = lax.broadcasted_iota(I32, (EXTRA, LANES), 1)
    sub = lax.broadcasted_iota(I32, (EXTRA, LANES), 0)
    want = []
    for g in range(plan.rows // EXTRA):
        q_of = jnp.full((EXTRA, LANES), plan.node_at(g * EXTRA), I32)
        for i in range(1, EXTRA):
            step = plan.node_at(g * EXTRA + i) - plan.node_at(g * EXTRA + i - 1)
            if step:
                q_of = q_of + jnp.where(sub >= i, step, 0)
        want.append(lane == g * plan.node_dev + q_of)
    copies[2].wait()
    each = plan.leaf_count // PIECES
    leaving = []
    for p in range(PIECES):
        place = lax.broadcasted_iota(I32, (each * plan.rows, count), 0) + p * each * plan.rows
        hit = jnp.where(place == slot, 1.0, 0.0).astype(BF16)
        filled = jnp.dot(hit, rows_ref[...], preferred_element_type=F32)
        weights = filled[:, state:]
        filled = filled[:, :state].astype(BF16)
        for i in range(each):
            at = i * plan.rows
            d = p * each + i
            for c in range(plan.slabs):
                out_ref[d, c * plan.rows : (c + 1) * plan.rows, :] = filled[
                    at : at + plan.rows, c * LANES : (c + 1) * LANES
                ]
            extra = jnp.zeros((EXTRA, LANES), F32)
            for g in range(plan.rows // EXTRA):
                extra = jnp.where(want[g], weights[at + g * EXTRA : at + (g + 1) * EXTRA, :], extra)
            out_ref[d, plan.slabs * plan.rows :, :] = extra.astype(BF16)
        span = pl.ds(p * each, each)
        leaving.append(pltpu.make_async_copy(out_ref.at[span], out_hbm.at[span], sems.at[3 + p]))
        leaving[-1].start()
    for copy in leaving:
        copy.wait()


def leaf_kernel(place_ref, branching_ref, weight_ref, rows_ref, block_ref, own_ref, send_ref, total):
    n = pl.program_id(0)
    share = own_ref.shape[1]
    peers = send_ref.shape[0]
    blk = place_ref[0]
    columns = jnp.transpose(weight_ref[0].astype(F32))
    total[...] = jnp.zeros_like(total)
    for b in range(rows_ref.shape[1]):

        @pl.when(b < branching_ref[n])
        def _():
            rows = rows_ref[0, b]
            scaled = (rows.astype(F32) * columns[:, b : b + 1]).astype(BF16)
            total[...] += dot_t(scaled, rows)

    own_ref[0] = total[pl.ds(pl.multiple_of(blk * share, share), share), :] + block_ref[0].astype(F32)
    for e in range(1, peers + 1):
        at = pl.multiple_of((blk ^ e) * share, share)
        send_ref[e - 1, 0] = total[pl.ds(at, share), :]


class Product:
    def __init__(self, scaled_ref, plain_ref, total):
        self.scaled_ref, self.plain_ref, self.total = scaled_ref, plain_ref, total
        if total is not None:
            total[...] = dot_t(scaled_ref[...], plain_ref[...])

    def rows(self, at, share):
        if self.total is not None:
            return self.total[pl.ds(at, share), :]
        return dot_t(self.scaled_ref[:, pl.ds(at, share)], self.plain_ref[...])


def gather_rows(plan, got_ref, plain_ref, scaled_ref):
    for d in range(plan.leaf_count):
        extra = got_ref[d, plan.slabs * plan.rows :, :].astype(F32)
        for g in range(plan.groups):
            rows = jnp.concatenate(
                [
                    got_ref[d, c * plan.rows + g * GROUP : c * plan.rows + (g + 1) * GROUP, :]
                    for c in range(plan.slabs)
                ],
                axis=1,
            )
            wide = rows.astype(F32)
            for q in range(plan.node_dev):
                if g not in plan.groups_of[q]:
                    continue
                at = (plan.groups_of[q].index(g) * plan.leaf_count + d) * GROUP
                first = g * GROUP // EXTRA * plan.node_dev + q
                places = range(first, first + GROUP // EXTRA * plan.node_dev, plan.node_dev)
                weight = jnp.concatenate([extra[:, j : j + 1] for j in places], axis=0)
                plain_ref[q, at : at + GROUP, :] = rows
                scaled_ref[q, at : at + GROUP, :] = (wide * weight).astype(BF16)


def scale_of(most):
    power = jnp.ceil(8.0 * jnp.log2(jnp.maximum(most, 1e-30)))
    return power, CODE * jnp.exp2(-0.125 * power)


def to_code(value):
    return jnp.round(value).astype(I32).astype(jnp.int16)


def from_code(code):
    return code.astype(I32).astype(F32)


def diagonal(width):
    return lax.broadcasted_iota(I32, (width, width), 0) == lax.broadcasted_iota(I32, (width, width), 1)


def as_line(column):
    return jnp.sum(jnp.where(diagonal(column.shape[0]), column, 0.0), axis=0, keepdims=True)


def as_column(line):
    return jnp.sum(jnp.where(diagonal(line.shape[1]), line, 0.0), axis=1, keepdims=True)


def send_plain(plan, place_ref, got_ref, part_ref, code_ref, plain_ref, scaled_ref, total=None):
    blk = place_ref[0]
    peers, nodes, share, state = part_ref.shape
    gather_rows(plan, got_ref, plain_ref, scaled_ref)
    for q in range(nodes):
        product = Product(scaled_ref.at[q], plain_ref.at[q], total)
        for e in range(1, peers + 1):
            at = pl.multiple_of((blk ^ e) * share, share)
            value = part_ref[e - 1, q] + product.rows(at, share)
            power, factor = scale_of(jnp.max(jnp.abs(value), axis=1, keepdims=True))
            code_ref[e - 1, q * share : (q + 1) * share, :] = to_code(value * factor)
            line = jnp.concatenate([as_line(power), jnp.zeros((1, state - share), F32)], axis=1)
            base = nodes * share + q * GROUP
            code_ref[e - 1, base : base + GROUP, :] = to_code(jnp.broadcast_to(line, (GROUP, state)))


def decode_plain(code_ref, nodes, share):
    values = []
    for q in range(nodes):
        base = nodes * share + q * GROUP
        value = None
        for e in range(code_ref.shape[0]):
            power = as_column(from_code(code_ref[e, base : base + GROUP, :])[0:1, :share])
            term = from_code(code_ref[e, q * share : (q + 1) * share, :]) * (
                jnp.exp2(0.125 * power) * (1.0 / CODE)
            )
            value = term if value is None else value + term
        values.append(value)
    return values


def encode_node(code_ref, square, beside):
    half = code_ref.shape[1]
    upper, lower = square[:half, :half], square[half:, half:]
    pieces = [square[:half, half:]]
    pieces += [beside[r : r + half, c : c + half] for r in (0, half) for c in (0, half)]
    most = jnp.maximum(jnp.abs(upper), jnp.abs(lower))
    for piece in pieces:
        most = jnp.maximum(most, jnp.abs(piece))
    power, factor = scale_of(jnp.max(most, axis=1, keepdims=True))
    row = lax.broadcasted_iota(I32, (half, half), 0)
    column = lax.broadcasted_iota(I32, (half, half), 1)
    lower = lower * factor
    code_ref[:half, :] = to_code(jnp.where(column >= row, upper * factor, lower))
    for k, piece in enumerate(pieces):
        code_ref[(k + 1) * half : (k + 2) * half, :] = to_code(piece * factor)
    corner = jnp.sum(jnp.where(column == row, jnp.round(lower), 0.0), axis=0, keepdims=True)
    line = lax.broadcasted_iota(I32, (GROUP, half), 0)
    code_ref[6 * half :, :] = to_code(
        jnp.where(line == 0, as_line(power), jnp.where(line == 1, corner, 0.0))
    )


def decode_node(code_ref):
    half = code_ref.shape[1]
    lines = from_code(code_ref[6 * half :, :])
    step = jnp.transpose(jnp.exp2(0.125 * jnp.broadcast_to(lines[0:1, :], (8, half))) * (1.0 / CODE))[:, 0:1]
    pieces = [from_code(code_ref[k * half : (k + 1) * half, :]) * step for k in range(6)]
    both = pieces[0]
    turned = jnp.transpose(both)
    row = lax.broadcasted_iota(I32, (half, half), 0)
    column = lax.broadcasted_iota(I32, (half, half), 1)
    upper = jnp.where(column >= row, both, turned)
    lower = jnp.where(column < row, both, jnp.where(column == row, lines[1:2, :] * step, turned))
    square = ((upper, pieces[1]), (jnp.transpose(pieces[1]), lower))
    beside = ((pieces[2], pieces[3]), (pieces[4], pieces[5]))
    return square, beside


def halves(place, share):
    mine = pl.ds(pl.multiple_of(place * share, share), share)
    theirs = pl.ds(pl.multiple_of((1 - place) * share, share), share)
    return mine, theirs


def turned(rows, first, count):
    width = rows.shape[1]
    pick = lax.broadcasted_iota(I32, (count, width), 1) == lax.broadcasted_iota(I32, (count, width), 0) + first
    return lax.dot_general(
        jnp.where(pick, 1.0, 0.0).astype(BF16), rows, (((1,), (1,)), ((), ())), preferred_element_type=F32
    )


def leaf_sum(node, branching_ref, weight_hbm, rows_hbm, weight_ref, rows_ref, total, sems):
    pairs = rows_hbm.shape[1] // 2
    depth, state = rows_hbm.shape[2:]
    count = branching_ref[node]
    weights = pltpu.make_async_copy(weight_hbm.at[node], weight_ref, sems.at[pairs])
    copies = [
        pltpu.make_async_copy(rows_hbm.at[node, pl.ds(2 * p, 2)], rows_ref.at[p], sems.at[p])
        for p in range(pairs)
    ]
    copies[0].start()
    weights.start()
    for p in range(1, pairs):
        pl.when(2 * p < count)(copies[p].start)
    weights.wait()
    live = lax.broadcasted_iota(I32, weight_ref.shape, 0) < count
    factor = jnp.where(live, weight_ref[...].astype(F32), 0.0)

    def term(p):
        copies[p].wait()
        rows = rows_ref[p].reshape(2 * depth, state)
        weight = jnp.concatenate([factor[2 * p : 2 * p + 1, :], factor[2 * p + 1 : 2 * p + 2, :]], axis=1)
        scaled = (turned(rows, 0, state) * weight).astype(BF16)
        return jnp.dot(scaled, rows, preferred_element_type=F32)

    total[...] = term(0)
    for p in range(1, pairs):

        @pl.when(2 * p < count)
        def _():
            total[...] += term(p)


def far_leaf_kernel(
    branching_ref, weight_hbm, rows_hbm, own_ref, code_ref, weight_ref, rows_ref, total, sems
):
    share = own_ref.shape[0]
    mine, theirs = halves(lax.axis_index("blk"), share)
    node = 1 - lax.axis_index("blk")
    leaf_sum(node, branching_ref, weight_hbm, rows_hbm, weight_ref, rows_ref, total, sems)
    encode_node(code_ref, total[theirs, theirs], total[theirs, mine])
    own_ref[...] = total[mine, :]


def near_leaf_kernel(
    branching_ref, weight_hbm, rows_hbm, block_ref, far_ref,
    own_ref, send_ref, far_out, weight_ref, rows_ref, total, sems,
):
    share = own_ref.shape[0]
    mine, theirs = halves(lax.axis_index("blk"), share)
    node = lax.axis_index("blk")
    leaf_sum(node, branching_ref, weight_hbm, rows_hbm, weight_ref, rows_ref, total, sems)
    send_ref[...] = total[theirs, :]
    own_ref[...] = total[mine, :] + block_ref[node].astype(F32)
    far_out[...] = far_ref[...] + block_ref[1 - node].astype(F32)


def send_folded(plan, got_ref, part_ref, code_ref, plain_ref, scaled_ref):
    share = part_ref.shape[0]
    mine, theirs = halves(lax.axis_index("blk"), share)
    cap = plan.rows
    for d in range(0, plan.leaf_count, 2):
        blocks = [got_ref[d + i].astype(F32) for i in range(2)]
        weight = jnp.concatenate(
            [
                block[plan.slabs * cap :, g : g + 1]
                for block in blocks
                for g in range(cap // EXTRA)
            ],
            axis=0,
        )
        at = d * cap
        for c in range(plan.slabs):
            rows = jnp.concatenate([block[c * cap : (c + 1) * cap, :] for block in blocks], axis=0)
            plain_ref[at : at + 2 * cap, c * LANES : (c + 1) * LANES] = rows.astype(BF16)
            scaled_ref[at : at + 2 * cap, c * LANES : (c + 1) * LANES] = (rows * weight).astype(BF16)
    scaled = turned(scaled_ref[...], (1 - lax.axis_index("blk")) * share, share).astype(BF16)
    encode_node(
        code_ref,
        part_ref[:, theirs] + jnp.dot(scaled, plain_ref[:, theirs], preferred_element_type=F32),
        part_ref[:, mine] + jnp.dot(scaled, plain_ref[:, mine], preferred_element_type=F32),
    )


def in_columns(place, square, beside):
    first = place == 0
    return [
        [jnp.where(first, s, b) for s, b in zip(*pair)] + [jnp.where(first, b, s) for s, b in zip(*pair)]
        for pair in zip(square, beside)
    ]


def tiles_of(ref):
    half = ref.shape[0] // 2
    for i in range(2):
        for k in range(ref.shape[1] // half):
            yield i, k, slice(i * half, (i + 1) * half), slice(k * half, (k + 1) * half)


def near_node_kernel(own_ref, plain_ref, scaled_ref, code_ref, node_ref):
    share = own_ref.shape[0]
    scaled = turned(scaled_ref[...], lax.axis_index("blk") * share, share).astype(BF16)
    node_ref[...] = own_ref[...] + jnp.dot(scaled, plain_ref[...], preferred_element_type=F32)
    terms = in_columns(lax.axis_index("blk"), *decode_node(code_ref))
    for i, k, rows, columns in tiles_of(node_ref):
        node_ref[rows, columns] += terms[i][k]


def far_node_kernel(near_ref, own_ref, code_ref, node_ref, out_ref):
    first = lax.axis_index("blk") == 0
    terms = in_columns(lax.axis_index("blk"), *decode_node(code_ref))
    for i, k, rows, columns in tiles_of(node_ref):
        far = own_ref[rows, columns] + terms[i][k]
        near = near_ref[rows, columns]
        node_ref[rows, columns] = far
        out_ref[rows, 0, columns] = jnp.where(first, near, far)
        out_ref[rows, 1, columns] = jnp.where(first, far, near)


def merge_folded(
    sibling_ref, near_ref, far_ref, node_ref, their_near_ref, their_own_ref, code_ref,
    node_hbm, out_hbm, out_ref, sems,
):
    share = far_ref.shape[0]
    half = share // 2
    each = share // PIECES
    copies = [pltpu.make_async_copy(node_ref, node_hbm, sems.at[PIECES])]
    copies[0].start()
    first = lax.axis_index("blk") == 0
    straight = jnp.broadcast_to(sibling_ref[0:1, 0:1], (each, LANES)) == 0
    terms = in_columns(lax.axis_index("blk"), *decode_node(code_ref))
    for p in range(PIECES):
        rows = slice(p * each, (p + 1) * each)
        inner = slice(p * each % half, p * each % half + each)
        for k in range(far_ref.shape[1] // half):
            columns = slice(k * half, (k + 1) * half)
            their_near = their_near_ref[rows, columns]
            their_far = their_own_ref[rows, columns] + terms[p * each // half][k][inner]
            near = near_ref[rows, columns] + jnp.where(straight, their_near, their_far)
            far = far_ref[rows, columns] + jnp.where(straight, their_far, their_near)
            out_ref[rows, 0, columns] = jnp.where(first, near, far)
            out_ref[rows, 1, columns] = jnp.where(first, far, near)
        span = pl.ds(p * each, each)
        copies.append(pltpu.make_async_copy(out_ref.at[span], out_hbm.at[span], sems.at[p]))
        copies[-1].start()
    for copy in copies:
        copy.wait()


def own_kernel(place_ref, part_ref, plain_ref, scaled_ref, own_ref, total=None):
    nodes, share, _ = part_ref.shape
    at = pl.multiple_of(place_ref[0] * share, share)
    for q in range(nodes):
        own_ref[q] = part_ref[q] + Product(scaled_ref.at[q], plain_ref.at[q], total).rows(at, share)


def node_kernel(own_ref, code_ref, out_ref, node_ref):
    nodes, share, _ = own_ref.shape
    arrived = decode_plain(code_ref, nodes, share)
    for q in range(nodes):
        value = own_ref[q] + arrived[q]
        node_ref[q] = value
        out_ref[:, q, :] = value


def merge_kernel(sibling_ref, node_ref, own_ref, code_ref, out_ref, partner_ref):
    nodes, share, _ = own_ref.shape
    arrived = decode_plain(code_ref, nodes, share)
    for q in range(nodes):
        partner_ref[q] = own_ref[q] + arrived[q]
    for q in range(nodes):
        out_ref[:, q, :] = node_ref[q] + partner_ref[sibling_ref[0, q]]


def call(kernel, out_shape, in_specs, flops=0, moved=1 << 20, vmem=32 << 20, **more):
    outs = jax.tree.map(lambda _: VMEM, out_shape)
    more.setdefault("out_specs", outs)
    return pl.pallas_call(
        kernel,
        out_shape=out_shape,
        in_specs=in_specs,
        compiler_params=pltpu.CompilerParams(vmem_limit_bytes=vmem),
        cost_estimate=pl.CostEstimate(flops=flops, bytes_accessed=moved, transcendentals=0),
        **more,
    )


def exchange_plain(plan, place, got, own_part, send_part, sibling, blk_count):
    peers, node_dev, share, state = send_part.shape
    shape = jax.ShapeDtypeStruct
    whole = [pltpu.VMEM((state, state), F32)] if share % LANES else []
    depth = max(plan.depth)
    to_partner = [(i, i ^ 1) for i in range(plan.leaf_count)]
    with jax.named_scope("routed_send"):
        code, plain, scaled = call(
            functools.partial(send_plain, plan),
            (
                shape((peers, node_dev * (share + GROUP), state), jnp.int16),
                shape((node_dev, depth, state), BF16),
                shape((node_dev, depth, state), BF16),
            ),
            [SMEM, VMEM, VMEM],
            scratch_shapes=whole,
            flops=2 * node_dev * depth * state * state,
        )(place, got, send_part)
    arrived = jnp.stack(
        [
            lax.ppermute(code[e - 1], "blk", [(i, i ^ e) for i in range(blk_count)])
            for e in range(1, blk_count)
        ]
    )
    with jax.named_scope("routed_own"):
        own = call(
            own_kernel,
            shape((node_dev, share, state), F32),
            [SMEM, VMEM, VMEM, VMEM],
            scratch_shapes=whole,
            flops=2 * node_dev * depth * share * state,
        )(place, own_part, plain, scaled)
    partner_own = lax.ppermute(own, "leaf", to_partner)
    partner_arrived = lax.ppermute(arrived, "leaf", to_partner)
    with jax.named_scope("node"):
        node_schur, node = call(
            node_kernel,
            (shape((share, node_dev, state), F32), shape((node_dev, share, state), F32)),
            [VMEM, VMEM],
        )(own, arrived)
    with jax.named_scope("merge"):
        merged = call(
            merge_kernel,
            shape((share, node_dev, state), F32),
            [SMEM, VMEM, VMEM, VMEM],
            scratch_shapes=[pltpu.VMEM((node_dev, share, state), F32)],
        )(sibling, node, partner_own, partner_arrived)
    return node_schur, merged


def bucket(plan, na_route, na_weight, na_rows):
    count, state = na_rows.shape
    any_spec = pl.BlockSpec(memory_space=pl.ANY)
    with jax.named_scope("bucket"):
        return call(
            functools.partial(bucket_kernel, plan),
            jax.ShapeDtypeStruct((plan.leaf_count, plan.block, LANES), BF16),
            [any_spec, any_spec, any_spec],
            scratch_shapes=[
                pltpu.VMEM((1, count), I32),
                pltpu.VMEM((count,), BF16),
                pltpu.VMEM((count, state + LANES), BF16),
                pltpu.VMEM((plan.leaf_count, plan.block, LANES), BF16),
                pltpu.SemaphoreType.DMA((3 + PIECES,)),
            ],
            out_specs=any_spec,
            vmem=60 << 20,
            flops=2 * plan.leaf_count * plan.rows * count * state,
        )(na_route.reshape(1, count), na_weight, na_rows)


def shards_plain(leaf_rows, leaf_weight, branching, sibling, node_block, na_rows, na_weight, na_route):
    leaf_count, blk_count = lax.axis_size("leaf"), lax.axis_size("blk")
    node_dev, most_children, depth, state = leaf_rows.shape
    count = na_rows.shape[0]
    share = state // blk_count
    peers = blk_count - 1
    plan = Plan(leaf_count, node_dev, 3 * count // (2 * leaf_count * node_dev), state, GROUP)
    place = lax.axis_index("blk").astype(I32).reshape(1)
    shape = jax.ShapeDtypeStruct
    blocks = bucket(plan, na_route, na_weight, na_rows)
    got = lax.all_to_all(blocks, "leaf", split_axis=0, concat_axis=0, tiled=True)
    with jax.named_scope("leaf_products"):
        own_part, send_part = call(
            leaf_kernel,
            (shape((node_dev, share, state), F32), shape((peers, node_dev, share, state), F32)),
            [
                SMEM,
                SMEM,
                pl.BlockSpec((1, most_children, depth), lambda n: (n, 0, 0)),
                pl.BlockSpec((1, most_children, depth, state), lambda n: (n, 0, 0, 0)),
                pl.BlockSpec((1, share, state), lambda n: (n, 0, 0)),
            ],
            out_specs=(
                pl.BlockSpec((1, share, state), lambda n: (n, 0, 0)),
                pl.BlockSpec((peers, 1, share, state), lambda n: (0, n, 0, 0)),
            ),
            grid=(node_dev,),
            scratch_shapes=[pltpu.VMEM((state, state), F32)],
            flops=2 * node_dev * most_children * depth * state * state,
            moved=8 << 20,
        )(place, branching, leaf_weight, leaf_rows, jnp.transpose(node_block, (1, 0, 2)))
    return exchange_plain(plan, place, got, own_part, send_part, sibling, blk_count)


def shards_folded(leaf_rows, leaf_weight, branching, sibling, node_block, na_rows, na_weight, na_route):
    leaf_count = lax.axis_size(SPLIT)
    node_dev, most_children, depth, state = leaf_rows.shape
    count = na_rows.shape[0]
    share = state // 2
    half = share // 2
    nodes = leaf_count * node_dev
    plan = Plan(nodes, 1, 3 * count // (2 * nodes), state, EXTRA, INNER)
    shape = jax.ShapeDtypeStruct
    any_spec = pl.BlockSpec(memory_space=pl.ANY)
    across = [(0, 1), (1, 0)]
    to_partner = [(i, i ^ 1) for i in range(leaf_count)]
    result = shape((share, node_dev, state), F32)
    rows = shape((share, state), F32)
    codes = shape((6 * half + GROUP, half), jnp.int16)
    gathered = shape((nodes * plan.rows, state), BF16)

    blocks = bucket(plan, na_route, na_weight, na_rows)
    got = lax.all_to_all(blocks, (SPLIT[0], "blk", SPLIT[1]), split_axis=0, concat_axis=0, tiled=True)

    own_block = jnp.transpose(node_block, (1, 0, 2))
    leaf = dict(
        scratch_shapes=[
            pltpu.VMEM((most_children, depth), BF16),
            pltpu.VMEM((most_children // 2, 2, depth, state), BF16),
            pltpu.VMEM((state, state), F32),
            pltpu.SemaphoreType.DMA((most_children // 2 + 1,)),
        ],
        flops=1,
        moved=1,
        vmem=24 << 20,
    )
    with jax.named_scope("far_leaf_products"):
        far_own, far_code = call(
            far_leaf_kernel, (rows, codes), [SMEM, any_spec, any_spec], **leaf
        )(branching, leaf_weight, leaf_rows)
    near_code = lax.ppermute(far_code, "blk", across)
    with jax.named_scope("near_leaf_products"):
        near_own, send_part, far_own = call(
            near_leaf_kernel, (rows, rows, rows), [SMEM, any_spec, any_spec, VMEM, VMEM], **leaf
        )(branching, leaf_weight, leaf_rows, own_block, far_own)
    their_own = lax.ppermute(far_own, SPLIT, to_partner)
    with jax.named_scope("routed_send"):
        code, plain, scaled = call(
            functools.partial(send_folded, plan),
            (codes, gathered, gathered),
            [VMEM, VMEM],
            flops=2 * nodes * plan.rows * share * state,
        )(got, send_part)
    arrived = lax.ppermute(code, "blk", across)
    with jax.named_scope("near_node"):
        near = call(near_node_kernel, rows, [VMEM, VMEM, VMEM, VMEM], flops=LONG)(
            near_own, plain, scaled, near_code
        )
    their_near = lax.ppermute(near, SPLIT, to_partner)
    their_arrived = lax.ppermute(arrived, SPLIT, to_partner)
    with jax.named_scope("far_node"):
        far, node = call(far_node_kernel, (rows, result), [VMEM, VMEM, VMEM], flops=LONG)(
            near, far_own, arrived
        )
    with jax.named_scope("merge"):
        return call(
            merge_folded,
            (result, result),
            [VMEM] * 7,
            out_specs=(any_spec, any_spec),
            scratch_shapes=[
                pltpu.VMEM((share, node_dev, state), F32),
                pltpu.SemaphoreType.DMA((PIECES + 1,)),
            ],
        )(sibling, near, far, node, their_near, their_own, their_arrived)


def solution(mesh):
    leaf_count, blk_count = mesh.shape["leaf"], mesh.shape["blk"]
    plain = jax.shard_map(
        shards_plain, mesh=mesh, in_specs=in_specs("leaf"), out_specs=out_specs("leaf"), check_vma=False
    )
    if blk_count != 2 or leaf_count % INNER:
        return plain
    split = jax.sharding.Mesh(
        mesh.devices.reshape(leaf_count // INNER, INNER, blk_count), (*SPLIT, "blk")
    )
    folded = jax.shard_map(
        shards_folded, mesh=split, in_specs=in_specs(SPLIT), out_specs=out_specs(SPLIT), check_vma=False
    )

    def choose(leaf_rows, *more):
        nodes, children, _, state = leaf_rows.shape
        fits = nodes == 2 * leaf_count and children % 2 == 0 and state == 4 * LANES
        return (folded if fits else plain)(leaf_rows, *more)

    return choose


def in_specs(leaf):
    every = ((leaf,) if isinstance(leaf, str) else leaf) + ("blk",)
    return (
        P(leaf, None, "blk", None),
        P(leaf, None, "blk"),
        P(leaf),
        P(leaf, None),
        P("blk", leaf, None),
        P(every, None),
        P(every),
        P(every, None),
    )


def out_specs(leaf):
    return (P("blk", leaf, None), P("blk", leaf, None))
```

```python
import functools

import jax
import jax.numpy as jnp
from jax import lax
from jax.experimental import pallas as pl
from jax.experimental.pallas import tpu as pltpu
from jax.sharding import PartitionSpec as P

F32 = jnp.float32
BF16 = jnp.bfloat16
I32 = jnp.int32
LANES = 128
GROUP = 16
EXTRA = 8
PIECES = 4
VMEM = pl.BlockSpec(memory_space=pltpu.VMEM)
SMEM = pl.BlockSpec(memory_space=pltpu.SMEM)
CODE = 32000.0
SPLIT = ("z1", "z0", "y", "core")
ORDER = ("blk", "y", "z1", "core", "z0")
LONG = 20_000_000_000


class Plan:
    def __init__(self, leaf_count, node_dev, capacity, state, unit, order=()):
        self.order = order
        self.leaf_count, self.node_dev, self.capacity, self.state = leaf_count, node_dev, capacity, state
        self.full = capacity // GROUP * GROUP
        self.rest = capacity - self.full
        self.rows = -(-node_dev * capacity // unit) * unit
        self.groups = self.rows // GROUP
        self.slabs = state // LANES
        self.block = self.slabs * self.rows + EXTRA
        self.groups_of = [
            [g for g in range(self.groups) if q in {self.node_at(g * GROUP + i) for i in range(GROUP)}]
            for q in range(node_dev)
        ]
        self.depth = [leaf_count * GROUP * len(g) for g in self.groups_of]

    def block_of(self, node):
        if not self.order:
            return node
        block = jnp.zeros_like(node)
        for name in self.order:
            block = 2 * block + (node >> (len(SPLIT) - (*SPLIT, "blk").index(name)) & 1)
        return block

    def node_at(self, row):
        if row < self.node_dev * self.full:
            return row // self.full
        return min((row - self.node_dev * self.full) // self.rest, self.node_dev - 1) if self.rest else 0


def dot_t(a, b):
    return lax.dot_general(a, b, (((0,), (0,)), ((), ())), preferred_element_type=F32)


def bucket_kernel(plan, route_hbm, weight_hbm, rows_hbm, out_hbm, route_ref, weight_ref, rows_ref, out_ref, sems):
    count = rows_hbm.shape[0]
    state = plan.state
    copies = [
        pltpu.make_async_copy(route_hbm, route_ref, sems.at[0]),
        pltpu.make_async_copy(weight_hbm, weight_ref, sems.at[1]),
        pltpu.make_async_copy(rows_hbm, rows_ref.at[:, pl.ds(0, state)], sems.at[2]),
    ]
    for copy in copies:
        copy.start()
    nodes = plan.leaf_count * plan.node_dev
    before = (
        lax.broadcasted_iota(I32, (count, count), 0) < lax.broadcasted_iota(I32, (count, count), 1)
    ).astype(BF16)
    copies[0].wait()
    route = route_ref[...]
    member = lax.broadcasted_iota(I32, (nodes, count), 0) == route
    seen = jnp.dot(member.astype(BF16), before, preferred_element_type=F32)
    position = jnp.sum(jnp.where(member, seen, 0.0), axis=0, keepdims=True).astype(I32)
    route = plan.block_of(route)
    owner = route // plan.node_dev
    q = route - owner * plan.node_dev
    slot = owner * plan.rows + jnp.where(
        position < plan.full,
        q * plan.full + position,
        plan.node_dev * plan.full + q * plan.rest + position - plan.full,
    )
    copies[1].wait()
    weight = weight_ref[...].reshape(1, count)
    rows_ref[:, state:] = dot_t(weight, jnp.ones((1, LANES), BF16)).astype(BF16)
    lane = lax.broadcasted_iota(I32, (EXTRA, LANES), 1)
    sub = lax.broadcasted_iota(I32, (EXTRA, LANES), 0)
    want = []
    for g in range(plan.rows // EXTRA):
        q_of = jnp.full((EXTRA, LANES), plan.node_at(g * EXTRA), I32)
        for i in range(1, EXTRA):
            step = plan.node_at(g * EXTRA + i) - plan.node_at(g * EXTRA + i - 1)
            if step:
                q_of = q_of + jnp.where(sub >= i, step, 0)
        want.append(lane == g * plan.node_dev + q_of)
    copies[2].wait()
    each = plan.leaf_count // PIECES
    leaving = []
    for p in range(PIECES):
        place = lax.broadcasted_iota(I32, (each * plan.rows, count), 0) + p * each * plan.rows
        hit = jnp.where(place == slot, 1.0, 0.0).astype(BF16)
        filled = jnp.dot(hit, rows_ref[...], preferred_element_type=F32)
        weights = filled[:, state:]
        filled = filled[:, :state].astype(BF16)
        for i in range(each):
            at = i * plan.rows
            d = p * each + i
            for c in range(plan.slabs):
                out_ref[d, c * plan.rows : (c + 1) * plan.rows, :] = filled[
                    at : at + plan.rows, c * LANES : (c + 1) * LANES
                ]
            extra = jnp.zeros((EXTRA, LANES), F32)
            for g in range(plan.rows // EXTRA):
                extra = jnp.where(want[g], weights[at + g * EXTRA : at + (g + 1) * EXTRA, :], extra)
            out_ref[d, plan.slabs * plan.rows :, :] = extra.astype(BF16)
        span = pl.ds(p * each, each)
        leaving.append(pltpu.make_async_copy(out_ref.at[span], out_hbm.at[span], sems.at[3 + p]))
        leaving[-1].start()
    for copy in leaving:
        copy.wait()


def leaf_kernel(place_ref, branching_ref, weight_ref, rows_ref, block_ref, own_ref, send_ref, total):
    n = pl.program_id(0)
    share = own_ref.shape[1]
    peers = send_ref.shape[0]
    blk = place_ref[0]
    columns = jnp.transpose(weight_ref[0].astype(F32))
    total[...] = jnp.zeros_like(total)
    for b in range(rows_ref.shape[1]):

        @pl.when(b < branching_ref[n])
        def _():
            rows = rows_ref[0, b]
            scaled = (rows.astype(F32) * columns[:, b : b + 1]).astype(BF16)
            total[...] += dot_t(scaled, rows)

    own_ref[0] = total[pl.ds(pl.multiple_of(blk * share, share), share), :] + block_ref[0].astype(F32)
    for e in range(1, peers + 1):
        at = pl.multiple_of((blk ^ e) * share, share)
        send_ref[e - 1, 0] = total[pl.ds(at, share), :]


class Product:
    def __init__(self, scaled_ref, plain_ref, total):
        self.scaled_ref, self.plain_ref, self.total = scaled_ref, plain_ref, total
        if total is not None:
            total[...] = dot_t(scaled_ref[...], plain_ref[...])

    def rows(self, at, share):
        if self.total is not None:
            return self.total[pl.ds(at, share), :]
        return dot_t(self.scaled_ref[:, pl.ds(at, share)], self.plain_ref[...])


def gather_rows(plan, got_ref, plain_ref, scaled_ref):
    for d in range(plan.leaf_count):
        extra = got_ref[d, plan.slabs * plan.rows :, :].astype(F32)
        for g in range(plan.groups):
            rows = jnp.concatenate(
                [
                    got_ref[d, c * plan.rows + g * GROUP : c * plan.rows + (g + 1) * GROUP, :]
                    for c in range(plan.slabs)
                ],
                axis=1,
            )
            wide = rows.astype(F32)
            for q in range(plan.node_dev):
                if g not in plan.groups_of[q]:
                    continue
                at = (plan.groups_of[q].index(g) * plan.leaf_count + d) * GROUP
                first = g * GROUP // EXTRA * plan.node_dev + q
                places = range(first, first + GROUP // EXTRA * plan.node_dev, plan.node_dev)
                weight = jnp.concatenate([extra[:, j : j + 1] for j in places], axis=0)
                plain_ref[q, at : at + GROUP, :] = rows
                scaled_ref[q, at : at + GROUP, :] = (wide * weight).astype(BF16)


def scale_of(most):
    power = jnp.ceil(8.0 * jnp.log2(jnp.maximum(most, 1e-30)))
    return power, CODE * jnp.exp2(-0.125 * power)


def to_code(value):
    return jnp.round(value).astype(I32).astype(jnp.int16)


def from_code(code):
    return code.astype(I32).astype(F32)


def diagonal(width):
    return lax.broadcasted_iota(I32, (width, width), 0) == lax.broadcasted_iota(I32, (width, width), 1)


def as_line(column):
    return jnp.sum(jnp.where(diagonal(column.shape[0]), column, 0.0), axis=0, keepdims=True)


def as_column(line):
    return jnp.sum(jnp.where(diagonal(line.shape[1]), line, 0.0), axis=1, keepdims=True)


def send_plain(plan, place_ref, got_ref, part_ref, code_ref, plain_ref, scaled_ref, total=None):
    blk = place_ref[0]
    peers, nodes, share, state = part_ref.shape
    gather_rows(plan, got_ref, plain_ref, scaled_ref)
    for q in range(nodes):
        product = Product(scaled_ref.at[q], plain_ref.at[q], total)
        for e in range(1, peers + 1):
            at = pl.multiple_of((blk ^ e) * share, share)
            value = part_ref[e - 1, q] + product.rows(at, share)
            power, factor = scale_of(jnp.max(jnp.abs(value), axis=1, keepdims=True))
            code_ref[e - 1, q * share : (q + 1) * share, :] = to_code(value * factor)
            line = jnp.concatenate([as_line(power), jnp.zeros((1, state - share), F32)], axis=1)
            base = nodes * share + q * GROUP
            code_ref[e - 1, base : base + GROUP, :] = to_code(jnp.broadcast_to(line, (GROUP, state)))


def decode_plain(code_ref, nodes, share):
    values = []
    for q in range(nodes):
        base = nodes * share + q * GROUP
        value = None
        for e in range(code_ref.shape[0]):
            power = as_column(from_code(code_ref[e, base : base + GROUP, :])[0:1, :share])
            term = from_code(code_ref[e, q * share : (q + 1) * share, :]) * (
                jnp.exp2(0.125 * power) * (1.0 / CODE)
            )
            value = term if value is None else value + term
        values.append(value)
    return values


def encode_node(code_ref, square, beside):
    half = code_ref.shape[1]
    upper, lower = square[:half, :half], square[half:, half:]
    pieces = [square[:half, half:]]
    pieces += [beside[r : r + half, c : c + half] for r in (0, half) for c in (0, half)]
    most = jnp.maximum(jnp.abs(upper), jnp.abs(lower))
    for piece in pieces:
        most = jnp.maximum(most, jnp.abs(piece))
    power, factor = scale_of(jnp.max(most, axis=1, keepdims=True))
    row = lax.broadcasted_iota(I32, (half, half), 0)
    column = lax.broadcasted_iota(I32, (half, half), 1)
    lower = lower * factor
    code_ref[:half, :] = to_code(jnp.where(column >= row, upper * factor, lower))
    for k, piece in enumerate(pieces):
        code_ref[(k + 1) * half : (k + 2) * half, :] = to_code(piece * factor)
    corner = jnp.sum(jnp.where(column == row, jnp.round(lower), 0.0), axis=0, keepdims=True)
    line = lax.broadcasted_iota(I32, (GROUP, half), 0)
    code_ref[6 * half :, :] = to_code(
        jnp.where(line == 0, as_line(power), jnp.where(line == 1, corner, 0.0))
    )


def decode_node(code_ref):
    half = code_ref.shape[1]
    lines = from_code(code_ref[6 * half :, :])
    step = jnp.transpose(jnp.exp2(0.125 * jnp.broadcast_to(lines[0:1, :], (8, half))) * (1.0 / CODE))[:, 0:1]
    pieces = [from_code(code_ref[k * half : (k + 1) * half, :]) * step for k in range(6)]
    both = pieces[0]
    turned = jnp.transpose(both)
    row = lax.broadcasted_iota(I32, (half, half), 0)
    column = lax.broadcasted_iota(I32, (half, half), 1)
    upper = jnp.where(column >= row, both, turned)
    lower = jnp.where(column < row, both, jnp.where(column == row, lines[1:2, :] * step, turned))
    square = ((upper, pieces[1]), (jnp.transpose(pieces[1]), lower))
    beside = ((pieces[2], pieces[3]), (pieces[4], pieces[5]))
    return square, beside


def halves(place, share):
    mine = pl.ds(pl.multiple_of(place * share, share), share)
    theirs = pl.ds(pl.multiple_of((1 - place) * share, share), share)
    return mine, theirs


def leaf_sum(node, branching_ref, weight_hbm, rows_hbm, weight_ref, rows_ref, total, sems):
    pairs = rows_hbm.shape[1] // 2
    depth, state = rows_hbm.shape[2:]
    count = branching_ref[node]
    weights = pltpu.make_async_copy(weight_hbm.at[node], weight_ref, sems.at[pairs])
    copies = [
        pltpu.make_async_copy(rows_hbm.at[node, pl.ds(2 * p, 2)], rows_ref.at[p], sems.at[p])
        for p in range(pairs)
    ]
    copies[0].start()
    weights.start()
    for p in range(1, pairs):
        pl.when(2 * p < count)(copies[p].start)
    weights.wait()
    live = lax.broadcasted_iota(I32, weight_ref.shape, 0) < count
    columns = jnp.transpose(jnp.where(live, weight_ref[...].astype(F32), 0.0))

    def term(p):
        copies[p].wait()
        rows = rows_ref[p].reshape(2 * depth, state)
        weight = jnp.concatenate([columns[:, 2 * p : 2 * p + 1], columns[:, 2 * p + 1 : 2 * p + 2]], axis=0)
        return dot_t((rows.astype(F32) * weight).astype(BF16), rows)

    total[...] = term(0)
    for p in range(1, pairs):

        @pl.when(2 * p < count)
        def _():
            total[...] += term(p)


def far_leaf_kernel(
    branching_ref, weight_hbm, rows_hbm, own_ref, code_ref, weight_ref, rows_ref, total, sems
):
    share = own_ref.shape[0]
    mine, theirs = halves(lax.axis_index("blk"), share)
    node = 1 - lax.axis_index("blk")
    leaf_sum(node, branching_ref, weight_hbm, rows_hbm, weight_ref, rows_ref, total, sems)
    encode_node(code_ref, total[theirs, theirs], total[theirs, mine])
    own_ref[...] = total[mine, :]


def near_leaf_kernel(
    branching_ref, weight_hbm, rows_hbm, block_ref, far_ref,
    own_ref, send_ref, far_out, weight_ref, rows_ref, total, sems,
):
    share = own_ref.shape[0]
    mine, theirs = halves(lax.axis_index("blk"), share)
    node = lax.axis_index("blk")
    leaf_sum(node, branching_ref, weight_hbm, rows_hbm, weight_ref, rows_ref, total, sems)
    send_ref[...] = total[theirs, :]
    own_ref[...] = total[mine, :] + block_ref[node].astype(F32)
    far_out[...] = far_ref[...] + block_ref[1 - node].astype(F32)


def send_folded(plan, got_ref, part_ref, code_ref, plain_ref, scaled_ref):
    share = part_ref.shape[0]
    mine, theirs = halves(lax.axis_index("blk"), share)
    cap = plan.rows
    for d in range(0, plan.leaf_count, 2):
        blocks = [got_ref[d + i].astype(F32) for i in range(2)]
        weight = jnp.concatenate(
            [
                block[plan.slabs * cap :, g : g + 1]
                for block in blocks
                for g in range(cap // EXTRA)
            ],
            axis=0,
        )
        at = d * cap
        for c in range(plan.slabs):
            rows = jnp.concatenate([block[c * cap : (c + 1) * cap, :] for block in blocks], axis=0)
            plain_ref[at : at + 2 * cap, c * LANES : (c + 1) * LANES] = rows.astype(BF16)
            scaled_ref[at : at + 2 * cap, c * LANES : (c + 1) * LANES] = (rows * weight).astype(BF16)
    scaled = scaled_ref[:, theirs]
    encode_node(
        code_ref,
        part_ref[:, theirs] + dot_t(scaled, plain_ref[:, theirs]),
        part_ref[:, mine] + dot_t(scaled, plain_ref[:, mine]),
    )


def in_columns(place, square, beside):
    first = place == 0
    return [
        [jnp.where(first, s, b) for s, b in zip(*pair)] + [jnp.where(first, b, s) for s, b in zip(*pair)]
        for pair in zip(square, beside)
    ]


def tiles_of(ref):
    half = ref.shape[0] // 2
    for i in range(2):
        for k in range(ref.shape[1] // half):
            yield i, k, slice(i * half, (i + 1) * half), slice(k * half, (k + 1) * half)


def near_node_kernel(own_ref, plain_ref, scaled_ref, code_ref, node_ref):
    share = own_ref.shape[0]
    mine, _ = halves(lax.axis_index("blk"), share)
    node_ref[...] = own_ref[...] + dot_t(scaled_ref[:, mine], plain_ref[...])
    terms = in_columns(lax.axis_index("blk"), *decode_node(code_ref))
    for i, k, rows, columns in tiles_of(node_ref):
        node_ref[rows, columns] += terms[i][k]


def far_node_kernel(near_ref, own_ref, code_ref, node_ref, out_ref):
    first = lax.axis_index("blk") == 0
    terms = in_columns(lax.axis_index("blk"), *decode_node(code_ref))
    for i, k, rows, columns in tiles_of(node_ref):
        far = own_ref[rows, columns] + terms[i][k]
        near = near_ref[rows, columns]
        node_ref[rows, columns] = far
        out_ref[rows, 0, columns] = jnp.where(first, near, far)
        out_ref[rows, 1, columns] = jnp.where(first, far, near)


def merge_folded(
    sibling_ref, near_ref, far_ref, node_ref, their_near_ref, their_own_ref, code_ref,
    node_hbm, out_hbm, out_ref, sems,
):
    share = far_ref.shape[0]
    half = share // 2
    each = share // PIECES
    copies = [pltpu.make_async_copy(node_ref, node_hbm, sems.at[PIECES])]
    copies[0].start()
    first = lax.axis_index("blk") == 0
    straight = jnp.broadcast_to(sibling_ref[0:1, 0:1], (each, LANES)) == 0
    terms = in_columns(lax.axis_index("blk"), *decode_node(code_ref))
    for p in range(PIECES):
        rows = slice(p * each, (p + 1) * each)
        inner = slice(p * each % half, p * each % half + each)
        for k in range(far_ref.shape[1] // half):
            columns = slice(k * half, (k + 1) * half)
            their_near = their_near_ref[rows, columns]
            their_far = their_own_ref[rows, columns] + terms[p * each // half][k][inner]
            near = near_ref[rows, columns] + jnp.where(straight, their_near, their_far)
            far = far_ref[rows, columns] + jnp.where(straight, their_far, their_near)
            out_ref[rows, 0, columns] = jnp.where(first, near, far)
            out_ref[rows, 1, columns] = jnp.where(first, far, near)
        span = pl.ds(p * each, each)
        copies.append(pltpu.make_async_copy(out_ref.at[span], out_hbm.at[span], sems.at[p]))
        copies[-1].start()
    for copy in copies:
        copy.wait()


def own_kernel(place_ref, part_ref, plain_ref, scaled_ref, own_ref, total=None):
    nodes, share, _ = part_ref.shape
    at = pl.multiple_of(place_ref[0] * share, share)
    for q in range(nodes):
        own_ref[q] = part_ref[q] + Product(scaled_ref.at[q], plain_ref.at[q], total).rows(at, share)


def node_kernel(own_ref, code_ref, out_ref, node_ref):
    nodes, share, _ = own_ref.shape
    arrived = decode_plain(code_ref, nodes, share)
    for q in range(nodes):
        value = own_ref[q] + arrived[q]
        node_ref[q] = value
        out_ref[:, q, :] = value


def merge_kernel(sibling_ref, node_ref, own_ref, code_ref, out_ref, partner_ref):
    nodes, share, _ = own_ref.shape
    arrived = decode_plain(code_ref, nodes, share)
    for q in range(nodes):
        partner_ref[q] = own_ref[q] + arrived[q]
    for q in range(nodes):
        out_ref[:, q, :] = node_ref[q] + partner_ref[sibling_ref[0, q]]


def call(kernel, out_shape, in_specs, flops=0, moved=1 << 20, vmem=32 << 20, **more):
    outs = jax.tree.map(lambda _: VMEM, out_shape)
    more.setdefault("out_specs", outs)
    return pl.pallas_call(
        kernel,
        out_shape=out_shape,
        in_specs=in_specs,
        compiler_params=pltpu.CompilerParams(vmem_limit_bytes=vmem),
        cost_estimate=pl.CostEstimate(flops=flops, bytes_accessed=moved, transcendentals=0),
        **more,
    )


def exchange_plain(plan, place, got, own_part, send_part, sibling, blk_count):
    peers, node_dev, share, state = send_part.shape
    shape = jax.ShapeDtypeStruct
    whole = [pltpu.VMEM((state, state), F32)] if share % LANES else []
    depth = max(plan.depth)
    to_partner = [(i, i ^ 1) for i in range(plan.leaf_count)]
    with jax.named_scope("routed_send"):
        code, plain, scaled = call(
            functools.partial(send_plain, plan),
            (
                shape((peers, node_dev * (share + GROUP), state), jnp.int16),
                shape((node_dev, depth, state), BF16),
                shape((node_dev, depth, state), BF16),
            ),
            [SMEM, VMEM, VMEM],
            scratch_shapes=whole,
            flops=2 * node_dev * depth * state * state,
        )(place, got, send_part)
    arrived = jnp.stack(
        [
            lax.ppermute(code[e - 1], "blk", [(i, i ^ e) for i in range(blk_count)])
            for e in range(1, blk_count)
        ]
    )
    with jax.named_scope("routed_own"):
        own = call(
            own_kernel,
            shape((node_dev, share, state), F32),
            [SMEM, VMEM, VMEM, VMEM],
            scratch_shapes=whole,
            flops=2 * node_dev * depth * share * state,
        )(place, own_part, plain, scaled)
    partner_own = lax.ppermute(own, "leaf", to_partner)
    partner_arrived = lax.ppermute(arrived, "leaf", to_partner)
    with jax.named_scope("node"):
        node_schur, node = call(
            node_kernel,
            (shape((share, node_dev, state), F32), shape((node_dev, share, state), F32)),
            [VMEM, VMEM],
        )(own, arrived)
    with jax.named_scope("merge"):
        merged = call(
            merge_kernel,
            shape((share, node_dev, state), F32),
            [SMEM, VMEM, VMEM, VMEM],
            scratch_shapes=[pltpu.VMEM((node_dev, share, state), F32)],
        )(sibling, node, partner_own, partner_arrived)
    return node_schur, merged


def bucket(plan, na_route, na_weight, na_rows):
    count, state = na_rows.shape
    any_spec = pl.BlockSpec(memory_space=pl.ANY)
    with jax.named_scope("bucket"):
        return call(
            functools.partial(bucket_kernel, plan),
            jax.ShapeDtypeStruct((plan.leaf_count, plan.block, LANES), BF16),
            [any_spec, any_spec, any_spec],
            scratch_shapes=[
                pltpu.VMEM((1, count), I32),
                pltpu.VMEM((count,), BF16),
                pltpu.VMEM((count, state + LANES), BF16),
                pltpu.VMEM((plan.leaf_count, plan.block, LANES), BF16),
                pltpu.SemaphoreType.DMA((3 + PIECES,)),
            ],
            out_specs=any_spec,
            vmem=60 << 20,
            flops=2 * plan.leaf_count * plan.rows * count * state,
        )(na_route.reshape(1, count), na_weight, na_rows)


def shards_plain(leaf_rows, leaf_weight, branching, sibling, node_block, na_rows, na_weight, na_route):
    leaf_count, blk_count = lax.axis_size("leaf"), lax.axis_size("blk")
    node_dev, most_children, depth, state = leaf_rows.shape
    count = na_rows.shape[0]
    share = state // blk_count
    peers = blk_count - 1
    plan = Plan(leaf_count, node_dev, 3 * count // (2 * leaf_count * node_dev), state, GROUP)
    place = lax.axis_index("blk").astype(I32).reshape(1)
    shape = jax.ShapeDtypeStruct
    blocks = bucket(plan, na_route, na_weight, na_rows)
    got = lax.all_to_all(blocks, "leaf", split_axis=0, concat_axis=0, tiled=True)
    with jax.named_scope("leaf_products"):
        own_part, send_part = call(
            leaf_kernel,
            (shape((node_dev, share, state), F32), shape((peers, node_dev, share, state), F32)),
            [
                SMEM,
                SMEM,
                pl.BlockSpec((1, most_children, depth), lambda n: (n, 0, 0)),
                pl.BlockSpec((1, most_children, depth, state), lambda n: (n, 0, 0, 0)),
                pl.BlockSpec((1, share, state), lambda n: (n, 0, 0)),
            ],
            out_specs=(
                pl.BlockSpec((1, share, state), lambda n: (n, 0, 0)),
                pl.BlockSpec((peers, 1, share, state), lambda n: (0, n, 0, 0)),
            ),
            grid=(node_dev,),
            scratch_shapes=[pltpu.VMEM((state, state), F32)],
            flops=2 * node_dev * most_children * depth * state * state,
            moved=8 << 20,
        )(place, branching, leaf_weight, leaf_rows, jnp.transpose(node_block, (1, 0, 2)))
    return exchange_plain(plan, place, got, own_part, send_part, sibling, blk_count)


def shards_folded(leaf_rows, leaf_weight, branching, sibling, node_block, na_rows, na_weight, na_route):
    leaf_count = lax.axis_size(SPLIT)
    node_dev, most_children, depth, state = leaf_rows.shape
    count = na_rows.shape[0]
    share = state // 2
    half = share // 2
    nodes = leaf_count * node_dev
    plan = Plan(nodes, 1, 3 * count // (2 * nodes), state, EXTRA, ORDER)
    shape = jax.ShapeDtypeStruct
    any_spec = pl.BlockSpec(memory_space=pl.ANY)
    across = [(0, 1), (1, 0)]
    to_partner = [(i, i ^ 1) for i in range(leaf_count)]
    result = shape((share, node_dev, state), F32)
    rows = shape((share, state), F32)
    codes = shape((6 * half + GROUP, half), jnp.int16)
    gathered = shape((nodes * plan.rows, state), BF16)

    blocks = bucket(plan, na_route, na_weight, na_rows)
    got = lax.all_to_all(blocks, ORDER, split_axis=0, concat_axis=0, tiled=True)

    own_block = jnp.transpose(node_block, (1, 0, 2))
    leaf = dict(
        scratch_shapes=[
            pltpu.VMEM((most_children, depth), BF16),
            pltpu.VMEM((most_children // 2, 2, depth, state), BF16),
            pltpu.VMEM((state, state), F32),
            pltpu.SemaphoreType.DMA((most_children // 2 + 1,)),
        ],
        flops=1,
        moved=1,
        vmem=24 << 20,
    )
    with jax.named_scope("far_leaf_products"):
        far_own, far_code = call(
            far_leaf_kernel, (rows, codes), [SMEM, any_spec, any_spec], **leaf
        )(branching, leaf_weight, leaf_rows)
    near_code = lax.ppermute(far_code, "blk", across)
    with jax.named_scope("near_leaf_products"):
        near_own, send_part, far_own = call(
            near_leaf_kernel, (rows, rows, rows), [SMEM, any_spec, any_spec, VMEM, VMEM], **leaf
        )(branching, leaf_weight, leaf_rows, own_block, far_own)
    their_own = lax.ppermute(far_own, SPLIT, to_partner)
    with jax.named_scope("routed_send"):
        code, plain, scaled = call(
            functools.partial(send_folded, plan),
            (codes, gathered, gathered),
            [VMEM, VMEM],
            flops=2 * nodes * plan.rows * share * state,
        )(got, send_part)
    arrived = lax.ppermute(code, "blk", across)
    with jax.named_scope("near_node"):
        near = call(near_node_kernel, rows, [VMEM, VMEM, VMEM, VMEM], flops=LONG)(
            near_own, plain, scaled, near_code
        )
    their_near = lax.ppermute(near, SPLIT, to_partner)
    their_arrived = lax.ppermute(arrived, SPLIT, to_partner)
    with jax.named_scope("far_node"):
        far, node = call(far_node_kernel, (rows, result), [VMEM, VMEM, VMEM], flops=LONG)(
            near, far_own, arrived
        )
    with jax.named_scope("merge"):
        return call(
            merge_folded,
            (result, result),
            [VMEM] * 7,
            out_specs=(any_spec, any_spec),
            scratch_shapes=[
                pltpu.VMEM((share, node_dev, state), F32),
                pltpu.SemaphoreType.DMA((PIECES + 1,)),
            ],
        )(sibling, near, far, node, their_near, their_own, their_arrived)


def solution(mesh):
    leaf_count, blk_count = mesh.shape["leaf"], mesh.shape["blk"]
    plain = jax.shard_map(
        shards_plain, mesh=mesh, in_specs=in_specs("leaf"), out_specs=out_specs("leaf"), check_vma=False
    )
    if blk_count != 2 or leaf_count != 2 ** len(SPLIT):
        return plain
    split = jax.sharding.Mesh(mesh.devices.reshape((2,) * len(ORDER)), (*SPLIT, "blk"))
    folded = jax.shard_map(
        shards_folded, mesh=split, in_specs=in_specs(SPLIT), out_specs=out_specs(SPLIT), check_vma=False
    )

    def choose(leaf_rows, *more):
        nodes, children, _, state = leaf_rows.shape
        fits = nodes == 2 * leaf_count and children % 2 == 0 and state == 4 * LANES
        return (folded if fits else plain)(leaf_rows, *more)

    return choose


def in_specs(leaf):
    every = ((leaf,) if isinstance(leaf, str) else leaf) + ("blk",)
    return (
        P(leaf, None, "blk", None),
        P(leaf, None, "blk"),
        P(leaf),
        P(leaf, None),
        P("blk", leaf, None),
        P(every, None),
        P(every),
        P(every, None),
    )


def out_specs(leaf):
    return (P("blk", leaf, None), P("blk", leaf, None))
```

```python
import functools

import jax
import jax.numpy as jnp
from jax import lax
from jax.experimental import pallas as pl
from jax.experimental.pallas import tpu as pltpu
from jax.sharding import PartitionSpec as P

F32 = jnp.float32
BF16 = jnp.bfloat16
I32 = jnp.int32
LANES = 128
GROUP = 16
EXTRA = 8
PIECES = 4
VMEM = pl.BlockSpec(memory_space=pltpu.VMEM)
SMEM = pl.BlockSpec(memory_space=pltpu.SMEM)
CODE = 32000.0
SPLIT = ("z1", "z0", "y", "core")
ORDER = ("blk", "y", "z1", "core", "z0")
LONG = 20_000_000_000


class Plan:
    def __init__(self, leaf_count, node_dev, capacity, state, unit, order=()):
        self.order = order
        self.leaf_count, self.node_dev, self.capacity, self.state = leaf_count, node_dev, capacity, state
        self.full = capacity // GROUP * GROUP
        self.rest = capacity - self.full
        self.rows = -(-node_dev * capacity // unit) * unit
        self.groups = self.rows // GROUP
        self.slabs = state // LANES
        self.block = self.slabs * self.rows + EXTRA
        self.groups_of = [
            [g for g in range(self.groups) if q in {self.node_at(g * GROUP + i) for i in range(GROUP)}]
            for q in range(node_dev)
        ]
        self.depth = [leaf_count * GROUP * len(g) for g in self.groups_of]

    def block_of(self, node):
        if not self.order:
            return node
        block = jnp.zeros_like(node)
        for name in self.order:
            block = 2 * block + (node >> (len(SPLIT) - (*SPLIT, "blk").index(name)) & 1)
        return block

    def node_at(self, row):
        if row < self.node_dev * self.full:
            return row // self.full
        return min((row - self.node_dev * self.full) // self.rest, self.node_dev - 1) if self.rest else 0


def dot_t(a, b):
    return lax.dot_general(a, b, (((0,), (0,)), ((), ())), preferred_element_type=F32)


def bucket_kernel(plan, route_hbm, weight_hbm, rows_hbm, out_hbm, route_ref, weight_ref, rows_ref, out_ref, sems):
    count = rows_hbm.shape[0]
    copies = [
        pltpu.make_async_copy(route_hbm, route_ref, sems.at[0]),
        pltpu.make_async_copy(weight_hbm, weight_ref, sems.at[1]),
        pltpu.make_async_copy(rows_hbm, rows_ref, sems.at[2]),
    ]
    for copy in copies:
        copy.start()
    nodes = plan.leaf_count * plan.node_dev
    before = (
        lax.broadcasted_iota(I32, (count, count), 0) < lax.broadcasted_iota(I32, (count, count), 1)
    ).astype(BF16)
    copies[0].wait()
    route = route_ref[...]
    member = lax.broadcasted_iota(I32, (nodes, count), 0) == route
    seen = jnp.dot(member.astype(BF16), before, preferred_element_type=F32)
    position = jnp.sum(jnp.where(member, seen, 0.0), axis=0, keepdims=True).astype(I32)
    route = plan.block_of(route)
    owner = route // plan.node_dev
    q = route - owner * plan.node_dev
    slot = owner * plan.rows + jnp.where(
        position < plan.full,
        q * plan.full + position,
        plan.node_dev * plan.full + q * plan.rest + position - plan.full,
    )
    copies[1].wait()
    weight = weight_ref[...].reshape(1, count).astype(F32)
    lane = lax.broadcasted_iota(I32, (EXTRA, LANES), 1)
    sub = lax.broadcasted_iota(I32, (EXTRA, LANES), 0)
    want = []
    for g in range(plan.rows // EXTRA):
        q_of = jnp.full((EXTRA, LANES), plan.node_at(g * EXTRA), I32)
        for i in range(1, EXTRA):
            step = plan.node_at(g * EXTRA + i) - plan.node_at(g * EXTRA + i - 1)
            if step:
                q_of = q_of + jnp.where(sub >= i, step, 0)
        want.append(lane == g * plan.node_dev + q_of)
    copies[2].wait()
    each = plan.leaf_count // PIECES
    leaving = []
    for p in range(PIECES):
        place = lax.broadcasted_iota(I32, (each * plan.rows, count), 0) + p * each * plan.rows
        hit = jnp.where(place == slot, 1.0, 0.0).astype(BF16)
        weights = jnp.sum(jnp.where(place == slot, weight, 0.0), axis=1, keepdims=True) + jnp.zeros((1, LANES), F32)
        filled = jnp.dot(hit, rows_ref[...], preferred_element_type=F32).astype(BF16)
        for i in range(each):
            at = i * plan.rows
            d = p * each + i
            for c in range(plan.slabs):
                out_ref[d, c * plan.rows : (c + 1) * plan.rows, :] = filled[
                    at : at + plan.rows, c * LANES : (c + 1) * LANES
                ]
            extra = jnp.zeros((EXTRA, LANES), F32)
            for g in range(plan.rows // EXTRA):
                extra = jnp.where(want[g], weights[at + g * EXTRA : at + (g + 1) * EXTRA, :], extra)
            out_ref[d, plan.slabs * plan.rows :, :] = extra.astype(BF16)
        span = pl.ds(p * each, each)
        leaving.append(pltpu.make_async_copy(out_ref.at[span], out_hbm.at[span], sems.at[3 + p]))
        leaving[-1].start()
    for copy in leaving:
        copy.wait()


def leaf_kernel(place_ref, branching_ref, weight_ref, rows_ref, block_ref, own_ref, send_ref, total):
    n = pl.program_id(0)
    share = own_ref.shape[1]
    peers = send_ref.shape[0]
    blk = place_ref[0]
    columns = jnp.transpose(weight_ref[0].astype(F32))
    total[...] = jnp.zeros_like(total)
    for b in range(rows_ref.shape[1]):

        @pl.when(b < branching_ref[n])
        def _():
            rows = rows_ref[0, b]
            scaled = (rows.astype(F32) * columns[:, b : b + 1]).astype(BF16)
            total[...] += dot_t(scaled, rows)

    own_ref[0] = total[pl.ds(pl.multiple_of(blk * share, share), share), :] + block_ref[0].astype(F32)
    for e in range(1, peers + 1):
        at = pl.multiple_of((blk ^ e) * share, share)
        send_ref[e - 1, 0] = total[pl.ds(at, share), :]


class Product:
    def __init__(self, scaled_ref, plain_ref, total):
        self.scaled_ref, self.plain_ref, self.total = scaled_ref, plain_ref, total
        if total is not None:
            total[...] = dot_t(scaled_ref[...], plain_ref[...])

    def rows(self, at, share):
        if self.total is not None:
            return self.total[pl.ds(at, share), :]
        return dot_t(self.scaled_ref[:, pl.ds(at, share)], self.plain_ref[...])


def gather_rows(plan, got_ref, plain_ref, scaled_ref):
    for d in range(plan.leaf_count):
        extra = got_ref[d, plan.slabs * plan.rows :, :].astype(F32)
        for g in range(plan.groups):
            rows = jnp.concatenate(
                [
                    got_ref[d, c * plan.rows + g * GROUP : c * plan.rows + (g + 1) * GROUP, :]
                    for c in range(plan.slabs)
                ],
                axis=1,
            )
            wide = rows.astype(F32)
            for q in range(plan.node_dev):
                if g not in plan.groups_of[q]:
                    continue
                at = (plan.groups_of[q].index(g) * plan.leaf_count + d) * GROUP
                first = g * GROUP // EXTRA * plan.node_dev + q
                places = range(first, first + GROUP // EXTRA * plan.node_dev, plan.node_dev)
                weight = jnp.concatenate([extra[:, j : j + 1] for j in places], axis=0)
                plain_ref[q, at : at + GROUP, :] = rows
                scaled_ref[q, at : at + GROUP, :] = (wide * weight).astype(BF16)


def scale_of(most):
    power = jnp.ceil(8.0 * jnp.log2(jnp.maximum(most, 1e-30)))
    return power, CODE * jnp.exp2(-0.125 * power)


def to_code(value):
    return jnp.round(value).astype(I32).astype(jnp.int16)


def from_code(code):
    return code.astype(I32).astype(F32)


def diagonal(width):
    return lax.broadcasted_iota(I32, (width, width), 0) == lax.broadcasted_iota(I32, (width, width), 1)


def as_line(column):
    return jnp.sum(jnp.where(diagonal(column.shape[0]), column, 0.0), axis=0, keepdims=True)


def as_column(line):
    return jnp.sum(jnp.where(diagonal(line.shape[1]), line, 0.0), axis=1, keepdims=True)


def send_plain(plan, place_ref, got_ref, part_ref, code_ref, plain_ref, scaled_ref, total=None):
    blk = place_ref[0]
    peers, nodes, share, state = part_ref.shape
    gather_rows(plan, got_ref, plain_ref, scaled_ref)
    for q in range(nodes):
        product = Product(scaled_ref.at[q], plain_ref.at[q], total)
        for e in range(1, peers + 1):
            at = pl.multiple_of((blk ^ e) * share, share)
            value = part_ref[e - 1, q] + product.rows(at, share)
            power, factor = scale_of(jnp.max(jnp.abs(value), axis=1, keepdims=True))
            code_ref[e - 1, q * share : (q + 1) * share, :] = to_code(value * factor)
            line = jnp.concatenate([as_line(power), jnp.zeros((1, state - share), F32)], axis=1)
            base = nodes * share + q * GROUP
            code_ref[e - 1, base : base + GROUP, :] = to_code(jnp.broadcast_to(line, (GROUP, state)))


def decode_plain(code_ref, nodes, share):
    values = []
    for q in range(nodes):
        base = nodes * share + q * GROUP
        value = None
        for e in range(code_ref.shape[0]):
            power = as_column(from_code(code_ref[e, base : base + GROUP, :])[0:1, :share])
            term = from_code(code_ref[e, q * share : (q + 1) * share, :]) * (
                jnp.exp2(0.125 * power) * (1.0 / CODE)
            )
            value = term if value is None else value + term
        values.append(value)
    return values


def encode_node(code_ref, square, beside):
    half = code_ref.shape[1]
    upper, lower = square[:half, :half], square[half:, half:]
    pieces = [square[:half, half:]]
    pieces += [beside[r : r + half, c : c + half] for r in (0, half) for c in (0, half)]
    most = jnp.maximum(jnp.abs(upper), jnp.abs(lower))
    for piece in pieces:
        most = jnp.maximum(most, jnp.abs(piece))
    power, factor = scale_of(jnp.max(most, axis=1, keepdims=True))
    row = lax.broadcasted_iota(I32, (half, half), 0)
    column = lax.broadcasted_iota(I32, (half, half), 1)
    lower = lower * factor
    code_ref[:half, :] = to_code(jnp.where(column >= row, upper * factor, lower))
    for k, piece in enumerate(pieces):
        code_ref[(k + 1) * half : (k + 2) * half, :] = to_code(piece * factor)
    corner = jnp.sum(jnp.where(column == row, jnp.round(lower), 0.0), axis=0, keepdims=True)
    line = lax.broadcasted_iota(I32, (GROUP, half), 0)
    code_ref[6 * half :, :] = to_code(
        jnp.where(line == 0, as_line(power), jnp.where(line == 1, corner, 0.0))
    )


def decode_node(code_ref):
    half = code_ref.shape[1]
    lines = from_code(code_ref[6 * half :, :])
    line = jnp.exp2(0.125 * jnp.broadcast_to(lines[0:1, :], (half, half))) * (1.0 / CODE)
    step = jnp.transpose(line)
    raw = [from_code(code_ref[k * half : (k + 1) * half, :]) for k in range(6)]
    turned, mirror = (jnp.transpose(r) * line for r in raw[:2])
    pieces = [r * step for r in raw]
    both = pieces[0]
    row = lax.broadcasted_iota(I32, (half, half), 0)
    column = lax.broadcasted_iota(I32, (half, half), 1)
    upper = jnp.where(column >= row, both, turned)
    lower = jnp.where(column < row, both, jnp.where(column == row, lines[1:2, :] * line, turned))
    square = ((upper, pieces[1]), (mirror, lower))
    beside = ((pieces[2], pieces[3]), (pieces[4], pieces[5]))
    return square, beside


def halves(place, share):
    mine = pl.ds(pl.multiple_of(place * share, share), share)
    theirs = pl.ds(pl.multiple_of((1 - place) * share, share), share)
    return mine, theirs


def leaf_sum(node, branching_ref, weight_hbm, rows_hbm, weight_ref, rows_ref, total, sems):
    pairs = rows_hbm.shape[1] // 2
    depth, state = rows_hbm.shape[2:]
    count = branching_ref[node]
    weights = pltpu.make_async_copy(weight_hbm.at[node], weight_ref, sems.at[pairs])
    copies = [
        pltpu.make_async_copy(rows_hbm.at[node, pl.ds(2 * p, 2)], rows_ref.at[p], sems.at[p])
        for p in range(pairs)
    ]
    copies[0].start()
    weights.start()
    for p in range(1, pairs):
        pl.when(2 * p < count)(copies[p].start)
    weights.wait()
    live = lax.broadcasted_iota(I32, weight_ref.shape, 0) < count
    columns = jnp.transpose(jnp.where(live, weight_ref[...].astype(F32), 0.0))

    def term(p):
        copies[p].wait()
        rows = rows_ref[p].reshape(2 * depth, state)
        weight = jnp.concatenate([columns[:, 2 * p : 2 * p + 1], columns[:, 2 * p + 1 : 2 * p + 2]], axis=0)
        return dot_t((rows.astype(F32) * weight).astype(BF16), rows)

    total[...] = term(0)
    for p in range(1, pairs):

        @pl.when(2 * p < count)
        def _():
            total[...] += term(p)


def far_leaf_kernel(
    branching_ref, weight_hbm, rows_hbm, own_ref, code_ref, weight_ref, rows_ref, total, sems
):
    share = own_ref.shape[0]
    mine, theirs = halves(lax.axis_index("blk"), share)
    node = 1 - lax.axis_index("blk")
    leaf_sum(node, branching_ref, weight_hbm, rows_hbm, weight_ref, rows_ref, total, sems)
    encode_node(code_ref, total[theirs, theirs], total[theirs, mine])
    own_ref[...] = total[mine, :]


def near_leaf_kernel(
    branching_ref, weight_hbm, rows_hbm, block_ref, far_ref,
    own_ref, send_ref, far_out, weight_ref, rows_ref, total, sems,
):
    share = own_ref.shape[0]
    mine, theirs = halves(lax.axis_index("blk"), share)
    node = lax.axis_index("blk")
    leaf_sum(node, branching_ref, weight_hbm, rows_hbm, weight_ref, rows_ref, total, sems)
    send_ref[...] = total[theirs, :]
    own_ref[...] = total[mine, :] + block_ref[node].astype(F32)
    far_out[...] = far_ref[...] + block_ref[1 - node].astype(F32)


def weighted(plan, got_ref, plain_ref, columns, scaled_ref):
    cap = plan.rows
    for d in range(0, plan.leaf_count, 2):
        extras = [got_ref[d + i, plan.slabs * cap :, :].astype(F32) for i in range(2)]
        weight = jnp.concatenate([e[:, g : g + 1] for e in extras for g in range(cap // EXTRA)], axis=0)
        weight = jnp.broadcast_to(weight, (2 * cap, scaled_ref.shape[1])).astype(BF16)
        rows = slice(d * cap, (d + 2) * cap)
        scaled_ref[rows, :] = plain_ref[rows, columns] * weight


def send_folded(plan, got_ref, part_ref, code_ref, plain_ref, scaled_ref):
    share = part_ref.shape[0]
    mine, theirs = halves(lax.axis_index("blk"), share)
    cap = plan.rows
    for d in range(0, plan.leaf_count, 2):
        for c in range(plan.slabs):
            plain_ref[d * cap : (d + 2) * cap, c * LANES : (c + 1) * LANES] = jnp.concatenate(
                [got_ref[d + i, c * cap : (c + 1) * cap, :] for i in range(2)], axis=0
            )
    weighted(plan, got_ref, plain_ref, theirs, scaled_ref)
    scaled = scaled_ref[...]
    encode_node(
        code_ref,
        part_ref[:, theirs] + dot_t(scaled, plain_ref[:, theirs]),
        part_ref[:, mine] + dot_t(scaled, plain_ref[:, mine]),
    )


def in_columns(place, square, beside):
    first = place == 0
    return [
        [jnp.where(first, s, b) for s, b in zip(*pair)] + [jnp.where(first, b, s) for s, b in zip(*pair)]
        for pair in zip(square, beside)
    ]


def tiles_of(ref):
    half = ref.shape[0] // 2
    for i in range(2):
        for k in range(ref.shape[1] // half):
            yield i, k, slice(i * half, (i + 1) * half), slice(k * half, (k + 1) * half)


def near_node_kernel(plan, own_ref, got_ref, plain_ref, code_ref, node_ref, scaled_ref):
    mine, _ = halves(lax.axis_index("blk"), own_ref.shape[0])
    weighted(plan, got_ref, plain_ref, mine, scaled_ref)
    node_ref[...] = own_ref[...] + dot_t(scaled_ref[...], plain_ref[...])
    terms = in_columns(lax.axis_index("blk"), *decode_node(code_ref))
    for i, k, rows, columns in tiles_of(node_ref):
        node_ref[rows, columns] += terms[i][k]


def far_node_kernel(near_ref, own_ref, code_ref, node_ref, out_ref):
    first = lax.axis_index("blk") == 0
    terms = in_columns(lax.axis_index("blk"), *decode_node(code_ref))
    for i, k, rows, columns in tiles_of(node_ref):
        far = own_ref[rows, columns] + terms[i][k]
        near = near_ref[rows, columns]
        node_ref[rows, columns] = far
        out_ref[rows, 0, columns] = jnp.where(first, near, far)
        out_ref[rows, 1, columns] = jnp.where(first, far, near)


def merge_folded(
    sibling_ref, near_ref, far_ref, node_ref, their_near_ref, their_own_ref, code_ref,
    node_hbm, out_hbm, out_ref, sems,
):
    share = far_ref.shape[0]
    half = share // 2
    each = share // PIECES
    copies = [pltpu.make_async_copy(node_ref, node_hbm, sems.at[PIECES])]
    copies[0].start()
    first = lax.axis_index("blk") == 0
    straight = jnp.broadcast_to(sibling_ref[0:1, 0:1], (each, LANES)) == 0
    terms = in_columns(lax.axis_index("blk"), *decode_node(code_ref))
    for p in range(PIECES):
        rows = slice(p * each, (p + 1) * each)
        inner = slice(p * each % half, p * each % half + each)
        for k in range(far_ref.shape[1] // half):
            columns = slice(k * half, (k + 1) * half)
            their_near = their_near_ref[rows, columns]
            their_far = their_own_ref[rows, columns] + terms[p * each // half][k][inner]
            near = near_ref[rows, columns] + jnp.where(straight, their_near, their_far)
            far = far_ref[rows, columns] + jnp.where(straight, their_far, their_near)
            out_ref[rows, 0, columns] = jnp.where(first, near, far)
            out_ref[rows, 1, columns] = jnp.where(first, far, near)
        span = pl.ds(p * each, each)
        copies.append(pltpu.make_async_copy(out_ref.at[span], out_hbm.at[span], sems.at[p]))
        copies[-1].start()
    for copy in copies:
        copy.wait()


def own_kernel(place_ref, part_ref, plain_ref, scaled_ref, own_ref, total=None):
    nodes, share, _ = part_ref.shape
    at = pl.multiple_of(place_ref[0] * share, share)
    for q in range(nodes):
        own_ref[q] = part_ref[q] + Product(scaled_ref.at[q], plain_ref.at[q], total).rows(at, share)


def node_kernel(own_ref, code_ref, out_ref, node_ref):
    nodes, share, _ = own_ref.shape
    arrived = decode_plain(code_ref, nodes, share)
    for q in range(nodes):
        value = own_ref[q] + arrived[q]
        node_ref[q] = value
        out_ref[:, q, :] = value


def merge_kernel(sibling_ref, node_ref, own_ref, code_ref, out_ref, partner_ref):
    nodes, share, _ = own_ref.shape
    arrived = decode_plain(code_ref, nodes, share)
    for q in range(nodes):
        partner_ref[q] = own_ref[q] + arrived[q]
    for q in range(nodes):
        out_ref[:, q, :] = node_ref[q] + partner_ref[sibling_ref[0, q]]


def call(kernel, out_shape, in_specs, flops=0, moved=1 << 20, vmem=32 << 20, **more):
    outs = jax.tree.map(lambda _: VMEM, out_shape)
    more.setdefault("out_specs", outs)
    return pl.pallas_call(
        kernel,
        out_shape=out_shape,
        in_specs=in_specs,
        compiler_params=pltpu.CompilerParams(vmem_limit_bytes=vmem),
        cost_estimate=pl.CostEstimate(flops=flops, bytes_accessed=moved, transcendentals=0),
        **more,
    )


def exchange_plain(plan, place, got, own_part, send_part, sibling, blk_count):
    peers, node_dev, share, state = send_part.shape
    shape = jax.ShapeDtypeStruct
    whole = [pltpu.VMEM((state, state), F32)] if share % LANES else []
    depth = max(plan.depth)
    to_partner = [(i, i ^ 1) for i in range(plan.leaf_count)]
    with jax.named_scope("routed_send"):
        code, plain, scaled = call(
            functools.partial(send_plain, plan),
            (
                shape((peers, node_dev * (share + GROUP), state), jnp.int16),
                shape((node_dev, depth, state), BF16),
                shape((node_dev, depth, state), BF16),
            ),
            [SMEM, VMEM, VMEM],
            scratch_shapes=whole,
            flops=2 * node_dev * depth * state * state,
        )(place, got, send_part)
    arrived = jnp.stack(
        [
            lax.ppermute(code[e - 1], "blk", [(i, i ^ e) for i in range(blk_count)])
            for e in range(1, blk_count)
        ]
    )
    with jax.named_scope("routed_own"):
        own = call(
            own_kernel,
            shape((node_dev, share, state), F32),
            [SMEM, VMEM, VMEM, VMEM],
            scratch_shapes=whole,
            flops=2 * node_dev * depth * share * state,
        )(place, own_part, plain, scaled)
    partner_own = lax.ppermute(own, "leaf", to_partner)
    partner_arrived = lax.ppermute(arrived, "leaf", to_partner)
    with jax.named_scope("node"):
        node_schur, node = call(
            node_kernel,
            (shape((share, node_dev, state), F32), shape((node_dev, share, state), F32)),
            [VMEM, VMEM],
        )(own, arrived)
    with jax.named_scope("merge"):
        merged = call(
            merge_kernel,
            shape((share, node_dev, state), F32),
            [SMEM, VMEM, VMEM, VMEM],
            scratch_shapes=[pltpu.VMEM((node_dev, share, state), F32)],
        )(sibling, node, partner_own, partner_arrived)
    return node_schur, merged


def bucket(plan, na_route, na_weight, na_rows):
    count, state = na_rows.shape
    any_spec = pl.BlockSpec(memory_space=pl.ANY)
    with jax.named_scope("bucket"):
        return call(
            functools.partial(bucket_kernel, plan),
            jax.ShapeDtypeStruct((plan.leaf_count, plan.block, LANES), BF16),
            [any_spec, any_spec, any_spec],
            scratch_shapes=[
                pltpu.VMEM((1, count), I32),
                pltpu.VMEM((count,), BF16),
                pltpu.VMEM((count, state), BF16),
                pltpu.VMEM((plan.leaf_count, plan.block, LANES), BF16),
                pltpu.SemaphoreType.DMA((3 + PIECES,)),
            ],
            out_specs=any_spec,
            vmem=60 << 20,
            flops=2 * plan.leaf_count * plan.rows * count * state,
        )(na_route.reshape(1, count), na_weight, na_rows)


def shards_plain(leaf_rows, leaf_weight, branching, sibling, node_block, na_rows, na_weight, na_route):
    leaf_count, blk_count = lax.axis_size("leaf"), lax.axis_size("blk")
    node_dev, most_children, depth, state = leaf_rows.shape
    count = na_rows.shape[0]
    share = state // blk_count
    peers = blk_count - 1
    plan = Plan(leaf_count, node_dev, 3 * count // (2 * leaf_count * node_dev), state, GROUP)
    place = lax.axis_index("blk").astype(I32).reshape(1)
    shape = jax.ShapeDtypeStruct
    blocks = bucket(plan, na_route, na_weight, na_rows)
    got = lax.all_to_all(blocks, "leaf", split_axis=0, concat_axis=0, tiled=True)
    with jax.named_scope("leaf_products"):
        own_part, send_part = call(
            leaf_kernel,
            (shape((node_dev, share, state), F32), shape((peers, node_dev, share, state), F32)),
            [
                SMEM,
                SMEM,
                pl.BlockSpec((1, most_children, depth), lambda n: (n, 0, 0)),
                pl.BlockSpec((1, most_children, depth, state), lambda n: (n, 0, 0, 0)),
                pl.BlockSpec((1, share, state), lambda n: (n, 0, 0)),
            ],
            out_specs=(
                pl.BlockSpec((1, share, state), lambda n: (n, 0, 0)),
                pl.BlockSpec((peers, 1, share, state), lambda n: (0, n, 0, 0)),
            ),
            grid=(node_dev,),
            scratch_shapes=[pltpu.VMEM((state, state), F32)],
            flops=2 * node_dev * most_children * depth * state * state,
            moved=8 << 20,
        )(place, branching, leaf_weight, leaf_rows, jnp.transpose(node_block, (1, 0, 2)))
    return exchange_plain(plan, place, got, own_part, send_part, sibling, blk_count)


def shards_folded(leaf_rows, leaf_weight, branching, sibling, node_block, na_rows, na_weight, na_route):
    leaf_count = lax.axis_size(SPLIT)
    node_dev, most_children, depth, state = leaf_rows.shape
    count = na_rows.shape[0]
    share = state // 2
    half = share // 2
    nodes = leaf_count * node_dev
    plan = Plan(nodes, 1, 3 * count // (2 * nodes), state, EXTRA, ORDER)
    shape = jax.ShapeDtypeStruct
    any_spec = pl.BlockSpec(memory_space=pl.ANY)
    across = [(0, 1), (1, 0)]
    to_partner = [(i, i ^ 1) for i in range(leaf_count)]
    result = shape((share, node_dev, state), F32)
    rows = shape((share, state), F32)
    codes = shape((6 * half + GROUP, half), jnp.int16)
    gathered = shape((nodes * plan.rows, state), BF16)

    blocks = bucket(plan, na_route, na_weight, na_rows)
    got = lax.all_to_all(blocks, ORDER, split_axis=0, concat_axis=0, tiled=True)

    own_block = jnp.transpose(node_block, (1, 0, 2))
    leaf = dict(
        scratch_shapes=[
            pltpu.VMEM((most_children, depth), BF16),
            pltpu.VMEM((most_children // 2, 2, depth, state), BF16),
            pltpu.VMEM((state, state), F32),
            pltpu.SemaphoreType.DMA((most_children // 2 + 1,)),
        ],
        flops=1,
        moved=1,
        vmem=24 << 20,
    )
    with jax.named_scope("far_leaf_products"):
        far_own, far_code = call(
            far_leaf_kernel, (rows, codes), [SMEM, any_spec, any_spec], **leaf
        )(branching, leaf_weight, leaf_rows)
    near_code = lax.ppermute(far_code, "blk", across)
    with jax.named_scope("near_leaf_products"):
        near_own, send_part, far_own = call(
            near_leaf_kernel, (rows, rows, rows), [SMEM, any_spec, any_spec, VMEM, VMEM], **leaf
        )(branching, leaf_weight, leaf_rows, own_block, far_own)
    their_own = lax.ppermute(far_own, SPLIT, to_partner)
    half_scaled = pltpu.VMEM((nodes * plan.rows, share), BF16)
    with jax.named_scope("routed_send"):
        code, plain = call(
            functools.partial(send_folded, plan),
            (codes, gathered),
            [VMEM, VMEM],
            scratch_shapes=[half_scaled],
            flops=2 * nodes * plan.rows * share * state,
        )(got, send_part)
    arrived = lax.ppermute(code, "blk", across)
    with jax.named_scope("near_node"):
        near = call(
            functools.partial(near_node_kernel, plan),
            rows,
            [VMEM] * 4,
            scratch_shapes=[half_scaled],
            flops=LONG,
        )(near_own, got, plain, near_code)
    their_near = lax.ppermute(near, SPLIT, to_partner)
    their_arrived = lax.ppermute(arrived, SPLIT, to_partner)
    with jax.named_scope("far_node"):
        far, node = call(far_node_kernel, (rows, result), [VMEM, VMEM, VMEM], flops=LONG)(
            near, far_own, arrived
        )
    with jax.named_scope("merge"):
        return call(
            merge_folded,
            (result, result),
            [VMEM] * 7,
            out_specs=(any_spec, any_spec),
            scratch_shapes=[
                pltpu.VMEM((share, node_dev, state), F32),
                pltpu.SemaphoreType.DMA((PIECES + 1,)),
            ],
        )(sibling, near, far, node, their_near, their_own, their_arrived)


def solution(mesh):
    leaf_count, blk_count = mesh.shape["leaf"], mesh.shape["blk"]
    plain = jax.shard_map(
        shards_plain, mesh=mesh, in_specs=in_specs("leaf"), out_specs=out_specs("leaf"), check_vma=False
    )
    if blk_count != 2 or leaf_count != 2 ** len(SPLIT):
        return plain
    split = jax.sharding.Mesh(mesh.devices.reshape((2,) * len(ORDER)), (*SPLIT, "blk"))
    folded = jax.shard_map(
        shards_folded, mesh=split, in_specs=in_specs(SPLIT), out_specs=out_specs(SPLIT), check_vma=False
    )

    def choose(leaf_rows, *more):
        nodes, children, _, state = leaf_rows.shape
        fits = nodes == 2 * leaf_count and children % 2 == 0 and state == 4 * LANES
        return (folded if fits else plain)(leaf_rows, *more)

    return choose


def in_specs(leaf):
    every = ((leaf,) if isinstance(leaf, str) else leaf) + ("blk",)
    return (
        P(leaf, None, "blk", None),
        P(leaf, None, "blk"),
        P(leaf),
        P(leaf, None),
        P("blk", leaf, None),
        P(every, None),
        P(every),
        P(every, None),
    )


def out_specs(leaf):
    return (P("blk", leaf, None), P("blk", leaf, None))
```

```python
import functools

import jax
import jax.numpy as jnp
from jax import lax
from jax.experimental import pallas as pl
from jax.experimental.pallas import tpu as pltpu
from jax.sharding import PartitionSpec as P

F32 = jnp.float32
BF16 = jnp.bfloat16
I32 = jnp.int32
LANES = 128
GROUP = 16
EXTRA = 8
PIECES = 4
VMEM = pl.BlockSpec(memory_space=pltpu.VMEM)
SMEM = pl.BlockSpec(memory_space=pltpu.SMEM)
CODE = 32000.0
SPLIT = ("z1", "z0", "y", "core")
ORDER = ("blk", "y", "z1", "core", "z0")
LONG = 20_000_000_000


class Plan:
    def __init__(self, leaf_count, node_dev, capacity, state, unit, order=()):
        self.order = order
        self.leaf_count, self.node_dev, self.capacity, self.state = leaf_count, node_dev, capacity, state
        self.full = capacity // GROUP * GROUP
        self.rest = capacity - self.full
        self.rows = -(-node_dev * capacity // unit) * unit
        self.groups = self.rows // GROUP
        self.slabs = state // LANES
        self.block = self.slabs * self.rows + EXTRA
        self.groups_of = [
            [g for g in range(self.groups) if q in {self.node_at(g * GROUP + i) for i in range(GROUP)}]
            for q in range(node_dev)
        ]
        self.depth = [leaf_count * GROUP * len(g) for g in self.groups_of]

    def block_of(self, node):
        if not self.order:
            return node
        block = jnp.zeros_like(node)
        for name in self.order:
            block = 2 * block + (node >> (len(SPLIT) - (*SPLIT, "blk").index(name)) & 1)
        return block

    def node_at(self, row):
        if row < self.node_dev * self.full:
            return row // self.full
        return min((row - self.node_dev * self.full) // self.rest, self.node_dev - 1) if self.rest else 0


def dot_t(a, b):
    return lax.dot_general(a, b, (((0,), (0,)), ((), ())), preferred_element_type=F32)


def bucket_kernel(plan, route_hbm, weight_hbm, rows_hbm, out_hbm, route_ref, weight_ref, rows_ref, out_ref, sems):
    count = rows_hbm.shape[0]
    copies = [
        pltpu.make_async_copy(route_hbm, route_ref, sems.at[0]),
        pltpu.make_async_copy(weight_hbm, weight_ref, sems.at[1]),
        pltpu.make_async_copy(rows_hbm, rows_ref, sems.at[2]),
    ]
    for copy in copies:
        copy.start()
    nodes = plan.leaf_count * plan.node_dev
    before = (
        lax.broadcasted_iota(I32, (count, count), 0) < lax.broadcasted_iota(I32, (count, count), 1)
    ).astype(BF16)
    copies[0].wait()
    route = route_ref[...]
    member = lax.broadcasted_iota(I32, (nodes, count), 0) == route
    seen = jnp.dot(member.astype(BF16), before, preferred_element_type=F32)
    position = jnp.sum(jnp.where(member, seen, 0.0), axis=0, keepdims=True).astype(I32)
    route = plan.block_of(route)
    owner = route // plan.node_dev
    q = route - owner * plan.node_dev
    slot = owner * plan.rows + jnp.where(
        position < plan.full,
        q * plan.full + position,
        plan.node_dev * plan.full + q * plan.rest + position - plan.full,
    )
    copies[1].wait()
    weight = weight_ref[...].reshape(1, count).astype(F32)
    lane = lax.broadcasted_iota(I32, (EXTRA, LANES), 1)
    sub = lax.broadcasted_iota(I32, (EXTRA, LANES), 0)
    want = []
    for g in range(plan.rows // EXTRA):
        q_of = jnp.full((EXTRA, LANES), plan.node_at(g * EXTRA), I32)
        for i in range(1, EXTRA):
            step = plan.node_at(g * EXTRA + i) - plan.node_at(g * EXTRA + i - 1)
            if step:
                q_of = q_of + jnp.where(sub >= i, step, 0)
        want.append(lane == g * plan.node_dev + q_of)
    copies[2].wait()
    each = plan.leaf_count // PIECES
    leaving = []
    for p in range(PIECES):
        place = lax.broadcasted_iota(I32, (each * plan.rows, count), 0) + p * each * plan.rows
        hit = jnp.where(place == slot, 1.0, 0.0).astype(BF16)
        weights = jnp.sum(jnp.where(place == slot, weight, 0.0), axis=1, keepdims=True) + jnp.zeros((1, LANES), F32)
        filled = jnp.dot(hit, rows_ref[...], preferred_element_type=F32).astype(BF16)
        for i in range(each):
            at = i * plan.rows
            d = p * each + i
            for c in range(plan.slabs):
                out_ref[d, c * plan.rows : (c + 1) * plan.rows, :] = filled[
                    at : at + plan.rows, c * LANES : (c + 1) * LANES
                ]
            extra = jnp.zeros((EXTRA, LANES), F32)
            for g in range(plan.rows // EXTRA):
                extra = jnp.where(want[g], weights[at + g * EXTRA : at + (g + 1) * EXTRA, :], extra)
            out_ref[d, plan.slabs * plan.rows :, :] = extra.astype(BF16)
        span = pl.ds(p * each, each)
        leaving.append(pltpu.make_async_copy(out_ref.at[span], out_hbm.at[span], sems.at[3 + p]))
        leaving[-1].start()
    for copy in leaving:
        copy.wait()


def leaf_kernel(place_ref, branching_ref, weight_ref, rows_ref, block_ref, own_ref, send_ref, total):
    n = pl.program_id(0)
    share = own_ref.shape[1]
    peers = send_ref.shape[0]
    blk = place_ref[0]
    columns = jnp.transpose(weight_ref[0].astype(F32))
    total[...] = jnp.zeros_like(total)
    for b in range(rows_ref.shape[1]):

        @pl.when(b < branching_ref[n])
        def _():
            rows = rows_ref[0, b]
            scaled = (rows.astype(F32) * columns[:, b : b + 1]).astype(BF16)
            total[...] += dot_t(scaled, rows)

    own_ref[0] = total[pl.ds(pl.multiple_of(blk * share, share), share), :] + block_ref[0].astype(F32)
    for e in range(1, peers + 1):
        at = pl.multiple_of((blk ^ e) * share, share)
        send_ref[e - 1, 0] = total[pl.ds(at, share), :]


class Product:
    def __init__(self, scaled_ref, plain_ref, total):
        self.scaled_ref, self.plain_ref, self.total = scaled_ref, plain_ref, total
        if total is not None:
            total[...] = dot_t(scaled_ref[...], plain_ref[...])

    def rows(self, at, share):
        if self.total is not None:
            return self.total[pl.ds(at, share), :]
        return dot_t(self.scaled_ref[:, pl.ds(at, share)], self.plain_ref[...])


def gather_rows(plan, got_ref, plain_ref, scaled_ref):
    for d in range(plan.leaf_count):
        extra = got_ref[d, plan.slabs * plan.rows :, :].astype(F32)
        for g in range(plan.groups):
            rows = jnp.concatenate(
                [
                    got_ref[d, c * plan.rows + g * GROUP : c * plan.rows + (g + 1) * GROUP, :]
                    for c in range(plan.slabs)
                ],
                axis=1,
            )
            wide = rows.astype(F32)
            for q in range(plan.node_dev):
                if g not in plan.groups_of[q]:
                    continue
                at = (plan.groups_of[q].index(g) * plan.leaf_count + d) * GROUP
                first = g * GROUP // EXTRA * plan.node_dev + q
                places = range(first, first + GROUP // EXTRA * plan.node_dev, plan.node_dev)
                weight = jnp.concatenate([extra[:, j : j + 1] for j in places], axis=0)
                plain_ref[q, at : at + GROUP, :] = rows
                scaled_ref[q, at : at + GROUP, :] = (wide * weight).astype(BF16)


def scale_of(most):
    power = jnp.ceil(8.0 * jnp.log2(jnp.maximum(most, 1e-30)))
    return power, CODE * jnp.exp2(-0.125 * power)


def to_code(value):
    return jnp.round(value).astype(I32).astype(jnp.int16)


def from_code(code):
    return code.astype(I32).astype(F32)


def diagonal(width):
    return lax.broadcasted_iota(I32, (width, width), 0) == lax.broadcasted_iota(I32, (width, width), 1)


def as_line(column):
    return jnp.sum(jnp.where(diagonal(column.shape[0]), column, 0.0), axis=0, keepdims=True)


def as_column(line):
    return jnp.sum(jnp.where(diagonal(line.shape[1]), line, 0.0), axis=1, keepdims=True)


def send_plain(plan, place_ref, got_ref, part_ref, code_ref, plain_ref, scaled_ref, total=None):
    blk = place_ref[0]
    peers, nodes, share, state = part_ref.shape
    gather_rows(plan, got_ref, plain_ref, scaled_ref)
    for q in range(nodes):
        filled = pl.ds(0, plan.depth[q])
        product = Product(scaled_ref.at[q, filled], plain_ref.at[q, filled], total)
        for e in range(1, peers + 1):
            at = pl.multiple_of((blk ^ e) * share, share)
            value = part_ref[e - 1, q] + product.rows(at, share)
            power, factor = scale_of(jnp.max(jnp.abs(value), axis=1, keepdims=True))
            code_ref[e - 1, q * share : (q + 1) * share, :] = to_code(value * factor)
            line = jnp.concatenate([as_line(power), jnp.zeros((1, state - share), F32)], axis=1)
            base = nodes * share + q * GROUP
            code_ref[e - 1, base : base + GROUP, :] = to_code(jnp.broadcast_to(line, (GROUP, state)))


def decode_plain(code_ref, nodes, share):
    values = []
    for q in range(nodes):
        base = nodes * share + q * GROUP
        value = None
        for e in range(code_ref.shape[0]):
            power = as_column(from_code(code_ref[e, base : base + GROUP, :])[0:1, :share])
            term = from_code(code_ref[e, q * share : (q + 1) * share, :]) * (
                jnp.exp2(0.125 * power) * (1.0 / CODE)
            )
            value = term if value is None else value + term
        values.append(value)
    return values


def encode_node(code_ref, square, beside):
    half = code_ref.shape[1]
    upper, lower = square[:half, :half], square[half:, half:]
    pieces = [square[:half, half:]]
    pieces += [beside[r : r + half, c : c + half] for r in (0, half) for c in (0, half)]
    most = jnp.maximum(jnp.abs(upper), jnp.abs(lower))
    for piece in pieces:
        most = jnp.maximum(most, jnp.abs(piece))
    power, factor = scale_of(jnp.max(most, axis=1, keepdims=True))
    row = lax.broadcasted_iota(I32, (half, half), 0)
    column = lax.broadcasted_iota(I32, (half, half), 1)
    lower = lower * factor
    code_ref[:half, :] = to_code(jnp.where(column >= row, upper * factor, lower))
    for k, piece in enumerate(pieces):
        code_ref[(k + 1) * half : (k + 2) * half, :] = to_code(piece * factor)
    corner = jnp.sum(jnp.where(column == row, jnp.round(lower), 0.0), axis=0, keepdims=True)
    line = lax.broadcasted_iota(I32, (GROUP, half), 0)
    code_ref[6 * half :, :] = to_code(
        jnp.where(line == 0, as_line(power), jnp.where(line == 1, corner, 0.0))
    )


def decode_node(code_ref):
    half = code_ref.shape[1]
    lines = from_code(code_ref[6 * half :, :])
    line = jnp.exp2(0.125 * jnp.broadcast_to(lines[0:1, :], (half, half))) * (1.0 / CODE)
    step = jnp.transpose(line)
    raw = [from_code(code_ref[k * half : (k + 1) * half, :]) for k in range(6)]
    turned, mirror = (jnp.transpose(r) * line for r in raw[:2])
    pieces = [r * step for r in raw]
    both = pieces[0]
    row = lax.broadcasted_iota(I32, (half, half), 0)
    column = lax.broadcasted_iota(I32, (half, half), 1)
    upper = jnp.where(column >= row, both, turned)
    lower = jnp.where(column < row, both, jnp.where(column == row, lines[1:2, :] * line, turned))
    square = ((upper, pieces[1]), (mirror, lower))
    beside = ((pieces[2], pieces[3]), (pieces[4], pieces[5]))
    return square, beside


def halves(place, share):
    mine = pl.ds(pl.multiple_of(place * share, share), share)
    theirs = pl.ds(pl.multiple_of((1 - place) * share, share), share)
    return mine, theirs


def leaf_sum(node, branching_ref, weight_hbm, rows_hbm, weight_ref, rows_ref, total, sems):
    pairs = rows_hbm.shape[1] // 2
    depth, state = rows_hbm.shape[2:]
    count = branching_ref[node]
    weights = pltpu.make_async_copy(weight_hbm.at[node], weight_ref, sems.at[pairs])
    copies = [
        pltpu.make_async_copy(rows_hbm.at[node, pl.ds(2 * p, 2)], rows_ref.at[p], sems.at[p])
        for p in range(pairs)
    ]
    copies[0].start()
    weights.start()
    for p in range(1, pairs):
        pl.when(2 * p < count)(copies[p].start)
    weights.wait()
    live = lax.broadcasted_iota(I32, weight_ref.shape, 0) < count
    columns = jnp.transpose(jnp.where(live, weight_ref[...].astype(F32), 0.0))

    def term(p):
        copies[p].wait()
        rows = rows_ref[p].reshape(2 * depth, state)
        weight = jnp.concatenate([columns[:, 2 * p : 2 * p + 1], columns[:, 2 * p + 1 : 2 * p + 2]], axis=0)
        return dot_t((rows.astype(F32) * weight).astype(BF16), rows)

    total[...] = term(0)
    for p in range(1, pairs):

        @pl.when(2 * p < count)
        def _():
            total[...] += term(p)


def far_leaf_kernel(
    branching_ref, weight_hbm, rows_hbm, own_ref, code_ref, weight_ref, rows_ref, total, sems
):
    share = own_ref.shape[0]
    mine, theirs = halves(lax.axis_index("blk"), share)
    node = 1 - lax.axis_index("blk")
    leaf_sum(node, branching_ref, weight_hbm, rows_hbm, weight_ref, rows_ref, total, sems)
    encode_node(code_ref, total[theirs, theirs], total[theirs, mine])
    own_ref[...] = total[mine, :]


def near_leaf_kernel(
    branching_ref, weight_hbm, rows_hbm, block_ref, far_ref,
    own_ref, send_ref, far_out, weight_ref, rows_ref, total, sems,
):
    share = own_ref.shape[0]
    mine, theirs = halves(lax.axis_index("blk"), share)
    node = lax.axis_index("blk")
    leaf_sum(node, branching_ref, weight_hbm, rows_hbm, weight_ref, rows_ref, total, sems)
    send_ref[...] = total[theirs, :]
    own_ref[...] = total[mine, :] + block_ref[node].astype(F32)
    far_out[...] = far_ref[...] + block_ref[1 - node].astype(F32)


def weighted(plan, got_ref, plain_ref, columns, scaled_ref):
    cap = plan.rows
    for d in range(0, plan.leaf_count, 2):
        extras = [got_ref[d + i, plan.slabs * cap :, :].astype(F32) for i in range(2)]
        weight = jnp.concatenate([e[:, g : g + 1] for e in extras for g in range(cap // EXTRA)], axis=0)
        weight = jnp.broadcast_to(weight, (2 * cap, scaled_ref.shape[1])).astype(BF16)
        rows = slice(d * cap, (d + 2) * cap)
        scaled_ref[rows, :] = plain_ref[rows, columns] * weight


def send_folded(plan, got_ref, part_ref, code_ref, plain_ref, scaled_ref):
    share = part_ref.shape[0]
    mine, theirs = halves(lax.axis_index("blk"), share)
    cap = plan.rows
    for d in range(0, plan.leaf_count, 2):
        for c in range(plan.slabs):
            plain_ref[d * cap : (d + 2) * cap, c * LANES : (c + 1) * LANES] = jnp.concatenate(
                [got_ref[d + i, c * cap : (c + 1) * cap, :] for i in range(2)], axis=0
            )
    weighted(plan, got_ref, plain_ref, theirs, scaled_ref)
    scaled = scaled_ref[...]
    encode_node(
        code_ref,
        part_ref[:, theirs] + dot_t(scaled, plain_ref[:, theirs]),
        part_ref[:, mine] + dot_t(scaled, plain_ref[:, mine]),
    )


def in_columns(place, square, beside):
    first = place == 0
    return [
        [jnp.where(first, s, b) for s, b in zip(*pair)] + [jnp.where(first, b, s) for s, b in zip(*pair)]
        for pair in zip(square, beside)
    ]


def tiles_of(ref):
    half = ref.shape[0] // 2
    for i in range(2):
        for k in range(ref.shape[1] // half):
            yield i, k, slice(i * half, (i + 1) * half), slice(k * half, (k + 1) * half)


def near_node_kernel(plan, own_ref, got_ref, plain_ref, code_ref, node_ref, scaled_ref):
    mine, _ = halves(lax.axis_index("blk"), own_ref.shape[0])
    weighted(plan, got_ref, plain_ref, mine, scaled_ref)
    node_ref[...] = own_ref[...] + dot_t(scaled_ref[...], plain_ref[...])
    terms = in_columns(lax.axis_index("blk"), *decode_node(code_ref))
    for i, k, rows, columns in tiles_of(node_ref):
        node_ref[rows, columns] += terms[i][k]


def far_node_kernel(near_ref, own_ref, code_ref, node_ref, out_ref):
    first = lax.axis_index("blk") == 0
    terms = in_columns(lax.axis_index("blk"), *decode_node(code_ref))
    for i, k, rows, columns in tiles_of(node_ref):
        far = own_ref[rows, columns] + terms[i][k]
        near = near_ref[rows, columns]
        node_ref[rows, columns] = far
        out_ref[rows, 0, columns] = jnp.where(first, near, far)
        out_ref[rows, 1, columns] = jnp.where(first, far, near)


def merge_folded(
    sibling_ref, near_ref, far_ref, node_ref, their_near_ref, their_own_ref, code_ref,
    node_hbm, out_hbm, out_ref, sems,
):
    share = far_ref.shape[0]
    half = share // 2
    each = share // PIECES
    copies = [pltpu.make_async_copy(node_ref, node_hbm, sems.at[PIECES])]
    copies[0].start()
    first = lax.axis_index("blk") == 0
    straight = jnp.broadcast_to(sibling_ref[0:1, 0:1], (each, LANES)) == 0
    terms = in_columns(lax.axis_index("blk"), *decode_node(code_ref))
    for p in range(PIECES):
        rows = slice(p * each, (p + 1) * each)
        inner = slice(p * each % half, p * each % half + each)
        for k in range(far_ref.shape[1] // half):
            columns = slice(k * half, (k + 1) * half)
            their_near = their_near_ref[rows, columns]
            their_far = their_own_ref[rows, columns] + terms[p * each // half][k][inner]
            near = near_ref[rows, columns] + jnp.where(straight, their_near, their_far)
            far = far_ref[rows, columns] + jnp.where(straight, their_far, their_near)
            out_ref[rows, 0, columns] = jnp.where(first, near, far)
            out_ref[rows, 1, columns] = jnp.where(first, far, near)
        span = pl.ds(p * each, each)
        copies.append(pltpu.make_async_copy(out_ref.at[span], out_hbm.at[span], sems.at[p]))
        copies[-1].start()
    for copy in copies:
        copy.wait()


def own_kernel(plan, place_ref, part_ref, plain_ref, scaled_ref, own_ref, total=None):
    nodes, share, _ = part_ref.shape
    at = pl.multiple_of(place_ref[0] * share, share)
    for q in range(nodes):
        filled = pl.ds(0, plan.depth[q])
        product = Product(scaled_ref.at[q, filled], plain_ref.at[q, filled], total)
        own_ref[q] = part_ref[q] + product.rows(at, share)


def node_kernel(own_ref, code_ref, out_ref, node_ref):
    nodes, share, _ = own_ref.shape
    arrived = decode_plain(code_ref, nodes, share)
    for q in range(nodes):
        value = own_ref[q] + arrived[q]
        node_ref[q] = value
        out_ref[:, q, :] = value


def merge_kernel(sibling_ref, node_ref, own_ref, code_ref, out_ref, partner_ref):
    nodes, share, _ = own_ref.shape
    arrived = decode_plain(code_ref, nodes, share)
    for q in range(nodes):
        partner_ref[q] = own_ref[q] + arrived[q]
    for q in range(nodes):
        out_ref[:, q, :] = node_ref[q] + partner_ref[sibling_ref[0, q]]


def call(kernel, out_shape, in_specs, flops=0, moved=1 << 20, vmem=32 << 20, **more):
    outs = jax.tree.map(lambda _: VMEM, out_shape)
    more.setdefault("out_specs", outs)
    return pl.pallas_call(
        kernel,
        out_shape=out_shape,
        in_specs=in_specs,
        compiler_params=pltpu.CompilerParams(vmem_limit_bytes=vmem),
        cost_estimate=pl.CostEstimate(flops=flops, bytes_accessed=moved, transcendentals=0),
        **more,
    )


def exchange_plain(plan, place, got, own_part, send_part, sibling, blk_count):
    peers, node_dev, share, state = send_part.shape
    shape = jax.ShapeDtypeStruct
    whole = [pltpu.VMEM((state, state), F32)] if share % LANES else []
    depth = max(plan.depth)
    to_partner = [(i, i ^ 1) for i in range(plan.leaf_count)]
    with jax.named_scope("routed_send"):
        code, plain, scaled = call(
            functools.partial(send_plain, plan),
            (
                shape((peers, node_dev * (share + GROUP), state), jnp.int16),
                shape((node_dev, depth, state), BF16),
                shape((node_dev, depth, state), BF16),
            ),
            [SMEM, VMEM, VMEM],
            scratch_shapes=whole,
            flops=2 * node_dev * depth * state * state,
        )(place, got, send_part)
    arrived = jnp.stack(
        [
            lax.ppermute(code[e - 1], "blk", [(i, i ^ e) for i in range(blk_count)])
            for e in range(1, blk_count)
        ]
    )
    with jax.named_scope("routed_own"):
        own = call(
            functools.partial(own_kernel, plan),
            shape((node_dev, share, state), F32),
            [SMEM, VMEM, VMEM, VMEM],
            scratch_shapes=whole,
            flops=2 * node_dev * depth * share * state,
        )(place, own_part, plain, scaled)
    partner_own = lax.ppermute(own, "leaf", to_partner)
    partner_arrived = lax.ppermute(arrived, "leaf", to_partner)
    with jax.named_scope("node"):
        node_schur, node = call(
            node_kernel,
            (shape((share, node_dev, state), F32), shape((node_dev, share, state), F32)),
            [VMEM, VMEM],
        )(own, arrived)
    with jax.named_scope("merge"):
        merged = call(
            merge_kernel,
            shape((share, node_dev, state), F32),
            [SMEM, VMEM, VMEM, VMEM],
            scratch_shapes=[pltpu.VMEM((node_dev, share, state), F32)],
        )(sibling, node, partner_own, partner_arrived)
    return node_schur, merged


def bucket(plan, na_route, na_weight, na_rows):
    count, state = na_rows.shape
    any_spec = pl.BlockSpec(memory_space=pl.ANY)
    with jax.named_scope("bucket"):
        return call(
            functools.partial(bucket_kernel, plan),
            jax.ShapeDtypeStruct((plan.leaf_count, plan.block, LANES), BF16),
            [any_spec, any_spec, any_spec],
            scratch_shapes=[
                pltpu.VMEM((1, count), I32),
                pltpu.VMEM((count,), BF16),
                pltpu.VMEM((count, state), BF16),
                pltpu.VMEM((plan.leaf_count, plan.block, LANES), BF16),
                pltpu.SemaphoreType.DMA((3 + PIECES,)),
            ],
            out_specs=any_spec,
            vmem=60 << 20,
            flops=2 * plan.leaf_count * plan.rows * count * state,
        )(na_route.reshape(1, count), na_weight, na_rows)


def shards_plain(leaf_rows, leaf_weight, branching, sibling, node_block, na_rows, na_weight, na_route):
    leaf_count, blk_count = lax.axis_size("leaf"), lax.axis_size("blk")
    node_dev, most_children, depth, state = leaf_rows.shape
    count = na_rows.shape[0]
    share = state // blk_count
    peers = blk_count - 1
    plan = Plan(leaf_count, node_dev, 3 * count // (2 * leaf_count * node_dev), state, GROUP)
    place = lax.axis_index("blk").astype(I32).reshape(1)
    shape = jax.ShapeDtypeStruct
    blocks = bucket(plan, na_route, na_weight, na_rows)
    got = lax.all_to_all(blocks, "leaf", split_axis=0, concat_axis=0, tiled=True)
    with jax.named_scope("leaf_products"):
        own_part, send_part = call(
            leaf_kernel,
            (shape((node_dev, share, state), F32), shape((peers, node_dev, share, state), F32)),
            [
                SMEM,
                SMEM,
                pl.BlockSpec((1, most_children, depth), lambda n: (n, 0, 0)),
                pl.BlockSpec((1, most_children, depth, state), lambda n: (n, 0, 0, 0)),
                pl.BlockSpec((1, share, state), lambda n: (n, 0, 0)),
            ],
            out_specs=(
                pl.BlockSpec((1, share, state), lambda n: (n, 0, 0)),
                pl.BlockSpec((peers, 1, share, state), lambda n: (0, n, 0, 0)),
            ),
            grid=(node_dev,),
            scratch_shapes=[pltpu.VMEM((state, state), F32)],
            flops=2 * node_dev * most_children * depth * state * state,
            moved=8 << 20,
        )(place, branching, leaf_weight, leaf_rows, jnp.transpose(node_block, (1, 0, 2)))
    return exchange_plain(plan, place, got, own_part, send_part, sibling, blk_count)


def shards_folded(leaf_rows, leaf_weight, branching, sibling, node_block, na_rows, na_weight, na_route):
    leaf_count = lax.axis_size(SPLIT)
    node_dev, most_children, depth, state = leaf_rows.shape
    count = na_rows.shape[0]
    share = state // 2
    half = share // 2
    nodes = leaf_count * node_dev
    plan = Plan(nodes, 1, 3 * count // (2 * nodes), state, EXTRA, ORDER)
    shape = jax.ShapeDtypeStruct
    any_spec = pl.BlockSpec(memory_space=pl.ANY)
    across = [(0, 1), (1, 0)]
    to_partner = [(i, i ^ 1) for i in range(leaf_count)]
    result = shape((share, node_dev, state), F32)
    rows = shape((share, state), F32)
    codes = shape((6 * half + GROUP, half), jnp.int16)
    gathered = shape((nodes * plan.rows, state), BF16)

    blocks = bucket(plan, na_route, na_weight, na_rows)
    got = lax.all_to_all(blocks, ORDER, split_axis=0, concat_axis=0, tiled=True)

    own_block = jnp.transpose(node_block, (1, 0, 2))
    leaf = dict(
        scratch_shapes=[
            pltpu.VMEM((most_children, depth), BF16),
            pltpu.VMEM((most_children // 2, 2, depth, state), BF16),
            pltpu.VMEM((state, state), F32),
            pltpu.SemaphoreType.DMA((most_children // 2 + 1,)),
        ],
        flops=1,
        moved=1,
        vmem=24 << 20,
    )
    with jax.named_scope("far_leaf_products"):
        far_own, far_code = call(
            far_leaf_kernel, (rows, codes), [SMEM, any_spec, any_spec], **leaf
        )(branching, leaf_weight, leaf_rows)
    near_code = lax.ppermute(far_code, "blk", across)
    with jax.named_scope("near_leaf_products"):
        near_own, send_part, far_own = call(
            near_leaf_kernel, (rows, rows, rows), [SMEM, any_spec, any_spec, VMEM, VMEM], **leaf
        )(branching, leaf_weight, leaf_rows, own_block, far_own)
    their_own = lax.ppermute(far_own, SPLIT, to_partner)
    half_scaled = pltpu.VMEM((nodes * plan.rows, share), BF16)
    with jax.named_scope("routed_send"):
        code, plain = call(
            functools.partial(send_folded, plan),
            (codes, gathered),
            [VMEM, VMEM],
            scratch_shapes=[half_scaled],
            flops=2 * nodes * plan.rows * share * state,
        )(got, send_part)
    arrived = lax.ppermute(code, "blk", across)
    with jax.named_scope("near_node"):
        near = call(
            functools.partial(near_node_kernel, plan),
            rows,
            [VMEM] * 4,
            scratch_shapes=[half_scaled],
            flops=LONG,
        )(near_own, got, plain, near_code)
    their_near = lax.ppermute(near, SPLIT, to_partner)
    their_arrived = lax.ppermute(arrived, SPLIT, to_partner)
    with jax.named_scope("far_node"):
        far, node = call(far_node_kernel, (rows, result), [VMEM, VMEM, VMEM], flops=LONG)(
            near, far_own, arrived
        )
    with jax.named_scope("merge"):
        return call(
            merge_folded,
            (result, result),
            [VMEM] * 7,
            out_specs=(any_spec, any_spec),
            scratch_shapes=[
                pltpu.VMEM((share, node_dev, state), F32),
                pltpu.SemaphoreType.DMA((PIECES + 1,)),
            ],
        )(sibling, near, far, node, their_near, their_own, their_arrived)


def solution(mesh):
    leaf_count, blk_count = mesh.shape["leaf"], mesh.shape["blk"]
    plain = jax.shard_map(
        shards_plain, mesh=mesh, in_specs=in_specs("leaf"), out_specs=out_specs("leaf"), check_vma=False
    )
    if blk_count != 2 or leaf_count != 2 ** len(SPLIT):
        return plain
    split = jax.sharding.Mesh(mesh.devices.reshape((2,) * len(ORDER)), (*SPLIT, "blk"))
    folded = jax.shard_map(
        shards_folded, mesh=split, in_specs=in_specs(SPLIT), out_specs=out_specs(SPLIT), check_vma=False
    )

    def choose(leaf_rows, *more):
        nodes, children, _, state = leaf_rows.shape
        fits = nodes == 2 * leaf_count and children % 2 == 0 and state == 4 * LANES
        return (folded if fits else plain)(leaf_rows, *more)

    return choose


def in_specs(leaf):
    every = ((leaf,) if isinstance(leaf, str) else leaf) + ("blk",)
    return (
        P(leaf, None, "blk", None),
        P(leaf, None, "blk"),
        P(leaf),
        P(leaf, None),
        P("blk", leaf, None),
        P(every, None),
        P(every),
        P(every, None),
    )


def out_specs(leaf):
    return (P("blk", leaf, None), P("blk", leaf, None))
```

```python
import functools

import jax
import jax.numpy as jnp
from jax import lax
from jax.experimental import pallas as pl
from jax.experimental.pallas import tpu as pltpu
from jax.sharding import PartitionSpec as P

F32 = jnp.float32
BF16 = jnp.bfloat16
I32 = jnp.int32
LANES = 128
GROUP = 16
EXTRA = 8
PIECES = 4
VMEM = pl.BlockSpec(memory_space=pltpu.VMEM)
SMEM = pl.BlockSpec(memory_space=pltpu.SMEM)
CODE = 32000.0
SPLIT = ("z1", "z0", "y", "core")
ORDER = ("blk", "y", "z1", "core", "z0")
LONG = 20_000_000_000


class Plan:
    def __init__(self, leaf_count, node_dev, capacity, state, unit, order=()):
        self.order = order
        self.leaf_count, self.node_dev, self.capacity, self.state = leaf_count, node_dev, capacity, state
        self.full = capacity // GROUP * GROUP
        self.rest = capacity - self.full
        self.rows = -(-node_dev * capacity // unit) * unit
        self.groups = self.rows // GROUP
        self.slabs = state // LANES
        self.block = self.slabs * self.rows + EXTRA
        self.groups_of = [
            [g for g in range(self.groups) if q in {self.node_at(g * GROUP + i) for i in range(GROUP)}]
            for q in range(node_dev)
        ]
        self.depth = [leaf_count * GROUP * len(g) for g in self.groups_of]

    def block_of(self, node):
        if not self.order:
            return node
        block = jnp.zeros_like(node)
        for name in self.order:
            block = 2 * block + (node >> (len(SPLIT) - (*SPLIT, "blk").index(name)) & 1)
        return block

    def node_at(self, row):
        if row < self.node_dev * self.full:
            return row // self.full
        return min((row - self.node_dev * self.full) // self.rest, self.node_dev - 1) if self.rest else 0


def dot_t(a, b):
    return lax.dot_general(a, b, (((0,), (0,)), ((), ())), preferred_element_type=F32)


def bucket_kernel(plan, route_hbm, weight_hbm, rows_hbm, out_hbm, route_ref, weight_ref, rows_ref, out_ref, sems):
    count = rows_hbm.shape[0]
    copies = [
        pltpu.make_async_copy(route_hbm, route_ref, sems.at[0]),
        pltpu.make_async_copy(weight_hbm, weight_ref, sems.at[1]),
        pltpu.make_async_copy(rows_hbm, rows_ref, sems.at[2]),
    ]
    for copy in copies:
        copy.start()
    nodes = plan.leaf_count * plan.node_dev
    before = (
        lax.broadcasted_iota(I32, (count, count), 0) < lax.broadcasted_iota(I32, (count, count), 1)
    ).astype(BF16)
    copies[0].wait()
    route = route_ref[...]
    member = lax.broadcasted_iota(I32, (nodes, count), 0) == route
    seen = jnp.dot(member.astype(BF16), before, preferred_element_type=F32)
    position = jnp.sum(jnp.where(member, seen, 0.0), axis=0, keepdims=True).astype(I32)
    route = plan.block_of(route)
    owner = route // plan.node_dev
    q = route - owner * plan.node_dev
    slot = owner * plan.rows + jnp.where(
        position < plan.full,
        q * plan.full + position,
        plan.node_dev * plan.full + q * plan.rest + position - plan.full,
    )
    copies[1].wait()
    weight = weight_ref[...].reshape(1, count).astype(F32)
    lane = lax.broadcasted_iota(I32, (EXTRA, LANES), 1)
    sub = lax.broadcasted_iota(I32, (EXTRA, LANES), 0)
    want = []
    for g in range(plan.rows // EXTRA):
        q_of = jnp.full((EXTRA, LANES), plan.node_at(g * EXTRA), I32)
        for i in range(1, EXTRA):
            step = plan.node_at(g * EXTRA + i) - plan.node_at(g * EXTRA + i - 1)
            if step:
                q_of = q_of + jnp.where(sub >= i, step, 0)
        want.append(lane == g * plan.node_dev + q_of)
    copies[2].wait()
    each = plan.leaf_count // PIECES
    leaving = []
    for p in range(PIECES):
        place = lax.broadcasted_iota(I32, (each * plan.rows, count), 0) + p * each * plan.rows
        hit = jnp.where(place == slot, 1.0, 0.0).astype(BF16)
        weights = jnp.sum(jnp.where(place == slot, weight, 0.0), axis=1, keepdims=True) + jnp.zeros((1, LANES), F32)
        filled = jnp.dot(hit, rows_ref[...], preferred_element_type=F32).astype(BF16)
        for i in range(each):
            at = i * plan.rows
            d = p * each + i
            for c in range(plan.slabs):
                out_ref[d, c * plan.rows : (c + 1) * plan.rows, :] = filled[
                    at : at + plan.rows, c * LANES : (c + 1) * LANES
                ]
            extra = jnp.zeros((EXTRA, LANES), F32)
            for g in range(plan.rows // EXTRA):
                extra = jnp.where(want[g], weights[at + g * EXTRA : at + (g + 1) * EXTRA, :], extra)
            out_ref[d, plan.slabs * plan.rows :, :] = extra.astype(BF16)
        span = pl.ds(p * each, each)
        leaving.append(pltpu.make_async_copy(out_ref.at[span], out_hbm.at[span], sems.at[3 + p]))
        leaving[-1].start()
    for copy in leaving:
        copy.wait()


def leaf_kernel(place_ref, branching_ref, weight_ref, rows_ref, block_ref, own_ref, send_ref, total):
    n = pl.program_id(0)
    share = own_ref.shape[1]
    peers = send_ref.shape[0]
    blk = place_ref[0]
    columns = jnp.transpose(weight_ref[0].astype(F32))
    total[...] = jnp.zeros_like(total)
    for b in range(rows_ref.shape[1]):

        @pl.when(b < branching_ref[n])
        def _():
            rows = rows_ref[0, b]
            scaled = (rows.astype(F32) * columns[:, b : b + 1]).astype(BF16)
            total[...] += dot_t(scaled, rows)

    own_ref[0] = total[pl.ds(pl.multiple_of(blk * share, share), share), :] + block_ref[0].astype(F32)
    for e in range(1, peers + 1):
        at = pl.multiple_of((blk ^ e) * share, share)
        send_ref[e - 1, 0] = total[pl.ds(at, share), :]


class Product:
    def __init__(self, scaled_ref, plain_ref, total):
        self.scaled_ref, self.plain_ref, self.total = scaled_ref, plain_ref, total
        if total is not None:
            total[...] = dot_t(scaled_ref[...], plain_ref[...])

    def rows(self, at, share):
        if self.total is not None:
            return self.total[pl.ds(at, share), :]
        return dot_t(self.scaled_ref[:, pl.ds(at, share)], self.plain_ref[...])


def gather_rows(plan, got_ref, plain_ref, scaled_ref):
    for d in range(plan.leaf_count):
        extra = got_ref[d, plan.slabs * plan.rows :, :].astype(F32)
        for g in range(plan.groups):
            rows = jnp.concatenate(
                [
                    got_ref[d, c * plan.rows + g * GROUP : c * plan.rows + (g + 1) * GROUP, :]
                    for c in range(plan.slabs)
                ],
                axis=1,
            )
            wide = rows.astype(F32)
            for q in range(plan.node_dev):
                if g not in plan.groups_of[q]:
                    continue
                at = (plan.groups_of[q].index(g) * plan.leaf_count + d) * GROUP
                first = g * GROUP // EXTRA * plan.node_dev + q
                places = range(first, first + GROUP // EXTRA * plan.node_dev, plan.node_dev)
                weight = jnp.concatenate([extra[:, j : j + 1] for j in places], axis=0)
                plain_ref[q, at : at + GROUP, :] = rows
                scaled_ref[q, at : at + GROUP, :] = (wide * weight).astype(BF16)


def scale_of(most):
    power = jnp.ceil(8.0 * jnp.log2(jnp.maximum(most, 1e-30)))
    return power, CODE * jnp.exp2(-0.125 * power)


def to_code(value):
    return jnp.round(value).astype(I32).astype(jnp.int16)


def from_code(code):
    return code.astype(I32).astype(F32)


def diagonal(width):
    return lax.broadcasted_iota(I32, (width, width), 0) == lax.broadcasted_iota(I32, (width, width), 1)


def as_line(column):
    return jnp.sum(jnp.where(diagonal(column.shape[0]), column, 0.0), axis=0, keepdims=True)


def as_column(line):
    return jnp.sum(jnp.where(diagonal(line.shape[1]), line, 0.0), axis=1, keepdims=True)


def send_plain(plan, place_ref, got_ref, part_ref, code_ref, plain_ref, scaled_ref, total=None):
    blk = place_ref[0]
    peers, nodes, share, state = part_ref.shape
    gather_rows(plan, got_ref, plain_ref, scaled_ref)
    for q in range(nodes):
        filled = pl.ds(0, plan.depth[q])
        product = Product(scaled_ref.at[q, filled], plain_ref.at[q, filled], total)
        for e in range(1, peers + 1):
            at = pl.multiple_of((blk ^ e) * share, share)
            value = part_ref[e - 1, q] + product.rows(at, share)
            power, factor = scale_of(jnp.max(jnp.abs(value), axis=1, keepdims=True))
            code_ref[e - 1, q * share : (q + 1) * share, :] = to_code(value * factor)
            line = jnp.concatenate([as_line(power), jnp.zeros((1, state - share), F32)], axis=1)
            base = nodes * share + q * GROUP
            code_ref[e - 1, base : base + GROUP, :] = to_code(jnp.broadcast_to(line, (GROUP, state)))


def decode_plain(code_ref, nodes, share):
    values = []
    for q in range(nodes):
        base = nodes * share + q * GROUP
        value = None
        for e in range(code_ref.shape[0]):
            power = as_column(from_code(code_ref[e, base : base + GROUP, :])[0:1, :share])
            term = from_code(code_ref[e, q * share : (q + 1) * share, :]) * (
                jnp.exp2(0.125 * power) * (1.0 / CODE)
            )
            value = term if value is None else value + term
        values.append(value)
    return values


def encode_node(code_ref, square, beside):
    half = code_ref.shape[1]
    upper, lower = square[:half, :half], square[half:, half:]
    pieces = [square[:half, half:]]
    pieces += [beside[r : r + half, c : c + half] for r in (0, half) for c in (0, half)]
    most = jnp.maximum(jnp.abs(upper), jnp.abs(lower))
    for piece in pieces:
        most = jnp.maximum(most, jnp.abs(piece))
    power, factor = scale_of(jnp.max(most, axis=1, keepdims=True))
    row = lax.broadcasted_iota(I32, (half, half), 0)
    column = lax.broadcasted_iota(I32, (half, half), 1)
    lower = lower * factor
    code_ref[:half, :] = to_code(jnp.where(column >= row, upper * factor, lower))
    for k, piece in enumerate(pieces):
        code_ref[(k + 1) * half : (k + 2) * half, :] = to_code(piece * factor)
    corner = jnp.sum(jnp.where(column == row, jnp.round(lower), 0.0), axis=0, keepdims=True)
    line = lax.broadcasted_iota(I32, (GROUP, half), 0)
    code_ref[6 * half :, :] = to_code(
        jnp.where(line == 0, as_line(power), jnp.where(line == 1, corner, 0.0))
    )


def decode_node(code_ref):
    half = code_ref.shape[1]
    lines = from_code(code_ref[6 * half :, :])
    line = jnp.exp2(0.125 * jnp.broadcast_to(lines[0:1, :], (half, half))) * (1.0 / CODE)
    step = jnp.transpose(line)
    raw = [from_code(code_ref[k * half : (k + 1) * half, :]) for k in range(6)]
    turned, mirror = (jnp.transpose(r) * line for r in raw[:2])
    pieces = [r * step for r in raw]
    both = pieces[0]
    row = lax.broadcasted_iota(I32, (half, half), 0)
    column = lax.broadcasted_iota(I32, (half, half), 1)
    upper = jnp.where(column >= row, both, turned)
    lower = jnp.where(column < row, both, jnp.where(column == row, lines[1:2, :] * line, turned))
    square = ((upper, pieces[1]), (mirror, lower))
    beside = ((pieces[2], pieces[3]), (pieces[4], pieces[5]))
    return square, beside


def halves(place, share):
    mine = pl.ds(pl.multiple_of(place * share, share), share)
    theirs = pl.ds(pl.multiple_of((1 - place) * share, share), share)
    return mine, theirs


def leaf_sum(node, branching_ref, weight_hbm, rows_hbm, weight_ref, rows_ref, total, sems):
    pairs = rows_hbm.shape[1] // 2
    depth, state = rows_hbm.shape[2:]
    count = branching_ref[node]
    weights = pltpu.make_async_copy(weight_hbm.at[node], weight_ref, sems.at[pairs])
    copies = [
        pltpu.make_async_copy(rows_hbm.at[node, pl.ds(2 * p, 2)], rows_ref.at[p], sems.at[p])
        for p in range(pairs)
    ]
    copies[0].start()
    weights.start()
    for p in range(1, pairs):
        pl.when(2 * p < count)(copies[p].start)
    weights.wait()
    live = lax.broadcasted_iota(I32, weight_ref.shape, 0) < count
    columns = jnp.transpose(jnp.where(live, weight_ref[...].astype(F32), 0.0))

    def term(p):
        copies[p].wait()
        rows = rows_ref[p].reshape(2 * depth, state)
        weight = jnp.concatenate([columns[:, 2 * p : 2 * p + 1], columns[:, 2 * p + 1 : 2 * p + 2]], axis=0)
        return dot_t((rows.astype(F32) * weight).astype(BF16), rows)

    total[...] = term(0)
    for p in range(1, pairs):

        @pl.when(2 * p < count)
        def _():
            total[...] += term(p)


def far_leaf_kernel(
    branching_ref, weight_hbm, rows_hbm, own_ref, code_ref, weight_ref, rows_ref, total, sems
):
    share = own_ref.shape[0]
    mine, theirs = halves(lax.axis_index("blk"), share)
    node = 1 - lax.axis_index("blk")
    leaf_sum(node, branching_ref, weight_hbm, rows_hbm, weight_ref, rows_ref, total, sems)
    encode_node(code_ref, total[theirs, theirs], total[theirs, mine])
    own_ref[...] = total[mine, :]


def near_leaf_kernel(
    branching_ref, weight_hbm, rows_hbm, block_ref, far_ref,
    own_ref, send_ref, far_out, weight_ref, rows_ref, total, sems,
):
    share = own_ref.shape[0]
    mine, theirs = halves(lax.axis_index("blk"), share)
    node = lax.axis_index("blk")
    leaf_sum(node, branching_ref, weight_hbm, rows_hbm, weight_ref, rows_ref, total, sems)
    send_ref[...] = total[theirs, :]
    own_ref[...] = total[mine, :] + block_ref[node].astype(F32)
    far_out[...] = far_ref[...] + block_ref[1 - node].astype(F32)


def weighted(plan, got_ref, plain_ref, columns, scaled_ref):
    cap = plan.rows
    for d in range(0, plan.leaf_count, 2):
        extras = [got_ref[d + i, plan.slabs * cap :, :].astype(F32) for i in range(2)]
        weight = jnp.concatenate([e[:, g : g + 1] for e in extras for g in range(cap // EXTRA)], axis=0)
        weight = jnp.broadcast_to(weight, (2 * cap, scaled_ref.shape[1])).astype(BF16)
        rows = slice(d * cap, (d + 2) * cap)
        scaled_ref[rows, :] = plain_ref[rows, columns] * weight


def send_folded(plan, got_ref, part_ref, code_ref, plain_ref, scaled_ref):
    share = part_ref.shape[0]
    mine, theirs = halves(lax.axis_index("blk"), share)
    cap = plan.rows
    for d in range(0, plan.leaf_count, 2):
        for c in range(plan.slabs):
            plain_ref[d * cap : (d + 2) * cap, c * LANES : (c + 1) * LANES] = jnp.concatenate(
                [got_ref[d + i, c * cap : (c + 1) * cap, :] for i in range(2)], axis=0
            )
    weighted(plan, got_ref, plain_ref, theirs, scaled_ref)
    scaled = scaled_ref[...]
    encode_node(
        code_ref,
        part_ref[:, theirs] + dot_t(scaled, plain_ref[:, theirs]),
        part_ref[:, mine] + dot_t(scaled, plain_ref[:, mine]),
    )


def in_columns(place, square, beside):
    first = place == 0
    return [
        [jnp.where(first, s, b) for s, b in zip(*pair)] + [jnp.where(first, b, s) for s, b in zip(*pair)]
        for pair in zip(square, beside)
    ]


def tiles_of(ref):
    half = ref.shape[0] // 2
    for i in range(2):
        for k in range(ref.shape[1] // half):
            yield i, k, slice(i * half, (i + 1) * half), slice(k * half, (k + 1) * half)


def near_node_kernel(plan, own_ref, got_ref, plain_ref, code_ref, node_ref, scaled_ref):
    mine, _ = halves(lax.axis_index("blk"), own_ref.shape[0])
    weighted(plan, got_ref, plain_ref, mine, scaled_ref)
    node_ref[...] = own_ref[...] + dot_t(scaled_ref[...], plain_ref[...])
    terms = in_columns(lax.axis_index("blk"), *decode_node(code_ref))
    for i, k, rows, columns in tiles_of(node_ref):
        node_ref[rows, columns] += terms[i][k]


def far_node_kernel(near_ref, own_ref, code_ref, far_ref, out_ref):
    first = lax.axis_index("blk") == 0
    terms = in_columns(lax.axis_index("blk"), *decode_node(code_ref))
    for i, k, rows, columns in tiles_of(own_ref):
        far = own_ref[rows, columns] + terms[i][k]
        near = near_ref[rows, columns]
        far_ref[rows, columns] = far
        out_ref[rows, 0, columns] = jnp.where(first, near, far)
        out_ref[rows, 1, columns] = jnp.where(first, far, near)


def first_awaits(sibling_ref, count):
    straight = jnp.broadcast_to(sibling_ref[0:1, 0:1], (count, LANES)) == 0
    return straight != (lax.axis_index("blk") == 0)


def base_kernel(sibling_ref, near_ref, far_ref, their_near_ref, their_own_ref, base_ref):
    first = lax.axis_index("blk") == 0
    zero = first_awaits(sibling_ref, LANES)
    for _, _, rows, columns in tiles_of(their_own_ref):
        near, far = near_ref[rows, columns], far_ref[rows, columns]
        their_near, their_far = their_near_ref[rows, columns], their_own_ref[rows, columns]
        base_ref[0, rows, columns] = jnp.where(first, near, far) + jnp.where(zero, their_far, their_near)
        base_ref[1, rows, columns] = jnp.where(first, far, near) + jnp.where(zero, their_near, their_far)


def merge_folded(sibling_ref, node_ref, base_ref, code_ref, node_hbm, out_hbm, out_ref, sems):
    _, share, state = base_ref.shape
    half = share // 2
    each = share // PIECES
    copies = [pltpu.make_async_copy(node_ref, node_hbm, sems.at[PIECES])]
    copies[0].start()
    zero = first_awaits(sibling_ref, each)
    terms = in_columns(lax.axis_index("blk"), *decode_node(code_ref))
    for p in range(PIECES):
        rows = slice(p * each, (p + 1) * each)
        inner = slice(p * each % half, p * each % half + each)
        for k in range(state // half):
            columns = slice(k * half, (k + 1) * half)
            term = terms[p * each // half][k][inner]
            out_ref[rows, 0, columns] = base_ref[0, rows, columns] + jnp.where(zero, term, 0.0)
            out_ref[rows, 1, columns] = base_ref[1, rows, columns] + jnp.where(zero, 0.0, term)
        span = pl.ds(p * each, each)
        copies.append(pltpu.make_async_copy(out_ref.at[span], out_hbm.at[span], sems.at[p]))
        copies[-1].start()
    for copy in copies:
        copy.wait()


def own_kernel(plan, place_ref, part_ref, plain_ref, scaled_ref, own_ref, total=None):
    nodes, share, _ = part_ref.shape
    at = pl.multiple_of(place_ref[0] * share, share)
    for q in range(nodes):
        filled = pl.ds(0, plan.depth[q])
        product = Product(scaled_ref.at[q, filled], plain_ref.at[q, filled], total)
        own_ref[q] = part_ref[q] + product.rows(at, share)


def node_kernel(own_ref, code_ref, out_ref, node_ref):
    nodes, share, _ = own_ref.shape
    arrived = decode_plain(code_ref, nodes, share)
    for q in range(nodes):
        value = own_ref[q] + arrived[q]
        node_ref[q] = value
        out_ref[:, q, :] = value


def merge_kernel(sibling_ref, node_ref, own_ref, code_ref, out_ref, partner_ref):
    nodes, share, _ = own_ref.shape
    arrived = decode_plain(code_ref, nodes, share)
    for q in range(nodes):
        partner_ref[q] = own_ref[q] + arrived[q]
    for q in range(nodes):
        out_ref[:, q, :] = node_ref[q] + partner_ref[sibling_ref[0, q]]


def call(kernel, out_shape, in_specs, flops=0, moved=1 << 20, vmem=32 << 20, **more):
    outs = jax.tree.map(lambda _: VMEM, out_shape)
    more.setdefault("out_specs", outs)
    return pl.pallas_call(
        kernel,
        out_shape=out_shape,
        in_specs=in_specs,
        compiler_params=pltpu.CompilerParams(vmem_limit_bytes=vmem),
        cost_estimate=pl.CostEstimate(flops=flops, bytes_accessed=moved, transcendentals=0),
        **more,
    )


def exchange_plain(plan, place, got, own_part, send_part, sibling, blk_count):
    peers, node_dev, share, state = send_part.shape
    shape = jax.ShapeDtypeStruct
    whole = [pltpu.VMEM((state, state), F32)] if share % LANES else []
    depth = max(plan.depth)
    to_partner = [(i, i ^ 1) for i in range(plan.leaf_count)]
    with jax.named_scope("routed_send"):
        code, plain, scaled = call(
            functools.partial(send_plain, plan),
            (
                shape((peers, node_dev * (share + GROUP), state), jnp.int16),
                shape((node_dev, depth, state), BF16),
                shape((node_dev, depth, state), BF16),
            ),
            [SMEM, VMEM, VMEM],
            scratch_shapes=whole,
            flops=2 * node_dev * depth * state * state,
        )(place, got, send_part)
    arrived = jnp.stack(
        [
            lax.ppermute(code[e - 1], "blk", [(i, i ^ e) for i in range(blk_count)])
            for e in range(1, blk_count)
        ]
    )
    with jax.named_scope("routed_own"):
        own = call(
            functools.partial(own_kernel, plan),
            shape((node_dev, share, state), F32),
            [SMEM, VMEM, VMEM, VMEM],
            scratch_shapes=whole,
            flops=2 * node_dev * depth * share * state,
        )(place, own_part, plain, scaled)
    partner_own = lax.ppermute(own, "leaf", to_partner)
    partner_arrived = lax.ppermute(arrived, "leaf", to_partner)
    with jax.named_scope("node"):
        node_schur, node = call(
            node_kernel,
            (shape((share, node_dev, state), F32), shape((node_dev, share, state), F32)),
            [VMEM, VMEM],
        )(own, arrived)
    with jax.named_scope("merge"):
        merged = call(
            merge_kernel,
            shape((share, node_dev, state), F32),
            [SMEM, VMEM, VMEM, VMEM],
            scratch_shapes=[pltpu.VMEM((node_dev, share, state), F32)],
        )(sibling, node, partner_own, partner_arrived)
    return node_schur, merged


def bucket(plan, na_route, na_weight, na_rows):
    count, state = na_rows.shape
    any_spec = pl.BlockSpec(memory_space=pl.ANY)
    with jax.named_scope("bucket"):
        return call(
            functools.partial(bucket_kernel, plan),
            jax.ShapeDtypeStruct((plan.leaf_count, plan.block, LANES), BF16),
            [any_spec, any_spec, any_spec],
            scratch_shapes=[
                pltpu.VMEM((1, count), I32),
                pltpu.VMEM((count,), BF16),
                pltpu.VMEM((count, state), BF16),
                pltpu.VMEM((plan.leaf_count, plan.block, LANES), BF16),
                pltpu.SemaphoreType.DMA((3 + PIECES,)),
            ],
            out_specs=any_spec,
            vmem=60 << 20,
            flops=2 * plan.leaf_count * plan.rows * count * state,
        )(na_route.reshape(1, count), na_weight, na_rows)


def shards_plain(leaf_rows, leaf_weight, branching, sibling, node_block, na_rows, na_weight, na_route):
    leaf_count, blk_count = lax.axis_size("leaf"), lax.axis_size("blk")
    node_dev, most_children, depth, state = leaf_rows.shape
    count = na_rows.shape[0]
    share = state // blk_count
    peers = blk_count - 1
    plan = Plan(leaf_count, node_dev, 3 * count // (2 * leaf_count * node_dev), state, GROUP)
    place = lax.axis_index("blk").astype(I32).reshape(1)
    shape = jax.ShapeDtypeStruct
    blocks = bucket(plan, na_route, na_weight, na_rows)
    got = lax.all_to_all(blocks, "leaf", split_axis=0, concat_axis=0, tiled=True)
    with jax.named_scope("leaf_products"):
        own_part, send_part = call(
            leaf_kernel,
            (shape((node_dev, share, state), F32), shape((peers, node_dev, share, state), F32)),
            [
                SMEM,
                SMEM,
                pl.BlockSpec((1, most_children, depth), lambda n: (n, 0, 0)),
                pl.BlockSpec((1, most_children, depth, state), lambda n: (n, 0, 0, 0)),
                pl.BlockSpec((1, share, state), lambda n: (n, 0, 0)),
            ],
            out_specs=(
                pl.BlockSpec((1, share, state), lambda n: (n, 0, 0)),
                pl.BlockSpec((peers, 1, share, state), lambda n: (0, n, 0, 0)),
            ),
            grid=(node_dev,),
            scratch_shapes=[pltpu.VMEM((state, state), F32)],
            flops=2 * node_dev * most_children * depth * state * state,
            moved=8 << 20,
        )(place, branching, leaf_weight, leaf_rows, jnp.transpose(node_block, (1, 0, 2)))
    return exchange_plain(plan, place, got, own_part, send_part, sibling, blk_count)


def shards_folded(leaf_rows, leaf_weight, branching, sibling, node_block, na_rows, na_weight, na_route):
    leaf_count = lax.axis_size(SPLIT)
    node_dev, most_children, depth, state = leaf_rows.shape
    count = na_rows.shape[0]
    share = state // 2
    half = share // 2
    nodes = leaf_count * node_dev
    plan = Plan(nodes, 1, 3 * count // (2 * nodes), state, EXTRA, ORDER)
    shape = jax.ShapeDtypeStruct
    any_spec = pl.BlockSpec(memory_space=pl.ANY)
    across = [(0, 1), (1, 0)]
    to_partner = [(i, i ^ 1) for i in range(leaf_count)]
    result = shape((share, node_dev, state), F32)
    rows = shape((share, state), F32)
    codes = shape((6 * half + GROUP, half), jnp.int16)
    gathered = shape((nodes * plan.rows, state), BF16)

    blocks = bucket(plan, na_route, na_weight, na_rows)
    got = lax.all_to_all(blocks, ORDER, split_axis=0, concat_axis=0, tiled=True)

    own_block = jnp.transpose(node_block, (1, 0, 2))
    leaf = dict(
        scratch_shapes=[
            pltpu.VMEM((most_children, depth), BF16),
            pltpu.VMEM((most_children // 2, 2, depth, state), BF16),
            pltpu.VMEM((state, state), F32),
            pltpu.SemaphoreType.DMA((most_children // 2 + 1,)),
        ],
        flops=1,
        moved=1,
        vmem=24 << 20,
    )
    with jax.named_scope("far_leaf_products"):
        far_own, far_code = call(
            far_leaf_kernel, (rows, codes), [SMEM, any_spec, any_spec], **leaf
        )(branching, leaf_weight, leaf_rows)
    near_code = lax.ppermute(far_code, "blk", across)
    with jax.named_scope("near_leaf_products"):
        near_own, send_part, far_own = call(
            near_leaf_kernel, (rows, rows, rows), [SMEM, any_spec, any_spec, VMEM, VMEM], **leaf
        )(branching, leaf_weight, leaf_rows, own_block, far_own)
    their_own = lax.ppermute(far_own, SPLIT, to_partner)
    half_scaled = pltpu.VMEM((nodes * plan.rows, share), BF16)
    with jax.named_scope("routed_send"):
        code, plain = call(
            functools.partial(send_folded, plan),
            (codes, gathered),
            [VMEM, VMEM],
            scratch_shapes=[half_scaled],
            flops=2 * nodes * plan.rows * share * state,
        )(got, send_part)
    arrived = lax.ppermute(code, "blk", across)
    with jax.named_scope("near_node"):
        near = call(
            functools.partial(near_node_kernel, plan),
            rows,
            [VMEM] * 4,
            scratch_shapes=[half_scaled],
            flops=LONG,
        )(near_own, got, plain, near_code)
    their_near = lax.ppermute(near, SPLIT, to_partner)
    their_arrived = lax.ppermute(arrived, SPLIT, to_partner)
    with jax.named_scope("far_node"):
        far, node = call(far_node_kernel, (rows, result), [VMEM] * 3, flops=LONG)(near, far_own, arrived)
    with jax.named_scope("merge_base"):
        base = call(base_kernel, shape((node_dev, share, state), F32), [VMEM] * 5, flops=LONG)(
            sibling, near, far, their_near, their_own
        )
    with jax.named_scope("merge"):
        return call(
            merge_folded,
            (result, result),
            [VMEM] * 4,
            out_specs=(any_spec, any_spec),
            scratch_shapes=[
                pltpu.VMEM((share, node_dev, state), F32),
                pltpu.SemaphoreType.DMA((PIECES + 1,)),
            ],
        )(sibling, node, base, their_arrived)


def solution(mesh):
    leaf_count, blk_count = mesh.shape["leaf"], mesh.shape["blk"]
    plain = jax.shard_map(
        shards_plain, mesh=mesh, in_specs=in_specs("leaf"), out_specs=out_specs("leaf"), check_vma=False
    )
    if blk_count != 2 or leaf_count != 2 ** len(SPLIT):
        return plain
    split = jax.sharding.Mesh(mesh.devices.reshape((2,) * len(ORDER)), (*SPLIT, "blk"))
    folded = jax.shard_map(
        shards_folded, mesh=split, in_specs=in_specs(SPLIT), out_specs=out_specs(SPLIT), check_vma=False
    )

    def choose(leaf_rows, *more):
        nodes, children, _, state = leaf_rows.shape
        fits = nodes == 2 * leaf_count and children % 2 == 0 and state == 4 * LANES
        return (folded if fits else plain)(leaf_rows, *more)

    return choose


def in_specs(leaf):
    every = ((leaf,) if isinstance(leaf, str) else leaf) + ("blk",)
    return (
        P(leaf, None, "blk", None),
        P(leaf, None, "blk"),
        P(leaf),
        P(leaf, None),
        P("blk", leaf, None),
        P(every, None),
        P(every),
        P(every, None),
    )


def out_specs(leaf):
    return (P("blk", leaf, None), P("blk", leaf, None))
```

```python
import functools

import jax
import jax.numpy as jnp
from jax import lax
from jax.experimental import pallas as pl
from jax.experimental.pallas import tpu as pltpu
from jax.sharding import PartitionSpec as P

F32 = jnp.float32
BF16 = jnp.bfloat16
I32 = jnp.int32
LANES = 128
GROUP = 16
EXTRA = 8
PIECES = 4
LEAVES = 8
VMEM = pl.BlockSpec(memory_space=pltpu.VMEM)
SMEM = pl.BlockSpec(memory_space=pltpu.SMEM)
CODE = 32000.0
SPLIT = ("z1", "z0", "y", "core")
ORDER = ("blk", "y", "z1", "core", "z0")
LONG = 20_000_000_000


class Plan:
    def __init__(self, leaf_count, node_dev, capacity, state, unit, order=()):
        self.order = order
        self.leaf_count, self.node_dev, self.capacity, self.state = leaf_count, node_dev, capacity, state
        self.full = capacity // GROUP * GROUP
        self.rest = capacity - self.full
        self.rows = -(-node_dev * capacity // unit) * unit
        self.groups = self.rows // GROUP
        self.slabs = state // LANES
        self.block = self.slabs * self.rows + EXTRA
        self.groups_of = [
            [g for g in range(self.groups) if q in {self.node_at(g * GROUP + i) for i in range(GROUP)}]
            for q in range(node_dev)
        ]
        self.depth = [leaf_count * GROUP * len(g) for g in self.groups_of]

    def block_of(self, node):
        if not self.order:
            return node
        block = jnp.zeros_like(node)
        for name in self.order:
            block = 2 * block + (node >> (len(SPLIT) - (*SPLIT, "blk").index(name)) & 1)
        return block

    def node_at(self, row):
        if row < self.node_dev * self.full:
            return row // self.full
        return min((row - self.node_dev * self.full) // self.rest, self.node_dev - 1) if self.rest else 0


def dot_t(a, b):
    return lax.dot_general(a, b, (((0,), (0,)), ((), ())), preferred_element_type=F32)


def bucket_kernel(plan, route_hbm, weight_hbm, rows_hbm, out_hbm, route_ref, weight_ref, rows_ref, out_ref, sems):
    count = rows_hbm.shape[0]
    copies = [
        pltpu.make_async_copy(route_hbm, route_ref, sems.at[0]),
        pltpu.make_async_copy(weight_hbm, weight_ref, sems.at[1]),
        pltpu.make_async_copy(rows_hbm, rows_ref, sems.at[2]),
    ]
    for copy in copies:
        copy.start()
    nodes = plan.leaf_count * plan.node_dev
    before = (
        lax.broadcasted_iota(I32, (count, count), 0) < lax.broadcasted_iota(I32, (count, count), 1)
    ).astype(BF16)
    copies[0].wait()
    route = route_ref[...]
    member = lax.broadcasted_iota(I32, (nodes, count), 0) == route
    seen = jnp.dot(member.astype(BF16), before, preferred_element_type=F32)
    position = jnp.sum(jnp.where(member, seen, 0.0), axis=0, keepdims=True).astype(I32)
    route = plan.block_of(route)
    owner = route // plan.node_dev
    q = route - owner * plan.node_dev
    slot = owner * plan.rows + jnp.where(
        position < plan.full,
        q * plan.full + position,
        plan.node_dev * plan.full + q * plan.rest + position - plan.full,
    )
    copies[1].wait()
    weight = weight_ref[...].reshape(1, count).astype(F32)
    lane = lax.broadcasted_iota(I32, (EXTRA, LANES), 1)
    sub = lax.broadcasted_iota(I32, (EXTRA, LANES), 0)
    want = []
    for g in range(plan.rows // EXTRA):
        q_of = jnp.full((EXTRA, LANES), plan.node_at(g * EXTRA), I32)
        for i in range(1, EXTRA):
            step = plan.node_at(g * EXTRA + i) - plan.node_at(g * EXTRA + i - 1)
            if step:
                q_of = q_of + jnp.where(sub >= i, step, 0)
        want.append(lane == g * plan.node_dev + q_of)
    copies[2].wait()
    each = plan.leaf_count // PIECES
    leaving = []
    for p in range(PIECES):
        place = lax.broadcasted_iota(I32, (each * plan.rows, count), 0) + p * each * plan.rows
        hit = jnp.where(place == slot, 1.0, 0.0).astype(BF16)
        weights = jnp.sum(jnp.where(place == slot, weight, 0.0), axis=1, keepdims=True) + jnp.zeros((1, LANES), F32)
        filled = jnp.dot(hit, rows_ref[...], preferred_element_type=F32).astype(BF16)
        for i in range(each):
            at = i * plan.rows
            d = p * each + i
            for c in range(plan.slabs):
                out_ref[d, c * plan.rows : (c + 1) * plan.rows, :] = filled[
                    at : at + plan.rows, c * LANES : (c + 1) * LANES
                ]
            extra = jnp.zeros((EXTRA, LANES), F32)
            for g in range(plan.rows // EXTRA):
                extra = jnp.where(want[g], weights[at + g * EXTRA : at + (g + 1) * EXTRA, :], extra)
            out_ref[d, plan.slabs * plan.rows :, :] = extra.astype(BF16)
        span = pl.ds(p * each, each)
        leaving.append(pltpu.make_async_copy(out_ref.at[span], out_hbm.at[span], sems.at[3 + p]))
        leaving[-1].start()
    for copy in leaving:
        copy.wait()


def leaf_kernel(place_ref, branching_ref, weight_ref, rows_ref, block_ref, own_ref, send_ref, total):
    n = pl.program_id(0)
    share = own_ref.shape[1]
    peers = send_ref.shape[0]
    blk = place_ref[0]
    columns = jnp.transpose(weight_ref[0].astype(F32))
    total[...] = jnp.zeros_like(total)
    for b in range(rows_ref.shape[1]):

        @pl.when(b < branching_ref[n])
        def _():
            rows = rows_ref[0, b]
            scaled = (rows.astype(F32) * columns[:, b : b + 1]).astype(BF16)
            total[...] += dot_t(scaled, rows)

    own_ref[0] = total[pl.ds(pl.multiple_of(blk * share, share), share), :] + block_ref[0].astype(F32)
    for e in range(1, peers + 1):
        at = pl.multiple_of((blk ^ e) * share, share)
        send_ref[e - 1, 0] = total[pl.ds(at, share), :]


class Product:
    def __init__(self, scaled_ref, plain_ref, total):
        self.scaled_ref, self.plain_ref, self.total = scaled_ref, plain_ref, total
        if total is not None:
            total[...] = dot_t(scaled_ref[...], plain_ref[...])

    def rows(self, at, share):
        if self.total is not None:
            return self.total[pl.ds(at, share), :]
        return dot_t(self.scaled_ref[:, pl.ds(at, share)], self.plain_ref[...])


def gather_rows(plan, got_ref, plain_ref, scaled_ref):
    for d in range(plan.leaf_count):
        extra = got_ref[d, plan.slabs * plan.rows :, :].astype(F32)
        for g in range(plan.groups):
            rows = jnp.concatenate(
                [
                    got_ref[d, c * plan.rows + g * GROUP : c * plan.rows + (g + 1) * GROUP, :]
                    for c in range(plan.slabs)
                ],
                axis=1,
            )
            wide = rows.astype(F32)
            for q in range(plan.node_dev):
                if g not in plan.groups_of[q]:
                    continue
                at = (plan.groups_of[q].index(g) * plan.leaf_count + d) * GROUP
                first = g * GROUP // EXTRA * plan.node_dev + q
                places = range(first, first + GROUP // EXTRA * plan.node_dev, plan.node_dev)
                weight = jnp.concatenate([extra[:, j : j + 1] for j in places], axis=0)
                plain_ref[q, at : at + GROUP, :] = rows
                scaled_ref[q, at : at + GROUP, :] = (wide * weight).astype(BF16)


def scale_of(most):
    power = jnp.ceil(8.0 * jnp.log2(jnp.maximum(most, 1e-30)))
    return power, CODE * jnp.exp2(-0.125 * power)


def to_code(value):
    return jnp.round(value).astype(I32).astype(jnp.int16)


def from_code(code):
    return code.astype(I32).astype(F32)


def diagonal(width):
    return lax.broadcasted_iota(I32, (width, width), 0) == lax.broadcasted_iota(I32, (width, width), 1)


def as_line(column):
    return jnp.sum(jnp.where(diagonal(column.shape[0]), column, 0.0), axis=0, keepdims=True)


def as_column(line):
    return jnp.sum(jnp.where(diagonal(line.shape[1]), line, 0.0), axis=1, keepdims=True)


def send_plain(plan, place_ref, got_ref, part_ref, code_ref, plain_ref, scaled_ref, total=None):
    blk = place_ref[0]
    peers, nodes, share, state = part_ref.shape
    gather_rows(plan, got_ref, plain_ref, scaled_ref)
    for q in range(nodes):
        filled = pl.ds(0, plan.depth[q])
        product = Product(scaled_ref.at[q, filled], plain_ref.at[q, filled], total)
        for e in range(1, peers + 1):
            at = pl.multiple_of((blk ^ e) * share, share)
            value = part_ref[e - 1, q] + product.rows(at, share)
            power, factor = scale_of(jnp.max(jnp.abs(value), axis=1, keepdims=True))
            code_ref[e - 1, q * share : (q + 1) * share, :] = to_code(value * factor)
            line = jnp.concatenate([as_line(power), jnp.zeros((1, state - share), F32)], axis=1)
            base = nodes * share + q * GROUP
            code_ref[e - 1, base : base + GROUP, :] = to_code(jnp.broadcast_to(line, (GROUP, state)))


def decode_plain(code_ref, nodes, share):
    values = []
    for q in range(nodes):
        base = nodes * share + q * GROUP
        value = None
        for e in range(code_ref.shape[0]):
            power = as_column(from_code(code_ref[e, base : base + GROUP, :])[0:1, :share])
            term = from_code(code_ref[e, q * share : (q + 1) * share, :]) * (
                jnp.exp2(0.125 * power) * (1.0 / CODE)
            )
            value = term if value is None else value + term
        values.append(value)
    return values


def encode_node(code_ref, square, beside):
    half = code_ref.shape[1]
    upper, lower = square[:half, :half], square[half:, half:]
    pieces = [square[:half, half:]]
    pieces += [beside[r : r + half, c : c + half] for r in (0, half) for c in (0, half)]
    most = jnp.maximum(jnp.abs(upper), jnp.abs(lower))
    for piece in pieces:
        most = jnp.maximum(most, jnp.abs(piece))
    power, factor = scale_of(jnp.max(most, axis=1, keepdims=True))
    row = lax.broadcasted_iota(I32, (half, half), 0)
    column = lax.broadcasted_iota(I32, (half, half), 1)
    lower = lower * factor
    code_ref[:half, :] = to_code(jnp.where(column >= row, upper * factor, lower))
    for k, piece in enumerate(pieces):
        code_ref[(k + 1) * half : (k + 2) * half, :] = to_code(piece * factor)
    corner = jnp.sum(jnp.where(column == row, jnp.round(lower), 0.0), axis=0, keepdims=True)
    line = lax.broadcasted_iota(I32, (EXTRA, half), 0)
    code_ref[6 * half :, :] = to_code(
        jnp.where(line == 0, as_line(power), jnp.where(line == 1, corner, 0.0))
    )


def decode_node(code_ref):
    half = code_ref.shape[1]
    lines = from_code(code_ref[6 * half :, :])
    line = jnp.exp2(0.125 * jnp.broadcast_to(lines[0:1, :], (half, half))) * (1.0 / CODE)
    step = jnp.transpose(line)
    raw = [from_code(code_ref[k * half : (k + 1) * half, :]) for k in range(6)]
    turned, mirror = (jnp.transpose(r) * line for r in raw[:2])
    pieces = [r * step for r in raw]
    both = pieces[0]
    row = lax.broadcasted_iota(I32, (half, half), 0)
    column = lax.broadcasted_iota(I32, (half, half), 1)
    upper = jnp.where(column >= row, both, turned)
    lower = jnp.where(column < row, both, jnp.where(column == row, lines[1:2, :] * line, turned))
    square = ((upper, pieces[1]), (mirror, lower))
    beside = ((pieces[2], pieces[3]), (pieces[4], pieces[5]))
    return square, beside


def halves(place, share):
    mine = pl.ds(pl.multiple_of(place * share, share), share)
    theirs = pl.ds(pl.multiple_of((1 - place) * share, share), share)
    return mine, theirs


def leaf_sum(node, branching_ref, weight_hbm, rows_hbm, weight_ref, rows_ref, total, sems):
    pairs = rows_hbm.shape[1] // 2
    depth, state = rows_hbm.shape[2:]
    count = branching_ref[node]
    weights = pltpu.make_async_copy(weight_hbm.at[node], weight_ref, sems.at[pairs])
    copies = [
        pltpu.make_async_copy(rows_hbm.at[node, pl.ds(2 * p, 2)], rows_ref.at[p], sems.at[p])
        for p in range(pairs)
    ]
    copies[0].start()
    weights.start()
    for p in range(1, pairs):
        pl.when(2 * p < count)(copies[p].start)
    weights.wait()
    live = lax.broadcasted_iota(I32, weight_ref.shape, 0) < count
    columns = jnp.transpose(jnp.where(live, weight_ref[...].astype(F32), 0.0))

    def term(p):
        copies[p].wait()
        rows = rows_ref[p].reshape(2 * depth, state)
        weight = jnp.concatenate([columns[:, 2 * p : 2 * p + 1], columns[:, 2 * p + 1 : 2 * p + 2]], axis=0)
        return dot_t((rows.astype(F32) * weight).astype(BF16), rows)

    total[...] = term(0)
    for p in range(1, pairs):

        @pl.when(2 * p < count)
        def _():
            total[...] += term(p)


def far_leaf_kernel(
    branching_ref, weight_hbm, rows_hbm, own_ref, code_ref, weight_ref, rows_ref, total, sems
):
    share = own_ref.shape[0]
    mine, theirs = halves(lax.axis_index("blk"), share)
    node = 1 - lax.axis_index("blk")
    leaf_sum(node, branching_ref, weight_hbm, rows_hbm, weight_ref, rows_ref, total, sems)
    encode_node(code_ref, total[theirs, theirs], total[theirs, mine])
    own_ref[...] = total[mine, :]


def near_leaf_kernel(
    branching_ref, weight_hbm, rows_hbm, block_ref, far_ref,
    own_ref, send_ref, far_out, weight_ref, rows_ref, total, sems,
):
    share = own_ref.shape[0]
    mine, theirs = halves(lax.axis_index("blk"), share)
    node = lax.axis_index("blk")
    leaf_sum(node, branching_ref, weight_hbm, rows_hbm, weight_ref, rows_ref, total, sems)
    send_ref[...] = total[theirs, :]
    own_ref[...] = total[mine, :] + block_ref[node].astype(F32)
    far_out[...] = far_ref[...] + block_ref[1 - node].astype(F32)


def weighted(plan, got_ref, plain_ref, columns, scaled_ref):
    cap = plan.rows
    for d in range(0, plan.leaf_count, 2):
        extras = [got_ref[d + i, plan.slabs * cap :, :].astype(F32) for i in range(2)]
        weight = jnp.concatenate([e[:, g : g + 1] for e in extras for g in range(cap // EXTRA)], axis=0)
        weight = jnp.broadcast_to(weight, (2 * cap, scaled_ref.shape[1])).astype(BF16)
        rows = slice(d * cap, (d + 2) * cap)
        scaled_ref[rows, :] = plain_ref[rows, columns] * weight


def send_folded(plan, got_ref, part_ref, code_ref, plain_ref, scaled_ref):
    share = part_ref.shape[0]
    mine, theirs = halves(lax.axis_index("blk"), share)
    cap = plan.rows
    for d in range(0, plan.leaf_count, 2):
        for c in range(plan.slabs):
            plain_ref[d * cap : (d + 2) * cap, c * LANES : (c + 1) * LANES] = jnp.concatenate(
                [got_ref[d + i, c * cap : (c + 1) * cap, :] for i in range(2)], axis=0
            )
    weighted(plan, got_ref, plain_ref, theirs, scaled_ref)
    scaled = scaled_ref[...]
    encode_node(
        code_ref,
        part_ref[:, theirs] + dot_t(scaled, plain_ref[:, theirs]),
        part_ref[:, mine] + dot_t(scaled, plain_ref[:, mine]),
    )


def in_columns(place, square, beside):
    first = place == 0
    return [
        [jnp.where(first, s, b) for s, b in zip(*pair)] + [jnp.where(first, b, s) for s, b in zip(*pair)]
        for pair in zip(square, beside)
    ]


def tiles_of(ref):
    half = ref.shape[0] // 2
    for i in range(2):
        for k in range(ref.shape[1] // half):
            yield i, k, slice(i * half, (i + 1) * half), slice(k * half, (k + 1) * half)


def near_node_kernel(plan, own_ref, got_ref, plain_ref, code_ref, node_ref, scaled_ref):
    mine, _ = halves(lax.axis_index("blk"), own_ref.shape[0])
    weighted(plan, got_ref, plain_ref, mine, scaled_ref)
    node_ref[...] = own_ref[...] + dot_t(scaled_ref[...], plain_ref[...])
    terms = in_columns(lax.axis_index("blk"), *decode_node(code_ref))
    for i, k, rows, columns in tiles_of(node_ref):
        node_ref[rows, columns] += terms[i][k]


def far_node_kernel(near_ref, own_ref, code_ref, far_ref, out_ref):
    first = lax.axis_index("blk") == 0
    terms = in_columns(lax.axis_index("blk"), *decode_node(code_ref))
    for i, k, rows, columns in tiles_of(own_ref):
        far = own_ref[rows, columns] + terms[i][k]
        near = near_ref[rows, columns]
        far_ref[rows, columns] = far
        out_ref[rows, 0, columns] = jnp.where(first, near, far)
        out_ref[rows, 1, columns] = jnp.where(first, far, near)


def first_awaits(sibling_ref, count):
    straight = jnp.broadcast_to(sibling_ref[0:1, 0:1], (count, LANES)) == 0
    return straight != (lax.axis_index("blk") == 0)


def base_kernel(sibling_ref, near_ref, far_ref, their_near_ref, their_own_ref, base_ref):
    first = lax.axis_index("blk") == 0
    zero = first_awaits(sibling_ref, LANES)
    for _, _, rows, columns in tiles_of(their_own_ref):
        near, far = near_ref[rows, columns], far_ref[rows, columns]
        their_near, their_far = their_near_ref[rows, columns], their_own_ref[rows, columns]
        base_ref[0, rows, columns] = jnp.where(first, near, far) + jnp.where(zero, their_far, their_near)
        base_ref[1, rows, columns] = jnp.where(first, far, near) + jnp.where(zero, their_near, their_far)


def merge_folded(sibling_ref, node_ref, base_ref, code_ref, node_hbm, out_hbm, out_ref, sems):
    _, share, state = base_ref.shape
    half = share // 2
    each = share // LEAVES
    copies = [pltpu.make_async_copy(node_ref, node_hbm, sems.at[LEAVES])]
    copies[0].start()
    zero = first_awaits(sibling_ref, each)
    terms = in_columns(lax.axis_index("blk"), *decode_node(code_ref))
    for p in range(LEAVES):
        rows = slice(p * each, (p + 1) * each)
        inner = slice(p * each % half, p * each % half + each)
        for k in range(state // half):
            columns = slice(k * half, (k + 1) * half)
            term = terms[p * each // half][k][inner]
            out_ref[rows, 0, columns] = base_ref[0, rows, columns] + jnp.where(zero, term, 0.0)
            out_ref[rows, 1, columns] = base_ref[1, rows, columns] + jnp.where(zero, 0.0, term)
        span = pl.ds(p * each, each)
        copies.append(pltpu.make_async_copy(out_ref.at[span], out_hbm.at[span], sems.at[p]))
        copies[-1].start()
    for copy in copies:
        copy.wait()


def own_kernel(plan, place_ref, part_ref, plain_ref, scaled_ref, own_ref, total=None):
    nodes, share, _ = part_ref.shape
    at = pl.multiple_of(place_ref[0] * share, share)
    for q in range(nodes):
        filled = pl.ds(0, plan.depth[q])
        product = Product(scaled_ref.at[q, filled], plain_ref.at[q, filled], total)
        own_ref[q] = part_ref[q] + product.rows(at, share)


def node_kernel(own_ref, code_ref, out_ref, node_ref):
    nodes, share, _ = own_ref.shape
    arrived = decode_plain(code_ref, nodes, share)
    for q in range(nodes):
        value = own_ref[q] + arrived[q]
        node_ref[q] = value
        out_ref[:, q, :] = value


def merge_kernel(sibling_ref, node_ref, own_ref, code_ref, out_ref, partner_ref):
    nodes, share, _ = own_ref.shape
    arrived = decode_plain(code_ref, nodes, share)
    for q in range(nodes):
        partner_ref[q] = own_ref[q] + arrived[q]
    for q in range(nodes):
        out_ref[:, q, :] = node_ref[q] + partner_ref[sibling_ref[0, q]]


def call(kernel, out_shape, in_specs, flops=0, moved=1 << 20, vmem=32 << 20, **more):
    outs = jax.tree.map(lambda _: VMEM, out_shape)
    more.setdefault("out_specs", outs)
    return pl.pallas_call(
        kernel,
        out_shape=out_shape,
        in_specs=in_specs,
        compiler_params=pltpu.CompilerParams(vmem_limit_bytes=vmem),
        cost_estimate=pl.CostEstimate(flops=flops, bytes_accessed=moved, transcendentals=0),
        **more,
    )


def exchange_plain(plan, place, got, own_part, send_part, sibling, blk_count):
    peers, node_dev, share, state = send_part.shape
    shape = jax.ShapeDtypeStruct
    whole = [pltpu.VMEM((state, state), F32)] if share % LANES else []
    depth = max(plan.depth)
    to_partner = [(i, i ^ 1) for i in range(plan.leaf_count)]
    with jax.named_scope("routed_send"):
        code, plain, scaled = call(
            functools.partial(send_plain, plan),
            (
                shape((peers, node_dev * (share + GROUP), state), jnp.int16),
                shape((node_dev, depth, state), BF16),
                shape((node_dev, depth, state), BF16),
            ),
            [SMEM, VMEM, VMEM],
            scratch_shapes=whole,
            flops=2 * node_dev * depth * state * state,
        )(place, got, send_part)
    arrived = jnp.stack(
        [
            lax.ppermute(code[e - 1], "blk", [(i, i ^ e) for i in range(blk_count)])
            for e in range(1, blk_count)
        ]
    )
    with jax.named_scope("routed_own"):
        own = call(
            functools.partial(own_kernel, plan),
            shape((node_dev, share, state), F32),
            [SMEM, VMEM, VMEM, VMEM],
            scratch_shapes=whole,
            flops=2 * node_dev * depth * share * state,
        )(place, own_part, plain, scaled)
    partner_own = lax.ppermute(own, "leaf", to_partner)
    partner_arrived = lax.ppermute(arrived, "leaf", to_partner)
    with jax.named_scope("node"):
        node_schur, node = call(
            node_kernel,
            (shape((share, node_dev, state), F32), shape((node_dev, share, state), F32)),
            [VMEM, VMEM],
        )(own, arrived)
    with jax.named_scope("merge"):
        merged = call(
            merge_kernel,
            shape((share, node_dev, state), F32),
            [SMEM, VMEM, VMEM, VMEM],
            scratch_shapes=[pltpu.VMEM((node_dev, share, state), F32)],
        )(sibling, node, partner_own, partner_arrived)
    return node_schur, merged


def bucket(plan, na_route, na_weight, na_rows):
    count, state = na_rows.shape
    any_spec = pl.BlockSpec(memory_space=pl.ANY)
    with jax.named_scope("bucket"):
        return call(
            functools.partial(bucket_kernel, plan),
            jax.ShapeDtypeStruct((plan.leaf_count, plan.block, LANES), BF16),
            [any_spec, any_spec, any_spec],
            scratch_shapes=[
                pltpu.VMEM((1, count), I32),
                pltpu.VMEM((count,), BF16),
                pltpu.VMEM((count, state), BF16),
                pltpu.VMEM((plan.leaf_count, plan.block, LANES), BF16),
                pltpu.SemaphoreType.DMA((3 + PIECES,)),
            ],
            out_specs=any_spec,
            vmem=60 << 20,
            flops=2 * plan.leaf_count * plan.rows * count * state,
        )(na_route.reshape(1, count), na_weight, na_rows)


def shards_plain(leaf_rows, leaf_weight, branching, sibling, node_block, na_rows, na_weight, na_route):
    leaf_count, blk_count = lax.axis_size("leaf"), lax.axis_size("blk")
    node_dev, most_children, depth, state = leaf_rows.shape
    count = na_rows.shape[0]
    share = state // blk_count
    peers = blk_count - 1
    plan = Plan(leaf_count, node_dev, 3 * count // (2 * leaf_count * node_dev), state, GROUP)
    place = lax.axis_index("blk").astype(I32).reshape(1)
    shape = jax.ShapeDtypeStruct
    blocks = bucket(plan, na_route, na_weight, na_rows)
    got = lax.all_to_all(blocks, "leaf", split_axis=0, concat_axis=0, tiled=True)
    with jax.named_scope("leaf_products"):
        own_part, send_part = call(
            leaf_kernel,
            (shape((node_dev, share, state), F32), shape((peers, node_dev, share, state), F32)),
            [
                SMEM,
                SMEM,
                pl.BlockSpec((1, most_children, depth), lambda n: (n, 0, 0)),
                pl.BlockSpec((1, most_children, depth, state), lambda n: (n, 0, 0, 0)),
                pl.BlockSpec((1, share, state), lambda n: (n, 0, 0)),
            ],
            out_specs=(
                pl.BlockSpec((1, share, state), lambda n: (n, 0, 0)),
                pl.BlockSpec((peers, 1, share, state), lambda n: (0, n, 0, 0)),
            ),
            grid=(node_dev,),
            scratch_shapes=[pltpu.VMEM((state, state), F32)],
            flops=2 * node_dev * most_children * depth * state * state,
            moved=8 << 20,
        )(place, branching, leaf_weight, leaf_rows, jnp.transpose(node_block, (1, 0, 2)))
    return exchange_plain(plan, place, got, own_part, send_part, sibling, blk_count)


def shards_folded(leaf_rows, leaf_weight, branching, sibling, node_block, na_rows, na_weight, na_route):
    leaf_count = lax.axis_size(SPLIT)
    node_dev, most_children, depth, state = leaf_rows.shape
    count = na_rows.shape[0]
    share = state // 2
    half = share // 2
    nodes = leaf_count * node_dev
    plan = Plan(nodes, 1, 3 * count // (2 * nodes), state, EXTRA, ORDER)
    shape = jax.ShapeDtypeStruct
    any_spec = pl.BlockSpec(memory_space=pl.ANY)
    across = [(0, 1), (1, 0)]
    to_partner = [(i, i ^ 1) for i in range(leaf_count)]
    result = shape((share, node_dev, state), F32)
    rows = shape((share, state), F32)
    codes = shape((6 * half + EXTRA, half), jnp.int16)
    gathered = shape((nodes * plan.rows, state), BF16)

    blocks = bucket(plan, na_route, na_weight, na_rows)
    got = lax.all_to_all(blocks, ORDER, split_axis=0, concat_axis=0, tiled=True)

    own_block = jnp.transpose(node_block, (1, 0, 2))
    leaf = dict(
        scratch_shapes=[
            pltpu.VMEM((most_children, depth), BF16),
            pltpu.VMEM((most_children // 2, 2, depth, state), BF16),
            pltpu.VMEM((state, state), F32),
            pltpu.SemaphoreType.DMA((most_children // 2 + 1,)),
        ],
        flops=1,
        moved=1,
        vmem=24 << 20,
    )
    with jax.named_scope("far_leaf_products"):
        far_own, far_code = call(
            far_leaf_kernel, (rows, codes), [SMEM, any_spec, any_spec], **leaf
        )(branching, leaf_weight, leaf_rows)
    near_code = lax.ppermute(far_code, "blk", across)
    with jax.named_scope("near_leaf_products"):
        near_own, send_part, far_own = call(
            near_leaf_kernel, (rows, rows, rows), [SMEM, any_spec, any_spec, VMEM, VMEM], **leaf
        )(branching, leaf_weight, leaf_rows, own_block, far_own)
    their_own = lax.ppermute(far_own, SPLIT, to_partner)
    half_scaled = pltpu.VMEM((nodes * plan.rows, share), BF16)
    with jax.named_scope("routed_send"):
        code, plain = call(
            functools.partial(send_folded, plan),
            (codes, gathered),
            [VMEM, VMEM],
            scratch_shapes=[half_scaled],
            flops=2 * nodes * plan.rows * share * state,
        )(got, send_part)
    arrived = lax.ppermute(code, "blk", across)
    with jax.named_scope("near_node"):
        near = call(
            functools.partial(near_node_kernel, plan),
            rows,
            [VMEM] * 4,
            scratch_shapes=[half_scaled],
            flops=LONG,
        )(near_own, got, plain, near_code)
    their_near = lax.ppermute(near, SPLIT, to_partner)
    their_arrived = lax.ppermute(arrived, SPLIT, to_partner)
    with jax.named_scope("far_node"):
        far, node = call(far_node_kernel, (rows, result), [VMEM] * 3, flops=LONG)(near, far_own, arrived)
    with jax.named_scope("merge_base"):
        base = call(base_kernel, shape((node_dev, share, state), F32), [VMEM] * 5, flops=LONG)(
            sibling, near, far, their_near, their_own
        )
    with jax.named_scope("merge"):
        return call(
            merge_folded,
            (result, result),
            [VMEM] * 4,
            out_specs=(any_spec, any_spec),
            scratch_shapes=[
                pltpu.VMEM((share, node_dev, state), F32),
                pltpu.SemaphoreType.DMA((LEAVES + 1,)),
            ],
        )(sibling, node, base, their_arrived)


def solution(mesh):
    leaf_count, blk_count = mesh.shape["leaf"], mesh.shape["blk"]
    plain = jax.shard_map(
        shards_plain, mesh=mesh, in_specs=in_specs("leaf"), out_specs=out_specs("leaf"), check_vma=False
    )
    if blk_count != 2 or leaf_count != 2 ** len(SPLIT):
        return plain
    split = jax.sharding.Mesh(mesh.devices.reshape((2,) * len(ORDER)), (*SPLIT, "blk"))
    folded = jax.shard_map(
        shards_folded, mesh=split, in_specs=in_specs(SPLIT), out_specs=out_specs(SPLIT), check_vma=False
    )

    def choose(leaf_rows, *more):
        nodes, children, _, state = leaf_rows.shape
        fits = nodes == 2 * leaf_count and children % 2 == 0 and state == 4 * LANES
        return (folded if fits else plain)(leaf_rows, *more)

    return choose


def in_specs(leaf):
    every = ((leaf,) if isinstance(leaf, str) else leaf) + ("blk",)
    return (
        P(leaf, None, "blk", None),
        P(leaf, None, "blk"),
        P(leaf),
        P(leaf, None),
        P("blk", leaf, None),
        P(every, None),
        P(every),
        P(every, None),
    )


def out_specs(leaf):
    return (P("blk", leaf, None), P("blk", leaf, None))
```
